32 devices in a mesh: dp: 8 (over y, x, core), tensor: 4 (over z).
Axes of the slice: x: 2, y: 2, z: 4, core: 2. Of those that a mesh axis runs over, the one named last changes fastest.
Arguments:
- tokens: bfloat16 [8192, 1024], P(('dp', 'tensor')), may hold values from -6 to 6
- cotangent: bfloat16 [8192, 1024], P(('dp', 'tensor')), may hold values from -6 to 6
- segments: int32 [8, 1024], P('dp'), may hold values from 0 to 3, never falling along the last dimension, each value on 1 to 800 neighbouring positions
- norm_gains: bfloat16 [2, 1024], replicated, may hold values from 0.5 to 1.5
- mixer_in: bfloat16 [1024, 6144], P('dp', 'tensor'), may hold values from -0.1875 to 0.1875
- mixer_small: bfloat16 [2, 1024, 8], P(None, 'dp', 'tensor'), may hold values from -0.1875 to 0.1875
- conv_weight: bfloat16 [4, 8, 512], P(None, 'tensor', 'dp'), may hold values from -3 to 3
- head_params: float32 [2, 8], replicated, may hold values from -10 to 3, as said below
- out_norm: bfloat16 [8, 256], P('tensor', 'dp'), may hold values from 0.5 to 1.5
- mixer_out: bfloat16 [2048, 1024], P('tensor', 'dp'), may hold values from -0.125 to 0.125
- ffn_in: bfloat16 [2, 1024, 2816], P(None, 'dp', 'tensor'), may hold values from -0.1875 to 0.1875
- ffn_out: bfloat16 [2816, 1024], P('tensor', 'dp'), may hold values from -0.109375 to 0.109375
Outputs:
- output: bfloat16 [8192, 1024], P(('dp', 'tensor'))
- grad_tokens: float32 [8192, 1024], P(('dp', 'tensor'))
- grad_norm_gains: float32 [2, 1024], replicated
- grad_mixer_in: float32 [1024, 6144], P('dp', 'tensor')
- grad_mixer_small: float32 [2, 1024, 8], P(None, 'dp', 'tensor')
- grad_conv_weight: float32 [4, 8, 512], P(None, 'tensor', 'dp')
- grad_head_params: float32 [2, 8], replicated
- grad_out_norm: float32 [8, 256], P('tensor', 'dp')
- grad_mixer_out: float32 [2048, 1024], P('tensor', 'dp')
- grad_ffn_in: float32 [2, 1024, 2816], P(None, 'dp', 'tensor')
- grad_ffn_out: float32 [2816, 1024], P('tensor', 'dp')
The draws below stay inside these ranges and needn't reach their ends.
Inputs may be any that keep to these rules, and one draw needn't show every extreme that they name: `segments`: within each sequence the numbers never fall; each document has 1 to 800 tokens and some document has exactly 800. `head_params`: row 0 is the logarithm of each head's decay rate, row 1 the bias added before the softplus.
All inputs are finite; a program needn't handle non-finite values.
Results may differ from the reference program's by a relative error of at most 0.019.
Values may be sent and summed in bfloat16 or wider, within the bound.
No kernel may reach another device: no remote copies, remote signals or barrier semaphores. Data moves between devices by JAX's collectives and lax.ppermute only.
A program may use at most 192 MiB of HBM per device.

```python
import math
import jax
import jax.numpy as jnp
import numpy as np
from jax import lax

D = 1024
H = 8
DK = 128
DV = 256
FF = 2816
KCONV = 4
SPAN = 64
TOK_DEV = 256
LENGTH = 1024
TOKENS = 8192
NSEQ = 8
DOC_MAX = 800
DOCS = 4
MIX = 768
CONVC = 512
N_DP = 8
N_TENSOR = 4


def draw_head_params(key, part):
    first = jax.random.fold_in(key, 11)
    second = jax.random.fold_in(key, 12)
    rate = jax.random.uniform(first, (H,), jnp.float32, 1.0, 16.0)
    low_end = math.log(0.001)
    high_end = math.log(0.1)
    step = jnp.exp(jax.random.uniform(second, (H,), jnp.float32, low_end, high_end))
    return jnp.stack([jnp.log(rate), jnp.log(jnp.expm1(step))])


def level_of(rng, extent, shards, low, high):
    factor_of, own = 1.0, jax.random.fold_in(rng, 6)
    for position, parts in shards:
        steps = jnp.exp(jax.random.uniform(jax.random.fold_in(own, position), (parts,), jnp.float32, low / len(shards), high / len(shards)))
        factor_of = factor_of * jnp.repeat(steps, extent[position] // parts).reshape([-1 if axis == position else 1 for axis in range(len(extent))])
    return factor_of


def length_profile(amount, total, limit, skew):
    portions = [(1 << 20) // math.isqrt(grade ** skew) + 1 for grade in range(2, amount + 1)]
    surplus, holding = total - limit - (amount - 1), [1] * (amount - 1)
    while surplus > 0:
        movable = [i for i in range(amount - 1) if holding[i] < limit]
        mass, remaining = sum([portions[i] for i in movable]), surplus
        for i in movable:
            addition = min(limit - holding[i], max(1, remaining * portions[i] // mass), surplus)
            holding[i] = holding[i] + addition
            surplus = surplus - addition
    return np.array([limit] + holding)


def ragged(stream_key, amount, total, limit, slope):
    if amount == 2:
        one = jax.random.randint(stream_key, (), max(1, total - limit), min(limit, total - 1) + 1)
        return jnp.stack([one, total - one])
    lengths = jnp.asarray(length_profile(amount, total, limit, slope), jnp.int32)
    twos = (amount - 1) // 2
    giver, sink = lengths[1:1 + 2 * twos:2], lengths[2:2 + 2 * twos:2]
    room = jnp.minimum(giver - 1, limit - sink)
    shifted = jax.random.randint(jax.random.fold_in(stream_key, 1), (twos,), 0, 1 << 20) % (room + 1)
    lengths = lengths.at[1:1 + 2 * twos:2].set(giver - shifted).at[2:2 + 2 * twos:2].set(sink + shifted)
    return lengths[jax.random.permutation(jax.random.fold_in(stream_key, 2), amount)]


def gaussian(rng, shape, deviation, bound, shards=(), dtype=jnp.bfloat16):
    gain = level_of(rng, shape, shards, -0.22, 0.18) if shards else 1.0
    entries = jax.random.normal(rng, shape, jnp.float32) * deviation * gain
    return jnp.minimum(jnp.maximum(entries, -bound), bound).astype(dtype)


def setup_inputs(seed: int = 0) -> dict:
    key_of = jax.random.split(jax.random.key(seed), 13)
    tokens = gaussian(key_of[0], (TOKENS, D), 1.0, 6.0, ((0, 32),))
    cotangent = gaussian(key_of[1], (TOKENS, D), 1.0, 6.0, ((0, 32),))
    segments = jax.vmap(lambda own: jnp.searchsorted(jnp.cumsum(ragged(own, DOCS, LENGTH, DOC_MAX, 0)), jnp.arange(LENGTH), side="right"))(jax.random.split(key_of[2], NSEQ)).reshape((NSEQ, LENGTH)).astype(jnp.int32)
    norm_gains = jnp.clip(1.0 + 0.1 * jax.random.normal(key_of[3], (2, D), jnp.float32), 0.5, 1.5).astype(jnp.bfloat16)
    mixer_in = gaussian(key_of[4], (D, H * MIX), D ** -0.5, 0.1875, ((0, 8), (1, 4)))
    mixer_small = gaussian(key_of[5], (2, D, H), D ** -0.5, 0.1875, ((1, 8), (2, 4)))
    conv_weight = gaussian(key_of[6], (KCONV, H, CONVC), KCONV ** -0.5, 3.0, ((1, 4), (2, 8)))
    head_params = draw_head_params(jax.random.fold_in(key_of[12], 71), 0)
    out_norm = jnp.clip(1.0 + 0.1 * jax.random.normal(key_of[8], (H, DV), jnp.float32), 0.5, 1.5).astype(jnp.bfloat16)
    mixer_out = gaussian(key_of[9], (H * DV, D), (H * DV) ** -0.5, 0.125, ((0, 4), (1, 8)))
    ffn_in = gaussian(key_of[10], (2, D, FF), D ** -0.5, 0.1875, ((1, 8), (2, 4)))
    ffn_out = gaussian(key_of[11], (FF, D), FF ** -0.5, 0.109375, ((0, 4), (1, 8)))
    return {"tokens": tokens, "cotangent": cotangent, "segments": segments, "norm_gains": norm_gains, "mixer_in": mixer_in, "mixer_small": mixer_small, "conv_weight": conv_weight, "head_params": head_params, "out_norm": out_norm, "mixer_out": mixer_out, "ffn_in": ffn_in, "ffn_out": ffn_out}


@jax.custom_vjp
def low(v):
    return lax.optimization_barrier(v.astype(jnp.bfloat16)).astype(jnp.float32)

@jax.custom_vjp
def low_back(v):
    return v

def low_keep(v):
    return (low(v), None)

def low_pass(kept, grad):
    return (grad,)

def back_keep(v):
    return (v, None)

def back_low(kept, grad):
    return (low(grad),)
low.defvjp(low_keep, low_pass)
low_back.defvjp(back_keep, back_low)
highest = lax.Precision.HIGHEST

def block_step(state, blocks):
    query, key_end, carried, carried_last, attend, fixed, across = blocks
    deltas = fixed - jnp.einsum('bhid,bhde->bhie', across, state, precision=highest)
    result = carried[..., None] * jnp.einsum('bhid,bhde->bhie', query, state, precision=highest)
    result = result + jnp.einsum('bhij,bhje->bhie', attend, deltas, precision=highest)
    new_state = carried_last[..., None, None] * state
    new_state = new_state + jnp.einsum('bhjd,bhje->bhde', key_end, deltas, precision=highest)
    return (new_state, result)

def to_blocks(values, nseq, count):
    return values.reshape(nseq, count, SPAN, values.shape[2], values.shape[3]).transpose(1, 0, 3, 2, 4)

def delta_rule(query, key, value, beta, log_decay, seg):
    nseq, length, heads = beta.shape
    count = length // SPAN
    query_b = to_blocks(query, nseq, count)
    key_b = to_blocks(key, nseq, count)
    value_b = to_blocks(value, nseq, count)
    beta_b = beta.reshape(nseq, count, SPAN, heads).transpose(1, 0, 3, 2)
    decay_b = log_decay.reshape(nseq, count, SPAN, heads).transpose(1, 0, 3, 2)
    seg_b = seg.reshape(nseq, count, SPAN).transpose(1, 0, 2)
    before = jnp.concatenate([jnp.full((1, nseq), -1, jnp.int32), seg_b[:-1, :, SPAN - 1]], 0)
    total = jnp.cumsum(decay_b, -1)
    row_ids = lax.broadcasted_iota(jnp.int32, (SPAN, SPAN), 0)
    col_ids = lax.broadcasted_iota(jnp.int32, (SPAN, SPAN), 1)
    same = (seg_b[..., :, None] == seg_b[..., None, :])[:, :, None]
    keep_mask = same & (row_ids >= col_ids)
    differ = total[..., :, None] - total[..., None, :]
    decay = jnp.where(keep_mask, jnp.exp(jnp.where(keep_mask, differ, 0.0)), 0.0)
    carried = jnp.where((seg_b == before[..., None])[:, :, None], jnp.exp(total), 0.0)
    inner_kk = jnp.einsum('abhid,abhjd->abhij', key_b, key_b, precision=highest)
    strict = jnp.where(row_ids > col_ids, decay, 0.0)
    lower_mat = beta_b[..., None] * strict * inner_kk + jnp.where(row_ids == col_ids, 1.0, 0.0)
    sides = jnp.concatenate([beta_b[..., None] * value_b, (beta_b * carried)[..., None] * key_b], -1)
    solved = lax.linalg.triangular_solve(lower_mat, sides, left_side=True, lower=True, unit_diagonal=True)
    fixed = solved[..., :DV]
    across = solved[..., DV:]
    inner_qk = jnp.einsum('abhid,abhjd->abhij', query_b, key_b, precision=highest)
    attend = decay * inner_qk
    key_end = key_b * decay[..., SPAN - 1, :][..., None]
    carried_last = carried[..., SPAN - 1]
    state = jnp.zeros((nseq, heads, DK, DV), jnp.float32)
    unused, outputs = lax.scan(jax.checkpoint(block_step), state, (query_b, key_end, carried, carried_last, attend, fixed, across))
    return outputs.transpose(1, 0, 3, 2, 4).reshape(nseq, length, heads, DV)

def mixer_core(proj, small, conv, head, onorm, seg):
    nseq, length = seg.shape
    heads = proj.shape[1]
    width = conv.shape[0]
    mixed_in = proj[:, :, :2 * DK + DV].reshape(nseq, length, heads, 2 * DK + DV)
    gate = proj[:, :, 2 * DK + DV:].reshape(nseq, length, heads, DV)
    seg_pad = jnp.pad(seg, ((0, 0), (width - 1, 0)), constant_values=-1)
    in_pad = jnp.pad(mixed_in, ((0, 0), (width - 1, 0), (0, 0), (0, 0)))
    mixed = jnp.zeros_like(mixed_in)
    for shift in range(width):
        begin = width - 1 - shift
        same = (seg_pad[:, begin:begin + length] == seg)[:, :, None, None]
        mixed = mixed + conv[width - 1 - shift] * jnp.where(same, in_pad[:, begin:begin + length], 0.0)
    active = jax.nn.silu(mixed)
    query = active[..., :DK]
    key = active[..., DK:2 * DK]
    value = active[..., 2 * DK:]
    query = query * lax.rsqrt(lax.optimization_barrier(jnp.sum(query * query, -1, keepdims=True)) + 1e-06) * DK ** (-0.5)
    key = key * lax.rsqrt(lax.optimization_barrier(jnp.sum(key * key, -1, keepdims=True)) + 1e-06)
    beta = jax.nn.sigmoid(small[:, 0, :]).reshape(nseq, length, heads)
    log_decay = (-jnp.exp(head[0]) * jax.nn.softplus(small[:, 1, :] + head[1])).reshape(nseq, length, heads)
    result = delta_rule(query, key, value, beta, log_decay, seg)
    factor = lax.rsqrt(lax.optimization_barrier(jnp.mean(result * result, -1, keepdims=True)) + 1e-05)
    return (result * factor * onorm * jax.nn.silu(gate)).reshape(nseq * length, heads * DV)

def normed(values):
    return values * lax.rsqrt(lax.optimization_barrier(jnp.mean(values * values, -1, keepdims=True)) + 1e-06)

def layer(inputs, gains, w_in, w_small, conv, head, onorm, w_out, w_ffn, w_down, seg):
    group = inputs.shape[0]
    first = low(normed(inputs) * gains[0])
    proj = low_back(jnp.dot(first, w_in, precision=highest)).reshape(group, H, 2 * DK + 2 * DV)
    small = low_back(jnp.einsum('nd,cdh->nch', first, w_small, precision=highest))
    mixed = low(mixer_core(proj, small, conv, head, onorm, seg))
    middle = inputs + low_back(jnp.dot(mixed, w_out, precision=highest))
    second = low(normed(middle) * gains[1])
    both = low_back(jnp.einsum('nd,cdf->ncf', second, w_ffn, precision=highest))
    hidden = low(jax.nn.silu(both[:, 0]) * both[:, 1])
    return middle + low_back(jnp.dot(hidden, w_down, precision=highest))

def reference(tokens, cotangent, segments, norm_gains, mixer_in, mixer_small, conv_weight, head_params, out_norm, mixer_out, ffn_in, ffn_out):
    weights = tuple((w.astype(jnp.float32) for w in (norm_gains, mixer_in, mixer_small, conv_weight, head_params, out_norm, mixer_out, ffn_in, ffn_out)))
    group = TOK_DEV * N_TENSOR
    inputs = tokens.astype(jnp.float32).reshape(N_DP, group, D)
    grads_out = cotangent.astype(jnp.float32).reshape(N_DP, group, D)
    seg_groups = segments.reshape(N_DP, group // LENGTH, LENGTH)

    def one_group(totals, items):
        values, grad_values, seg = items

        def run(first, *params):
            return layer(first, *params, seg)
        result, pullback = jax.vjp(run, values, *weights)
        grads = pullback(grad_values)
        return (tuple((t + g for t, g in zip(totals, grads[1:]))), (result, grads[0]))
    zeros = tuple((jnp.zeros_like(w) for w in weights))
    totals, (results, grad_inputs) = lax.scan(one_group, zeros, (inputs, grads_out, seg_groups))
    return (results.reshape(TOKENS, D).astype(jnp.bfloat16), grad_inputs.reshape(TOKENS, D), totals[0], totals[1], totals[2], totals[3], totals[4], totals[5], totals[6], totals[7], totals[8])
```

```python
import functools
import jax
import jax.numpy as jnp
from jax import lax
from jax.experimental import pallas as pl
from jax.experimental.pallas import tpu as pltpu
from jax.sharding import PartitionSpec as P

DK = 128
DV = 256
MIX = 2 * DK + 2 * DV
CONV = 2 * DK + DV
CHUNK = 128
LANES = 128
TAPS = 4
BETA_AT = 8

NN = ((1,), (0,))
NT = ((1,), (1,))
TN = ((0,), (0,))

f32 = jnp.float32
bf16 = jnp.bfloat16


def dot(a, b, dims, passes):
    if passes == 6:
        return lax.dot_general(
            a, b, (dims, ((), ())), precision=lax.Precision.HIGHEST, preferred_element_type=f32
        )
    a_hi = a.astype(bf16)
    b_hi = b.astype(bf16)
    out = lax.dot_general(a_hi, b_hi, (dims, ((), ())), preferred_element_type=f32)
    if passes == 3:
        a_lo = (a - a_hi.astype(f32)).astype(bf16)
        b_lo = (b - b_hi.astype(f32)).astype(bf16)
        out = out + lax.dot_general(a_hi, b_lo, (dims, ((), ())), preferred_element_type=f32)
        out = out + lax.dot_general(a_lo, b_hi, (dims, ((), ())), preferred_element_type=f32)
    return out


def exact_left(mask, b):
    hi = b.astype(bf16)
    rest = b - hi.astype(f32)
    mid = rest.astype(bf16)
    low = (rest - mid.astype(f32)).astype(bf16)
    out = lax.dot_general(mask, hi, (NN, ((), ())), preferred_element_type=f32)
    out = out + lax.dot_general(mask, mid, (NN, ((), ())), preferred_element_type=f32)
    return out + lax.dot_general(mask, low, (NN, ((), ())), preferred_element_type=f32)


def sigmoid(x):
    return 1.0 / (1.0 + jnp.exp(-x))


def log1p(y):
    return jnp.where(y < 1e-4, y - 0.5 * y * y, jnp.log(1.0 + y))


def softplus(x):
    return jnp.maximum(x, 0.0) + log1p(jnp.exp(-jnp.abs(x)))


def iotas():
    shape = (CHUNK, CHUNK)
    return lax.broadcasted_iota(jnp.int32, shape, 0), lax.broadcasted_iota(jnp.int32, shape, 1)


def token_scalars(info, head_rows, heads):
    row, col = iotas()
    beta = sigmoid(info)
    rate = -jnp.exp(head_rows[0:1])
    pre = info + head_rows[1:2]
    g = rate * softplus(pre)
    total = exact_left((row >= col).astype(bf16), g)
    lane = lax.broadcasted_iota(jnp.int32, (CHUNK, LANES), 1)
    across = jnp.where(lane < BETA_AT, info, total).T
    return beta, g, pre, total, across


def head_scalars(h, heads, info, beta, total, across):
    row, col = iotas()
    at = BETA_AT + heads + h
    seg_col = info[:, 0:1]
    seg_row = across[0:1, :]
    tot_col = total[:, at : at + 1]
    tot_row = across[at : at + 1, :]
    keep = (seg_col == seg_row) & (row >= col)
    decay = jnp.exp(jnp.where(keep, tot_col - tot_row, -1e30))
    strict = jnp.where(row > col, decay, 0.0)
    beta_col = beta[:, BETA_AT + h : BETA_AT + h + 1]
    carried = jnp.exp(tot_col) * info[:, 7:8]
    last = CHUNK - 1
    end = jnp.where(
        seg_col == seg_col[last : last + 1], jnp.exp(tot_col[last : last + 1] - tot_col), 0.0
    )
    carried_last = carried[last : last + 1]
    return decay, strict, beta_col, carried, end, carried_last


def invert(lower, passes):
    row, col = iotas()
    eye = jnp.where(row == col, 1.0, 0.0)
    size = 1
    inv = None
    while size < CHUNK:
        part = ((row // (2 * size)) == (col // (2 * size))) & ((row // size) != (col // size))
        step = jnp.where(part, lower, 0.0)
        if inv is None:
            inv = eye - step
        else:
            inv = inv - dot(inv, dot(step, inv, NN, passes), NN, passes)
        size *= 2
    return inv


def normalised(act):
    factor = lax.rsqrt(jnp.sum(act * act, -1, keepdims=True) + 1e-06)
    return act * factor, factor


def forward_body(
    heads, prec, info_ref, proj_ref, conv_ref, head_ref, onorm_ref,
    z_ref, mixed_ref, out_ref, delta_ref, across_ref, state_out_ref, solve_ref, kk_ref, qk_ref,
    state_ref, tail_ref,
):
    @pl.when(pl.program_id(0) == 0)
    def _():
        state_ref[...] = jnp.zeros_like(state_ref)
        tail_ref[...] = jnp.zeros_like(tail_ref)

    info = info_ref[...]
    beta, g, pre, total, across = token_scalars(info, head_ref[...], heads)
    for h in range(heads):
        at = h * MIX
        cat = h * CONV
        part = proj_ref[:, at : at + CONV]
        ext = jnp.concatenate([tail_ref[:, cat : cat + CONV], part], 0)
        tail_ref[:, cat : cat + CONV] = part[CHUNK - 8 :]
        mixed = conv_ref[TAPS - 1 : TAPS, cat : cat + CONV] * part
        for s in range(1, TAPS):
            shifted = ext[8 - s : 8 - s + CHUNK]
            mixed = mixed + conv_ref[TAPS - 1 - s : TAPS - s, cat : cat + CONV] * jnp.where(
                info[:, s : s + 1] > 0.5, shifted, 0.0
            )
        mixed_ref[:, cat : cat + CONV] = mixed
        act = mixed * sigmoid(mixed)
        query, _ = normalised(act[:, :DK])
        query = query * DK ** (-0.5)
        key, _ = normalised(act[:, DK : 2 * DK])
        value = act[:, 2 * DK :]
        decay, strict, beta_col, carried, end, carried_last = head_scalars(
            h, heads, info, beta, total, across
        )
        inner = dot(jnp.concatenate([key, query], 0), key, NT, prec["kk"])
        kk = inner[:CHUNK]
        qk = inner[CHUNK:]
        kk_ref[0, h] = kk
        qk_ref[0, h] = qk
        inv = invert(beta_col * strict * kk, prec["inv"])
        solve_ref[0, h] = inv
        sides = jnp.concatenate([beta_col * value, (beta_col * carried) * key], 1)
        solved = dot(inv, sides, NN, prec["solve"])
        state = state_ref[h]
        state_out_ref[0, h] = state
        reads = dot(
            jnp.concatenate([carried * query, solved[:, DV:]], 0), state, NN, prec["state"]
        )
        delta = solved[:, :DV] - reads[CHUNK:]
        result = reads[:CHUNK] + dot(decay * qk, delta, NN, prec["attend"])
        state_ref[h] = carried_last * state + dot(end * key, delta, TN, prec["state"])
        across_ref[:, h * DK : (h + 1) * DK] = solved[:, DV:]
        delta_ref[:, h * DV : (h + 1) * DV] = delta
        out_ref[:, h * DV : (h + 1) * DV] = result
        gate = proj_ref[:, at + CONV : at + MIX]
        factor = lax.rsqrt(jnp.mean(result * result, -1, keepdims=True) + 1e-05)
        z = result * factor * onorm_ref[:, h * DV : (h + 1) * DV] * (gate * sigmoid(gate))
        z_ref[:, h * DV : (h + 1) * DV] = z.astype(bf16)


def backward_body(
    heads, prec, info_ref, proj_ref, conv_ref, head_ref, onorm_ref,
    mixed_ref, out_ref, delta_ref, across_ref, state_in_ref, solve_ref, kk_ref, qk_ref, dz_ref,
    dproj_ref, dsmall_ref, dconv_ref, dhead_ref, donorm_ref,
    dstate_ref, lead_ref,
):
    @pl.when(pl.program_id(0) == 0)
    def _():
        dstate_ref[...] = jnp.zeros_like(dstate_ref)
        lead_ref[...] = jnp.zeros_like(lead_ref)
        dconv_ref[...] = jnp.zeros_like(dconv_ref)
        dhead_ref[...] = jnp.zeros_like(dhead_ref)
        donorm_ref[...] = jnp.zeros_like(donorm_ref)

    info = info_ref[...]
    beta, g, pre, total, across = token_scalars(info, head_ref[...], heads)
    row, col = iotas()
    lane = lax.broadcasted_iota(jnp.int32, (CHUNK, LANES), 1)
    dbeta_all = jnp.zeros((CHUNK, LANES), f32)
    reach_all = jnp.zeros((CHUNK, LANES), f32)
    leave_all = jnp.zeros((CHUNK, LANES), f32)
    spans_all = jnp.zeros((CHUNK, LANES), f32)
    from_here = (row <= col).astype(bf16)
    for h in range(heads):
        at = h * MIX
        cat = h * CONV
        mixed = mixed_ref[:, cat : cat + CONV]
        msig = sigmoid(mixed)
        act = mixed * msig
        q_unit, q_factor = normalised(act[:, :DK])
        query = q_unit * DK ** (-0.5)
        key, k_factor = normalised(act[:, DK : 2 * DK])
        value = act[:, 2 * DK :]
        decay, strict, beta_col, carried, end, carried_last = head_scalars(
            h, heads, info, beta, total, across
        )
        kk = kk_ref[0, h]
        qk = qk_ref[0, h]
        inv = solve_ref[0, h]
        delta = delta_ref[:, h * DV : (h + 1) * DV]
        across_w = across_ref[:, h * DK : (h + 1) * DK]
        result = out_ref[:, h * DV : (h + 1) * DV]
        state = state_in_ref[0, h]
        dnext = dstate_ref[h]
        gate = proj_ref[:, at + CONV : at + MIX]
        gsig = sigmoid(gate)
        silu = gate * gsig
        onorm = onorm_ref[:, h * DV : (h + 1) * DV]
        factor = lax.rsqrt(jnp.mean(result * result, -1, keepdims=True) + 1e-05)
        normed = result * factor
        dz = dz_ref[:, h * DV : (h + 1) * DV].astype(f32)
        dzn = dz * normed
        donorm_ref[:, h * DV : (h + 1) * DV] += jnp.sum(dzn * silu, 0, keepdims=True)
        dgate = dzn * onorm * (gsig * (1.0 + gate * (1.0 - gsig)))
        dproj_ref[:, at + CONV : at + MIX] = dgate.astype(bf16)
        dnormed = dz * onorm * silu
        dout = factor * (dnormed - normed * jnp.mean(dnormed * normed, -1, keepdims=True))
        ends = end * key
        ddelta = dot(decay * qk, dout, TN, prec["attend"]) + dot(ends, dnext, NN, prec["state"])
        dstate_ref[h] = carried_last * dnext + dot(
            jnp.concatenate([carried * query, -across_w], 0),
            jnp.concatenate([dout, ddelta], 0),
            TN,
            prec["state"],
        )
        x = dot(inv, ddelta, TN, prec["solve"])
        big = dot(
            jnp.concatenate([dout, x], 0), jnp.concatenate([state, delta], 0), NT, prec["big"]
        )
        dqc = big[:CHUNK, :DK]
        dp = big[:CHUNK, DK:]
        dkb = -big[CHUNK:, :DK]
        dm = -big[CHUNK:, DK:]
        dend = dot(delta, dnext, NT, prec["big"])
        dcl = jnp.sum(jnp.sum(state * dnext, 0, keepdims=True), 1, keepdims=True)
        dqk = decay * dp
        das = strict * dm
        rows = dot(jnp.concatenate([dqk, das], 0), key, NN, prec["kk"])
        dq = rows[:CHUNK] + carried * dqc
        das_k = rows[CHUNK:]
        bdas = beta_col * das
        cols = dot(
            jnp.concatenate([dqk, bdas], 0),
            jnp.concatenate([query, key], 0),
            TN,
            prec["kk"],
        )
        dk_end = end * dend
        dkb_c = carried * dkb
        dk_row_b = das_k + dkb_c
        dk = beta_col * dk_row_b + cols + dk_end
        xv = x * value
        dbeta = jnp.sum(xv[:, :DK] + xv[:, DK:] + key * dk_row_b, -1, keepdims=True)
        reach = jnp.sum(query * (carried * dqc) + key * (beta_col * dkb_c), -1, keepdims=True)
        leave = jnp.sum(key * dk_end, -1, keepdims=True)
        pairs = jnp.where(row > col, dqk * qk + bdas * kk, 0.0)
        pairs = exact_left(from_here, pairs)
        spans = jnp.sum(jnp.where(row > col, pairs, 0.0), -1, keepdims=True) + carried_last * dcl
        dbeta_all = jnp.where(lane == BETA_AT + h, dbeta, dbeta_all)
        at_h = lane == BETA_AT + heads + h
        reach_all = jnp.where(at_h, reach, reach_all)
        leave_all = jnp.where(at_h, leave, leave_all)
        spans_all = jnp.where(at_h, spans, spans_all)
        dv = beta_col * x
        scale_q = DK ** (-0.5) * q_factor
        daq = scale_q * (dq - q_unit * jnp.sum(q_unit * dq, -1, keepdims=True))
        dak = k_factor * (dk - key * jnp.sum(key * dk, -1, keepdims=True))
        dact = jnp.concatenate([daq, dak, dv], 1)
        dmixed = dact * (msig * (1.0 + mixed * (1.0 - msig)))
        ext = jnp.concatenate([dmixed, lead_ref[:, cat : cat + CONV]], 0)
        lead_ref[:, cat : cat + CONV] = dmixed[:8]
        part = proj_ref[:, at : at + CONV]
        dpart = conv_ref[TAPS - 1 : TAPS, cat : cat + CONV] * dmixed
        dconv_ref[TAPS - 1 : TAPS, cat : cat + CONV] += jnp.sum(dmixed * part, 0, keepdims=True)
        for s in range(1, TAPS):
            shifted = jnp.where(info[:, 3 + s : 4 + s] > 0.5, ext[s : s + CHUNK], 0.0)
            dpart = dpart + conv_ref[TAPS - 1 - s : TAPS - s, cat : cat + CONV] * shifted
            dconv_ref[TAPS - 1 - s : TAPS - s, cat : cat + CONV] += jnp.sum(
                shifted * part, 0, keepdims=True
            )
        dproj_ref[:, at : at + CONV] = dpart.astype(bf16)
    dg = spans_all + exact_left(from_here, reach_all)
    dg = dg + exact_left((row > col).astype(bf16), leave_all)
    rate = -jnp.exp(head_ref[0:1])
    dpre = dg * rate * sigmoid(pre)
    dsmall_ref[...] = dbeta_all * beta * (1.0 - beta) + dpre
    dhead_ref[0:1] += jnp.sum(dg * g, 0, keepdims=True)
    dhead_ref[1:2] += jnp.sum(dpre, 0, keepdims=True)


PREC = {"kk": 3, "inv": 3, "solve": 3, "state": 3, "attend": 3, "big": 3}
BUDGET = 56 << 20


def mixer_forward(info, proj, conv, head_rows, onorm, heads, prec=PREC):
    length = proj.shape[0]
    count = length // CHUNK
    chunk = lambda width: pl.BlockSpec((CHUNK, width), lambda c: (c, 0))
    whole = lambda rows, width: pl.BlockSpec((rows, width), lambda c: (0, 0))
    square = lambda rows, width: pl.BlockSpec((1, heads, rows, width), lambda c: (c, 0, 0, 0))
    return pl.pallas_call(
        functools.partial(forward_body, heads, prec),
        grid=(count,),
        in_specs=[
            chunk(LANES), chunk(heads * MIX), whole(TAPS, heads * CONV), whole(8, LANES),
            whole(1, heads * DV),
        ],
        out_specs=[
            chunk(heads * DV), chunk(heads * CONV), chunk(heads * DV), chunk(heads * DV),
            chunk(heads * DK), square(DK, DV), square(CHUNK, CHUNK), square(CHUNK, CHUNK),
            square(CHUNK, CHUNK),
        ],
        out_shape=[
            jax.ShapeDtypeStruct((length, heads * DV), bf16),
            jax.ShapeDtypeStruct((length, heads * CONV), f32),
            jax.ShapeDtypeStruct((length, heads * DV), f32),
            jax.ShapeDtypeStruct((length, heads * DV), f32),
            jax.ShapeDtypeStruct((length, heads * DK), f32),
            jax.ShapeDtypeStruct((count, heads, DK, DV), f32),
            jax.ShapeDtypeStruct((count, heads, CHUNK, CHUNK), f32),
            jax.ShapeDtypeStruct((count, heads, CHUNK, CHUNK), f32),
            jax.ShapeDtypeStruct((count, heads, CHUNK, CHUNK), f32),
        ],
        scratch_shapes=[
            pltpu.VMEM((heads, DK, DV), f32),
            pltpu.VMEM((8, heads * CONV), f32),
        ],
        compiler_params=pltpu.CompilerParams(
            dimension_semantics=("arbitrary",), vmem_limit_bytes=BUDGET
        ),
        name="mixer_forward",
    )(info, proj, conv, head_rows, onorm)


def mixer_backward(info, proj, conv, head_rows, onorm, kept, dz, heads, prec=PREC):
    length = proj.shape[0]
    count = length // CHUNK
    chunk = lambda width: pl.BlockSpec((CHUNK, width), lambda c: (count - 1 - c, 0))
    whole = lambda rows, width: pl.BlockSpec((rows, width), lambda c: (0, 0))
    square = lambda rows, width: pl.BlockSpec(
        (1, heads, rows, width), lambda c: (count - 1 - c, 0, 0, 0)
    )
    return pl.pallas_call(
        functools.partial(backward_body, heads, prec),
        grid=(count,),
        in_specs=[
            chunk(LANES), chunk(heads * MIX), whole(TAPS, heads * CONV), whole(8, LANES),
            whole(1, heads * DV),
            chunk(heads * CONV), chunk(heads * DV), chunk(heads * DV),
            chunk(heads * DK), square(DK, DV), square(CHUNK, CHUNK), square(CHUNK, CHUNK),
            square(CHUNK, CHUNK), chunk(heads * DV),
        ],
        out_specs=[
            chunk(heads * MIX), chunk(LANES), whole(TAPS, heads * CONV), whole(8, LANES),
            whole(1, heads * DV),
        ],
        out_shape=[
            jax.ShapeDtypeStruct((length, heads * MIX), bf16),
            jax.ShapeDtypeStruct((length, LANES), f32),
            jax.ShapeDtypeStruct((TAPS, heads * CONV), f32),
            jax.ShapeDtypeStruct((8, LANES), f32),
            jax.ShapeDtypeStruct((1, heads * DV), f32),
        ],
        scratch_shapes=[
            pltpu.VMEM((heads, DK, DV), f32),
            pltpu.VMEM((8, heads * CONV), f32),
        ],
        compiler_params=pltpu.CompilerParams(
            dimension_semantics=("arbitrary",), vmem_limit_bytes=BUDGET
        ),
        name="mixer_backward",
    )(info, proj, conv, head_rows, onorm, *kept, dz)


def token_info(segments, small):
    length = segments.shape[-1]
    seg = segments.reshape(length)
    heads = small.shape[-1]
    columns = [seg.astype(f32)]
    for s in range(1, TAPS):
        before = jnp.concatenate([jnp.full((s,), -1, seg.dtype), seg[:-s]])
        columns.append((before == seg).astype(f32))
    for s in range(1, TAPS):
        after = jnp.concatenate([seg[s:], jnp.full((s,), -1, seg.dtype)])
        columns.append((after == seg).astype(f32))
    ends = seg.reshape(-1, CHUNK)[:, -1]
    ends = jnp.concatenate([jnp.full((1,), -1, seg.dtype), ends[:-1]])
    columns.append((jnp.repeat(ends, CHUNK) == seg).astype(f32))
    info = jnp.stack(columns, 1)
    info = jnp.concatenate([info, small.reshape(length, 2 * heads)], 1)
    return jnp.pad(info, ((0, 0), (0, LANES - BETA_AT - 2 * heads)))


def head_lanes(head):
    heads = head.shape[1]
    return jnp.pad(head, ((0, 6), (BETA_AT + heads, LANES - BETA_AT - 2 * heads)))


def norm_factor(values):
    return lax.rsqrt(jnp.mean(values * values, -1, keepdims=True) + 1e-06)


def norm_backward(grad_out, scaled, factor, gain):
    grad_scaled = grad_out * gain
    grad_input = factor * (grad_scaled - scaled * jnp.mean(grad_scaled * scaled, -1, keepdims=True))
    return (grad_input, jnp.sum(grad_out * scaled, 0))


def product(left, right, dims):
    return lax.dot_general(left, right, (dims, ((), ())), preferred_element_type=f32)


def shards(
    tokens, cotangent, segments, norm_gains, mixer_in, mixer_small, conv_weight, head_params,
    out_norm, mixer_out, ffn_in, ffn_out,
):
    heads = mixer_in.shape[1] // MIX
    all_heads = head_params.shape[1]
    head_start = lax.axis_index("tensor") * heads
    head_local = lax.dynamic_slice_in_dim(head_params, head_start, heads, 1)
    gains = norm_gains.astype(f32)
    inputs = tokens.astype(f32)
    factor_one = norm_factor(inputs)
    scaled_one = inputs * factor_one
    normed_one = (scaled_one * gains[0]).astype(bf16)
    rows_one = lax.all_gather(normed_one, "tensor", axis=0, tiled=True)
    small_shapes = [mixer_small.shape, conv_weight.shape, out_norm.shape]
    small_dims = [1, 2, 1]
    packed = jnp.concatenate([mixer_small.reshape(-1), conv_weight.reshape(-1), out_norm.reshape(-1)])
    gathered = lax.all_gather(packed, "dp", axis=0, tiled=False)
    ways = gathered.shape[0]
    pieces = []
    offset = 0
    for shape, dim in zip(small_shapes, small_dims):
        size = 1
        for extent in shape:
            size *= extent
        piece = gathered[:, offset : offset + size].reshape((ways,) + shape)
        piece = jnp.moveaxis(piece, 0, dim)
        pieces.append(
            piece.reshape(shape[:dim] + (ways * shape[dim],) + shape[dim + 1 :])
        )
        offset += size
    w_small, w_conv, w_onorm = pieces
    w_in = lax.all_gather(mixer_in, "dp", axis=0, tiled=True)
    w_out = lax.all_gather(mixer_out, "dp", axis=1, tiled=True)
    group = rows_one.shape[0]
    proj = product(rows_one, w_in, NN)
    small = jnp.einsum("nd,cdh->nch", rows_one, w_small, preferred_element_type=f32)
    info = token_info(segments, small)
    conv_rows = w_conv.astype(f32).reshape(TAPS, heads * CONV)
    onorm_row = w_onorm.astype(f32).reshape(1, heads * DV)
    head_rows = head_lanes(head_local)
    mixed, *kept = mixer_forward(info, proj, conv_rows, head_rows, onorm_row, heads)
    middle = inputs + lax.psum_scatter(
        product(mixed, w_out, NN).astype(bf16), "tensor", scatter_dimension=0, tiled=True
    ).astype(f32)
    factor_two = norm_factor(middle)
    scaled_two = middle * factor_two
    normed_two = (scaled_two * gains[1]).astype(bf16)
    rows_two = lax.all_gather(normed_two, "tensor", axis=0, tiled=True)
    w_ffn = lax.all_gather(ffn_in, "dp", axis=1, tiled=True)
    w_down = lax.all_gather(ffn_out, "dp", axis=1, tiled=True)
    grad_rows = lax.all_gather(cotangent, "tensor", axis=0, tiled=True)
    gate_part = product(rows_two, w_ffn[0], NN)
    up_part = product(rows_two, w_ffn[1], NN)
    sigma = jax.nn.sigmoid(gate_part)
    activ = gate_part * sigma
    hidden = (activ * up_part).astype(bf16)
    result = middle + lax.psum_scatter(
        product(hidden, w_down, NN).astype(bf16), "tensor", scatter_dimension=0, tiled=True
    ).astype(f32)
    grad_hidden = product(grad_rows, w_down, NT)
    grad_down = product(hidden, grad_rows, TN)
    grad_gate = (grad_hidden * up_part * sigma * (1.0 + gate_part * (1.0 - sigma))).astype(bf16)
    grad_up = (grad_hidden * activ).astype(bf16)
    grad_normed_two = lax.psum_scatter(
        (product(grad_gate, w_ffn[0], NT) + product(grad_up, w_ffn[1], NT)).astype(bf16),
        "tensor",
        scatter_dimension=0,
        tiled=True,
    ).astype(f32)
    grad_ffn = jnp.stack([product(rows_two, grad_gate, TN), product(rows_two, grad_up, TN)])
    grad_middle_norm, grad_gain_two = norm_backward(
        grad_normed_two, scaled_two, factor_two, gains[1]
    )
    grad_middle = cotangent.astype(f32) + grad_middle_norm
    out_ffn = lax.psum_scatter(grad_ffn.astype(bf16), "dp", scatter_dimension=1, tiled=True)
    out_down = lax.psum_scatter(grad_down.astype(bf16), "dp", scatter_dimension=1, tiled=True)
    branch_grad = lax.all_gather(grad_middle.astype(bf16), "tensor", axis=0, tiled=True)
    grad_mixed = product(branch_grad, w_out, NT)
    grad_out = product(mixed, branch_grad, TN)
    grad_proj, grad_info, grad_conv, grad_head, grad_onorm = mixer_backward(
        info, proj, conv_rows, head_rows, onorm_row, kept, grad_mixed, heads
    )
    grad_small = grad_info[:, BETA_AT : BETA_AT + 2 * heads].reshape(group, 2, heads).astype(bf16)
    grad_normed_one = product(grad_proj, w_in, NT) + jnp.einsum(
        "nch,cdh->nd", grad_small, w_small, preferred_element_type=f32
    )
    grad_gain_one = jnp.sum(grad_normed_one * rows_one.astype(f32), 0) / gains[0]
    grad_normed_one = lax.psum_scatter(
        grad_normed_one.astype(bf16), "tensor", scatter_dimension=0, tiled=True
    ).astype(f32)
    grad_in = product(rows_one, grad_proj, TN)
    grad_small_w = jnp.einsum("nd,nch->cdh", rows_one, grad_small, preferred_element_type=f32)
    head_full = lax.dynamic_update_slice_in_dim(
        jnp.zeros((2, all_heads), f32),
        grad_head[:2, BETA_AT + heads : BETA_AT + 2 * heads],
        head_start,
        1,
    )
    gain_total, head_total = lax.psum(
        (jnp.stack([grad_gain_one, grad_gain_two]), head_full), ("dp", "tensor")
    )
    grad_scaled = grad_normed_one * gains[0]
    grad_tokens = grad_middle + factor_one * (
        grad_scaled - scaled_one * jnp.mean(grad_scaled * scaled_one, -1, keepdims=True)
    )
    out_in = lax.psum_scatter(grad_in.astype(bf16), "dp", scatter_dimension=0, tiled=True)
    out_out = lax.psum_scatter(grad_out.astype(bf16), "dp", scatter_dimension=1, tiled=True)
    smalls = [
        grad_small_w,
        grad_conv.reshape(TAPS, heads, CONV),
        grad_onorm.reshape(heads, DV),
    ]
    flat = []
    for value, dim in zip(smalls, small_dims):
        shape = value.shape
        value = value.reshape(shape[:dim] + (ways, shape[dim] // ways) + shape[dim + 1 :])
        flat.append(jnp.moveaxis(value, dim, 0).reshape(ways, -1))
    flat = lax.psum_scatter(
        jnp.concatenate(flat, 1).astype(bf16), "dp", scatter_dimension=0, tiled=False
    ).astype(f32)
    outs = []
    offset = 0
    for shape in small_shapes:
        size = 1
        for extent in shape:
            size *= extent
        outs.append(flat[offset : offset + size].reshape(shape))
        offset += size
    return (
        result.astype(bf16),
        grad_tokens,
        gain_total,
        out_in.astype(f32),
        outs[0],
        outs[1],
        head_total,
        outs[2],
        out_out.astype(f32),
        out_ffn.astype(f32),
        out_down.astype(f32),
    )


def solution(mesh):
    in_specs = (
        P(("dp", "tensor"), None),
        P(("dp", "tensor"), None),
        P("dp", None),
        P(),
        P("dp", "tensor"),
        P(None, "dp", "tensor"),
        P(None, "tensor", "dp"),
        P(),
        P("tensor", "dp"),
        P("tensor", "dp"),
        P(None, "dp", "tensor"),
        P("tensor", "dp"),
    )
    out_specs = (
        P(("dp", "tensor"), None),
        P(("dp", "tensor"), None),
        P(),
        P("dp", "tensor"),
        P(None, "dp", "tensor"),
        P(None, "tensor", "dp"),
        P(),
        P("tensor", "dp"),
        P("tensor", "dp"),
        P(None, "dp", "tensor"),
        P("tensor", "dp"),
    )
    return jax.shard_map(shards, mesh=mesh, in_specs=in_specs, out_specs=out_specs, check_vma=False)
```

```python
import functools
import jax
import jax.numpy as jnp
from jax import lax
from jax.experimental import pallas as pl
from jax.experimental.pallas import tpu as pltpu
from jax.sharding import PartitionSpec as P

DK = 128
DV = 256
MIX = 2 * DK + 2 * DV
CONV = 2 * DK + DV
CHUNK = 128
LANES = 128
TAPS = 4
BASE = 16
PER = 2
BACK = 2
PARTS = 2
BETA_AT = 8

NN = ((1,), (0,))
NT = ((1,), (1,))
TN = ((0,), (0,))

f32 = jnp.float32
bf16 = jnp.bfloat16


def dot(a, b, dims, passes):
    if passes == 6:
        return lax.dot_general(
            a, b, (dims, ((), ())), precision=lax.Precision.HIGHEST, preferred_element_type=f32
        )
    a_hi = a.astype(bf16)
    b_hi = b.astype(bf16)
    out = lax.dot_general(a_hi, b_hi, (dims, ((), ())), preferred_element_type=f32)
    if passes == 3:
        a_lo = (a - a_hi.astype(f32)).astype(bf16)
        b_lo = (b - b_hi.astype(f32)).astype(bf16)
        out = out + lax.dot_general(a_hi, b_lo, (dims, ((), ())), preferred_element_type=f32)
        out = out + lax.dot_general(a_lo, b_hi, (dims, ((), ())), preferred_element_type=f32)
    return out


def exact_left(mask, b):
    hi = b.astype(bf16)
    rest = b - hi.astype(f32)
    mid = rest.astype(bf16)
    low = (rest - mid.astype(f32)).astype(bf16)
    out = lax.dot_general(mask, hi, (NN, ((), ())), preferred_element_type=f32)
    out = out + lax.dot_general(mask, mid, (NN, ((), ())), preferred_element_type=f32)
    return out + lax.dot_general(mask, low, (NN, ((), ())), preferred_element_type=f32)


def sigmoid(x):
    return 1.0 / (1.0 + jnp.exp(-x))


def log1p(y):
    return jnp.where(y < 1e-4, y - 0.5 * y * y, jnp.log(1.0 + y))


def softplus(x):
    return jnp.maximum(x, 0.0) + log1p(jnp.exp(-jnp.abs(x)))


def iotas():
    shape = (CHUNK, CHUNK)
    return lax.broadcasted_iota(jnp.int32, shape, 0), lax.broadcasted_iota(jnp.int32, shape, 1)


def token_scalars(info, head_rows, heads):
    row, col = iotas()
    beta = sigmoid(info)
    rate = -jnp.exp(head_rows[0:1])
    pre = info + head_rows[1:2]
    g = rate * softplus(pre)
    total = exact_left((row >= col).astype(bf16), g)
    lane = lax.broadcasted_iota(jnp.int32, (CHUNK, LANES), 1)
    across = jnp.where(lane < BETA_AT, info, total).T
    return beta, g, pre, total, across


def head_scalars(h, heads, info, beta, total, across):
    row, col = iotas()
    at = BETA_AT + heads + h
    seg_col = info[:, 0:1]
    seg_row = across[0:1, :]
    tot_col = total[:, at : at + 1]
    tot_row = across[at : at + 1, :]
    keep = (seg_col == seg_row) & (row >= col)
    decay = jnp.exp(jnp.where(keep, tot_col - tot_row, -1e30))
    strict = jnp.where(row > col, decay, 0.0)
    beta_col = beta[:, BETA_AT + h : BETA_AT + h + 1]
    carried = jnp.exp(tot_col) * info[:, 7:8]
    last = CHUNK - 1
    end = jnp.where(
        seg_col == seg_col[last : last + 1], jnp.exp(tot_col[last : last + 1] - tot_col), 0.0
    )
    carried_last = carried[last : last + 1]
    return decay, strict, beta_col, carried, end, carried_last


def invert(lowers, passes):
    row, col = iotas()
    shape = (BASE, CHUNK)
    lane = lax.broadcasted_iota(jnp.int32, shape, 1)
    own = lax.broadcasted_iota(jnp.int32, shape, 0)
    start = lane // BASE * BASE
    blocks = CHUNK // BASE
    inside = [lane // BASE == b for b in range(blocks)]
    packs = []
    for lower in lowers:
        packed = jnp.zeros(shape, f32)
        for b in range(blocks):
            packed = jnp.where(inside[b], lower[b * BASE : (b + 1) * BASE], packed)
        packs.append(packed)
    invs = [jnp.where(own == lane % BASE, 1.0, 0.0)] * len(lowers)
    for j in range(BASE - 1):
        at = start + j
        invs = [
            inv - jnp.take_along_axis(packed, at, axis=1) * inv[j : j + 1]
            for inv, packed in zip(invs, packs)
        ]
    invs = [
        jnp.concatenate([jnp.where(inside[b], inv, 0.0) for b in range(blocks)], 0) for inv in invs
    ]
    size = BASE
    while size < CHUNK:
        part = ((row // (2 * size)) == (col // (2 * size))) & ((row // size) != (col // size))
        steps = [
            dot(jnp.where(part, lower, 0.0), inv, NN, passes) for lower, inv in zip(lowers, invs)
        ]
        invs = [inv - dot(inv, step, NN, passes) for inv, step in zip(invs, steps)]
        size *= 2
    return invs


def normalised(act):
    factor = lax.rsqrt(jnp.sum(act * act, -1, keepdims=True) + 1e-06)
    return act * factor, factor


def with_scalars(places, extra, heads):
    lane = lax.broadcasted_iota(jnp.int32, places.shape, 1)
    return jnp.where((lane >= BETA_AT) & (lane < BETA_AT + 2 * heads), extra, places)


def forward_body(
    heads, prec, places_ref, proj_ref, conv_ref, head_ref, onorm_ref, state_in_ref, tail_in_ref,
    z_before_ref, z_ref, mixed_ref, out_ref, delta_ref, across_ref, state_out_ref, solve_ref, kk_ref, qk_ref,
    state_ref, tail_ref,
):
    @pl.when(pl.program_id(0) == 0)
    def _():
        state_ref[...] = state_in_ref[...]
        tail_ref[...] = tail_in_ref[...]

    rows = PER * CHUNK
    ready = {}
    first = {}
    infos = [
        with_scalars(
            places_ref[u * CHUNK : (u + 1) * CHUNK],
            proj_ref[u * CHUNK : (u + 1) * CHUNK, heads * MIX :],
            heads,
        )
        for u in range(PER)
    ]
    scalars = [token_scalars(info, head_ref[...], heads) for info in infos]
    for h in range(heads):
        at = h * MIX
        cat = h * CONV
        part = proj_ref[:, at : at + CONV]
        ext = jnp.concatenate([tail_ref[:, cat : cat + CONV], part], 0)
        tail_ref[:, cat : cat + CONV] = part[rows - 8 :]
        mixed = conv_ref[TAPS - 1 : TAPS, cat : cat + CONV] * part
        for s in range(1, TAPS):
            shifted = ext[8 - s : 8 - s + rows]
            mixed = mixed + conv_ref[TAPS - 1 - s : TAPS - s, cat : cat + CONV] * jnp.where(
                places_ref[:, s : s + 1] > 0.5, shifted, 0.0
            )
        mixed_ref[:, cat : cat + CONV] = mixed
        act = mixed * sigmoid(mixed)
        queries, _ = normalised(act[:, :DK])
        queries = queries * DK ** (-0.5)
        keys, _ = normalised(act[:, DK : 2 * DK])
        for u in range(PER):
            own = slice(u * CHUNK, (u + 1) * CHUNK)
            query = queries[own]
            key = keys[own]
            value = act[own, 2 * DK :]
            beta, g, pre, total, across = scalars[u]
            decay, strict, beta_col, carried, end, carried_last = head_scalars(
                h, heads, infos[u], beta, total, across
            )
            inner = dot(jnp.concatenate([key, query], 0), key, NT, prec["kk"])
            kk = inner[:CHUNK]
            qk = inner[CHUNK:]
            kk_ref[u, h] = kk
            qk_ref[u, h] = qk
            first[u, h] = (
                beta_col * strict * kk,
                jnp.concatenate([beta_col * value, (beta_col * carried) * key], 1),
                carried * query, decay * qk, end * key, carried_last,
            )
    order = list(first)
    for at, inv in zip(order, invert([first[at][0] for at in order], prec["inv"])):
        u, h = at
        own = slice(u * CHUNK, (u + 1) * CHUNK)
        lower, sides, reads_q, attend, ends, carried_last = first[at]
        solve_ref[u, h] = inv
        solved = dot(inv, sides, NN, prec["solve"])
        across_ref[own, h * DK : (h + 1) * DK] = solved[:, DV:]
        ready[at] = (
            jnp.concatenate([reads_q, solved[:, DV:]], 0), solved[:, :DV], attend, ends,
            carried_last,
        )
    for u in range(PER):
        own = slice(u * CHUNK, (u + 1) * CHUNK)
        for h in range(heads):
            readers, fixed, attend, ends, carried_last = ready[u, h]
            state = state_ref[h]
            state_out_ref[u, h] = state
            reads = dot(readers, state, NN, prec["state"])
            delta = fixed - reads[CHUNK:]
            state_ref[h] = carried_last * state + dot(ends, delta, TN, prec["state"])
            result = reads[:CHUNK] + dot(attend, delta, NN, prec["attend"])
            delta_ref[own, h * DV : (h + 1) * DV] = delta
            out_ref[own, h * DV : (h + 1) * DV] = result
            gate = proj_ref[own, h * MIX + CONV : (h + 1) * MIX]
            factor = lax.rsqrt(jnp.mean(result * result, -1, keepdims=True) + 1e-05)
            z = result * factor * onorm_ref[:, h * DV : (h + 1) * DV] * (gate * sigmoid(gate))
            z_ref[own, h * DV : (h + 1) * DV] = z.astype(bf16)


def backward_body(
    heads, prec, places_ref, proj_ref, conv_ref, head_ref, onorm_ref,
    mixed_ref, out_ref, delta_ref, across_ref, state_in_ref, solve_ref, kk_ref, qk_ref, dz_ref,
    dstate_in_ref, lead_in_ref, dconv_in_ref, dhead_in_ref, donorm_in_ref,
    dproj_before_ref, dproj_ref, dstate_ref, lead_ref, dconv_ref, dhead_ref, donorm_ref,
):
    @pl.when(pl.program_id(0) == 0)
    def _():
        dstate_ref[...] = dstate_in_ref[...]
        lead_ref[...] = lead_in_ref[...]
        dconv_ref[...] = dconv_in_ref[...]
        dhead_ref[...] = dhead_in_ref[...]
        donorm_ref[...] = donorm_in_ref[...]

    row, col = iotas()
    lane = lax.broadcasted_iota(jnp.int32, (CHUNK, LANES), 1)
    from_here = (row <= col).astype(bf16)
    items = [(u, h) for u in reversed(range(BACK)) for h in range(heads)]
    rows_of = {u: slice(u * CHUNK, (u + 1) * CHUNK) for u in range(BACK)}
    infos = {
        u: with_scalars(places_ref[rows_of[u]], proj_ref[rows_of[u], heads * MIX :], heads)
        for u in range(BACK)
    }
    scalars = {u: token_scalars(infos[u], head_ref[...], heads) for u in range(BACK)}
    made = {}
    for u, h in items:
        own = rows_of[u]
        cat = h * CONV
        at = h * MIX
        mixed = mixed_ref[own, cat : cat + CONV]
        msig = sigmoid(mixed)
        act = mixed * msig
        q_unit, q_factor = normalised(act[:, :DK])
        key, k_factor = normalised(act[:, DK : 2 * DK])
        value = act[:, 2 * DK :]
        beta, g, pre, total, across = scalars[u]
        decay, strict, beta_col, carried, end, carried_last = head_scalars(
            h, heads, infos[u], beta, total, across
        )
        result = out_ref[own, h * DV : (h + 1) * DV]
        gate = proj_ref[own, at + CONV : at + MIX]
        gsig = sigmoid(gate)
        silu = gate * gsig
        onorm = onorm_ref[:, h * DV : (h + 1) * DV]
        factor = lax.rsqrt(jnp.mean(result * result, -1, keepdims=True) + 1e-05)
        normed = result * factor
        dz = dz_ref[own, h * DV : (h + 1) * DV].astype(f32)
        dzn = dz * normed
        donorm_ref[:, h * DV : (h + 1) * DV] += jnp.sum(dzn * silu, 0, keepdims=True)
        dgate = dzn * onorm * (gsig * (1.0 + gate * (1.0 - gsig)))
        dproj_ref[own, at + CONV : at + MIX] = dgate.astype(bf16)
        dnormed = dz * onorm * silu
        dout = factor * (dnormed - normed * jnp.mean(dnormed * normed, -1, keepdims=True))
        through = dot(decay * qk_ref[u, h], dout, TN, prec["attend"])
        made[u, h] = (
            mixed, msig, q_unit, q_factor, key, k_factor, value, decay, strict, beta_col, carried,
            end, carried_last, dout, through,
        )
    chain = {}
    for u, h in items:
        own = rows_of[u]
        q_unit, key, carried, end, carried_last, dout, through = (
            made[u, h][i] for i in (2, 4, 10, 11, 12, 13, 14)
        )
        dnext = dstate_ref[h]
        ddelta = through + dot(end * key, dnext, NN, prec["state"])
        dstate_ref[h] = carried_last * dnext + dot(
            jnp.concatenate(
                [carried * (q_unit * DK ** (-0.5)), -across_ref[own, h * DK : (h + 1) * DK]], 0
            ),
            jnp.concatenate([dout, ddelta], 0),
            TN,
            prec["state"],
        )
        chain[u, h] = (dnext, ddelta)
    solved = {}
    for u, h in items:
        own = rows_of[u]
        dnext, ddelta = chain[u, h]
        delta = delta_ref[own, h * DV : (h + 1) * DV]
        state = state_in_ref[u, h]
        x = dot(solve_ref[u, h], ddelta, TN, prec["solve"])
        dend = dot(delta, dnext, NT, prec["big"])
        dcl = jnp.sum(jnp.sum(state * dnext, 0, keepdims=True), 1, keepdims=True)
        big = dot(
            jnp.concatenate([made[u, h][13], x], 0),
            jnp.concatenate([state, delta], 0),
            NT,
            prec["big"],
        )
        solved[u, h] = (x, dend, dcl, big)
    inner = {}
    for u, h in items:
        q_unit, key, decay, strict, beta_col = (made[u, h][i] for i in (2, 4, 7, 8, 9))
        x, dend, dcl, big = solved[u, h]
        query = q_unit * DK ** (-0.5)
        dqk = decay * big[:CHUNK, DK:]
        das = -strict * big[CHUNK:, DK:]
        bdas = beta_col * das
        rows = dot(jnp.concatenate([dqk, das], 0), key, NN, prec["kk"])
        cols = dot(
            jnp.concatenate([dqk, bdas], 0),
            jnp.concatenate([query, key], 0),
            TN,
            prec["kk"],
        )
        pairs = jnp.where(row > col, dqk * qk_ref[u, h] + bdas * kk_ref[u, h], 0.0)
        inner[u, h] = (rows, cols, exact_left(from_here, pairs))
    sums = {
        u: [jnp.zeros((CHUNK, LANES), f32) for _ in range(4)] for u in range(BACK)
    }
    dacts = {}
    for u, h in items:
        (
            mixed, msig, q_unit, q_factor, key, k_factor, value, decay, strict, beta_col, carried,
            end, carried_last, dout, through,
        ) = made[u, h]
        x, dend, dcl, big = solved[u, h]
        rows, cols, pairs = inner[u, h]
        query = q_unit * DK ** (-0.5)
        dqc = carried * big[:CHUNK, :DK]
        dq = rows[:CHUNK] + dqc
        dk_end = end * dend
        dkb_c = -carried * big[CHUNK:, :DK]
        dk_row_b = rows[CHUNK:] + dkb_c
        dk = beta_col * dk_row_b + cols + dk_end
        xv = x * value
        dbeta = jnp.sum(xv[:, :DK] + xv[:, DK:] + key * dk_row_b, -1, keepdims=True)
        reach = jnp.sum(query * dqc + key * (beta_col * dkb_c), -1, keepdims=True)
        leave = jnp.sum(key * dk_end, -1, keepdims=True)
        spans = jnp.sum(jnp.where(row > col, pairs, 0.0), -1, keepdims=True) + carried_last * dcl
        at_h = lane == BETA_AT + heads + h
        sums[u][0] = jnp.where(lane == BETA_AT + h, dbeta, sums[u][0])
        sums[u][1] = jnp.where(at_h, reach, sums[u][1])
        sums[u][2] = jnp.where(at_h, leave, sums[u][2])
        sums[u][3] = jnp.where(at_h, spans, sums[u][3])
        scale_q = DK ** (-0.5) * q_factor
        daq = scale_q * (dq - q_unit * jnp.sum(q_unit * dq, -1, keepdims=True))
        dak = k_factor * (dk - key * jnp.sum(key * dk, -1, keepdims=True))
        dact = jnp.concatenate([daq, dak, beta_col * x], 1)
        dacts[u, h] = dact * (msig * (1.0 + mixed * (1.0 - msig)))
    for h in range(heads):
        at = h * MIX
        cat = h * CONV
        dmixed = jnp.concatenate([dacts[u, h] for u in range(BACK)], 0)
        ext = jnp.concatenate([dmixed, lead_ref[:, cat : cat + CONV]], 0)
        lead_ref[:, cat : cat + CONV] = dmixed[:8]
        part = proj_ref[:, at : at + CONV]
        dpart = conv_ref[TAPS - 1 : TAPS, cat : cat + CONV] * dmixed
        dconv_ref[TAPS - 1 : TAPS, cat : cat + CONV] += jnp.sum(dmixed * part, 0, keepdims=True)
        for s in range(1, TAPS):
            shifted = jnp.where(
                places_ref[:, 3 + s : 4 + s] > 0.5, ext[s : s + BACK * CHUNK], 0.0
            )
            dpart = dpart + conv_ref[TAPS - 1 - s : TAPS - s, cat : cat + CONV] * shifted
            dconv_ref[TAPS - 1 - s : TAPS - s, cat : cat + CONV] += jnp.sum(
                shifted * part, 0, keepdims=True
            )
        dproj_ref[:, at : at + CONV] = dpart.astype(bf16)
    rate = -jnp.exp(head_ref[0:1])
    for u in range(BACK):
        beta, g, pre, total, across = scalars[u]
        dbeta_all, reach_all, leave_all, spans_all = sums[u]
        dg = spans_all + exact_left(from_here, reach_all)
        dg = dg + exact_left((row > col).astype(bf16), leave_all)
        dpre = dg * rate * sigmoid(pre)
        dsmall = dbeta_all * beta * (1.0 - beta) + dpre
        dproj_ref[rows_of[u], heads * MIX :] = dsmall.astype(bf16)
        dhead_ref[0:1] += jnp.sum(dg * g, 0, keepdims=True)
        dhead_ref[1:2] += jnp.sum(dpre, 0, keepdims=True)


PREC = {"kk": 3, "inv": 3, "solve": 3, "state": 3, "attend": 3, "big": 3}
BUDGET = 56 << 20


def whole(shape):
    return pl.BlockSpec(shape, lambda c: (0,) * len(shape))


def forward_start(heads):
    return [jnp.zeros((heads, DK, DV), f32), jnp.zeros((8, heads * CONV), f32)]


def mixer_forward(part, before, places, proj, conv, head_rows, onorm, carry, heads, prec=PREC):
    length = proj.shape[0] // PARTS
    count = length // CHUNK
    steps = count // PER
    token = lambda width: pl.BlockSpec((PER * CHUNK, width), lambda c: (part * steps + c, 0))
    chunk = lambda width: pl.BlockSpec((PER * CHUNK, width), lambda c: (c, 0))
    square = lambda rows, width: pl.BlockSpec((PER, heads, rows, width), lambda c: (c, 0, 0, 0))
    z, *kept = pl.pallas_call(
        functools.partial(forward_body, heads, prec),
        grid=(steps,),
        in_specs=[token(LANES), token(heads * MIX + LANES)]
        + [whole(x.shape) for x in (conv, head_rows, onorm, *carry)]
        + [pl.BlockSpec(memory_space=pl.ANY)],
        out_specs=[
            token(heads * DV), chunk(heads * CONV), chunk(heads * DV), chunk(heads * DV),
            chunk(heads * DK), square(DK, DV), square(CHUNK, CHUNK), square(CHUNK, CHUNK),
            square(CHUNK, CHUNK),
        ]
        + [whole(x.shape) for x in carry],
        out_shape=[
            jax.ShapeDtypeStruct((proj.shape[0], heads * DV), bf16),
            jax.ShapeDtypeStruct((length, heads * CONV), f32),
            jax.ShapeDtypeStruct((length, heads * DV), f32),
            jax.ShapeDtypeStruct((length, heads * DV), f32),
            jax.ShapeDtypeStruct((length, heads * DK), f32),
            jax.ShapeDtypeStruct((count, heads, DK, DV), f32),
            jax.ShapeDtypeStruct((count, heads, CHUNK, CHUNK), f32),
            jax.ShapeDtypeStruct((count, heads, CHUNK, CHUNK), f32),
            jax.ShapeDtypeStruct((count, heads, CHUNK, CHUNK), f32),
        ]
        + [jax.ShapeDtypeStruct(x.shape, f32) for x in carry],
        compiler_params=pltpu.CompilerParams(
            dimension_semantics=("arbitrary",), vmem_limit_bytes=BUDGET
        ),
        cost_estimate=pl.CostEstimate(
            flops=length * heads * 6000000, bytes_accessed=length * heads * 12000, transcendentals=0
        ),
        input_output_aliases={5 + len(carry): 0},
        name="mixer_forward",
    )(places, proj, conv, head_rows, onorm, *carry, before)
    return z, kept[:-2], kept[-2:]


def backward_start(heads):
    return [
        jnp.zeros((heads, DK, DV), f32), jnp.zeros((8, heads * CONV), f32),
        jnp.zeros((TAPS, heads * CONV), f32), jnp.zeros((8, LANES), f32),
        jnp.zeros((1, heads * DV), f32),
    ]


def mixer_backward(
    part, before, places, proj, conv, head_rows, onorm, kept, dz, carry, heads, prec=PREC
):
    length = proj.shape[0] // PARTS
    steps = length // (BACK * CHUNK)
    token = lambda width: pl.BlockSpec(
        (BACK * CHUNK, width), lambda c: (part * steps + steps - 1 - c, 0)
    )
    chunk = lambda width: pl.BlockSpec((BACK * CHUNK, width), lambda c: (steps - 1 - c, 0))
    square = lambda rows, width: pl.BlockSpec(
        (BACK, heads, rows, width), lambda c: (steps - 1 - c, 0, 0, 0)
    )
    dproj, *carry = pl.pallas_call(
        functools.partial(backward_body, heads, prec),
        grid=(steps,),
        in_specs=[token(LANES), token(heads * MIX + LANES)]
        + [whole(x.shape) for x in (conv, head_rows, onorm)]
        + [
            chunk(heads * CONV), chunk(heads * DV), chunk(heads * DV),
            chunk(heads * DK), square(DK, DV), square(CHUNK, CHUNK), square(CHUNK, CHUNK),
            square(CHUNK, CHUNK), token(heads * DV),
        ]
        + [whole(x.shape) for x in carry]
        + [pl.BlockSpec(memory_space=pl.ANY)],
        out_specs=[token(heads * MIX + LANES)] + [whole(x.shape) for x in carry],
        out_shape=[jax.ShapeDtypeStruct((proj.shape[0], heads * MIX + LANES), bf16)]
        + [jax.ShapeDtypeStruct(x.shape, f32) for x in carry],
        compiler_params=pltpu.CompilerParams(
            dimension_semantics=("arbitrary",), vmem_limit_bytes=BUDGET
        ),
        cost_estimate=pl.CostEstimate(
            flops=length * heads * 7000000, bytes_accessed=length * heads * 14000, transcendentals=0
        ),
        input_output_aliases={6 + len(kept) + len(carry): 0},
        name="mixer_backward",
    )(places, proj, conv, head_rows, onorm, *kept, dz, *carry, before)
    return dproj, carry


def token_places(segments):
    length = segments.shape[-1]
    seg = segments.reshape(length)
    columns = [seg.astype(f32)]
    for s in range(1, TAPS):
        before = jnp.concatenate([jnp.full((s,), -1, seg.dtype), seg[:-s]])
        columns.append((before == seg).astype(f32))
    for s in range(1, TAPS):
        beyond = jnp.concatenate([seg[s:], jnp.full((s,), -1, seg.dtype)])
        columns.append((beyond == seg).astype(f32))
    ends = seg.reshape(-1, CHUNK)[:, -1]
    ends = jnp.concatenate([jnp.full((1,), -1, seg.dtype), ends[:-1]])
    columns.append((jnp.repeat(ends, CHUNK) == seg).astype(f32))
    return jnp.pad(jnp.stack(columns, 1), ((0, 0), (0, LANES - len(columns))))


def head_lanes(head):
    heads = head.shape[1]
    return jnp.pad(head, ((0, 6), (BETA_AT + heads, LANES - BETA_AT - 2 * heads)))


def ffn_body(rows_ref, cot_ref, w_ref, gate_ref, up_ref, hidden_ref, back_ref, out_ref):
    pieces, _, _, size = w_ref.shape

    def project(left_ref, which):
        total = None
        for p in range(pieces):
            part = lax.dot_general(
                left_ref[:, p * size : (p + 1) * size], w_ref[p, which], (NT, ((), ())),
                preferred_element_type=f32,
            )
            total = part if total is None else total + part
        return total

    gate = project(rows_ref, 0)
    up = project(rows_ref, 1)
    grad_hidden = project(cot_ref, 2)
    sigma = sigmoid(gate)
    activ = gate * sigma
    hidden = (activ * up).astype(bf16)
    grad_gate = (grad_hidden * up * sigma * (1.0 + gate * (1.0 - sigma))).astype(bf16)
    grad_up = (grad_hidden * activ).astype(bf16)
    hidden_ref[...] = hidden
    gate_ref[...] = grad_gate
    up_ref[...] = grad_up
    for p in range(pieces):
        own = slice(p * size, (p + 1) * size)
        back = lax.dot_general(
            grad_gate, w_ref[p, 0], (NN, ((), ())), preferred_element_type=f32
        )
        back = back + lax.dot_general(
            grad_up, w_ref[p, 1], (NN, ((), ())), preferred_element_type=f32
        )
        back_ref[:, own] = back.astype(bf16)
        out_ref[:, own] = lax.dot_general(
            hidden, w_ref[p, 2], (NN, ((), ())), preferred_element_type=f32
        ).astype(bf16)


FFN_TILE = 256


def ffn_both(rows, cot, weights):
    count, d = rows.shape
    hidden = weights.shape[2]
    tile = lambda width: pl.BlockSpec((FFN_TILE, width), lambda c: (c, 0))
    return pl.pallas_call(
        ffn_body,
        grid=(count // FFN_TILE,),
        in_specs=[
            tile(d), tile(d), pl.BlockSpec(weights.shape, lambda c: (0, 0, 0, 0)),
        ],
        out_specs=[tile(hidden), tile(hidden), tile(hidden), tile(d), tile(d)],
        out_shape=[
            jax.ShapeDtypeStruct((count, width), bf16) for width in (hidden, hidden, hidden, d, d)
        ],
        compiler_params=pltpu.CompilerParams(
            dimension_semantics=("arbitrary",), vmem_limit_bytes=BUDGET
        ),
        cost_estimate=pl.CostEstimate(
            flops=12 * count * d * hidden, bytes_accessed=8 * count * d, transcendentals=0
        ),
        name="ffn_both",
    )(rows, cot, weights)


def ffn_grads_body(rows_ref, cot_ref, gate_ref, up_ref, hidden_ref, out_ref):
    for i, (left, right) in enumerate(
        ((rows_ref, gate_ref), (rows_ref, up_ref), (cot_ref, hidden_ref))
    ):
        out_ref[0, i] = lax.dot_general(
            right[...], left[...], (TN, ((), ())), preferred_element_type=f32
        ).astype(bf16)


def ffn_weight_grads(rows, cot, gate, up, hidden, pieces):
    count, d = rows.shape
    width = hidden.shape[1]
    size = d // pieces
    column = pl.BlockSpec((count, size), lambda p: (0, p))
    whole = pl.BlockSpec((count, width), lambda p: (0, 0))
    return pl.pallas_call(
        ffn_grads_body,
        grid=(pieces,),
        in_specs=[column, column, whole, whole, whole],
        out_specs=pl.BlockSpec((1, 3, width, size), lambda p: (p, 0, 0, 0)),
        out_shape=jax.ShapeDtypeStruct((pieces, 3, width, size), bf16),
        compiler_params=pltpu.CompilerParams(
            dimension_semantics=("arbitrary",), vmem_limit_bytes=BUDGET
        ),
        cost_estimate=pl.CostEstimate(
            flops=6 * count * d * width, bytes_accessed=8 * count * d, transcendentals=0
        ),
        name="ffn_weight_grads",
    )(rows, cot, gate, up, hidden)


def norm_factor(values):
    return lax.rsqrt(jnp.mean(values * values, -1, keepdims=True) + 1e-06)


def norm_backward(grad_out, scaled, factor, gain):
    grad_scaled = grad_out * gain
    grad_input = factor * (grad_scaled - scaled * jnp.mean(grad_scaled * scaled, -1, keepdims=True))
    return (grad_input, jnp.sum(grad_out * scaled, 0))


def product(left, right, dims):
    return lax.dot_general(left, right, (dims, ((), ())), preferred_element_type=f32)


def after(x, done):
    return lax.optimization_barrier((x, done))[0]


def exchange(x, axis, bit):
    return lax.ppermute(x, axis, [(i, i ^ bit) for i in range(lax.axis_size(axis))])


def sum_everywhere(x, axes):
    for axis in axes:
        ways = lax.axis_size(axis)
        if ways & (ways - 1):
            x = lax.psum(x, axis)
            continue
        bit = 1
        while bit < ways:
            x = x + exchange(x, axis, bit)
            bit *= 2
    return x


def line_gather(x, axis):
    ways = lax.axis_size(axis)
    here = lax.axis_index(axis)
    up = [(i, i + 1) for i in range(ways - 1)]
    down = [(i + 1, i) for i in range(ways - 1)]
    below = [x]
    above = [x]
    for _ in range(ways - 1):
        below.append(lax.ppermute(below[-1], axis, up))
        above.append(lax.ppermute(above[-1], axis, down))
    blocks = []
    for slot in range(ways):
        block = x
        for at in range(ways):
            if at != slot:
                block = jnp.where(here == at, below[at - slot] if at > slot else above[slot - at], block)
        blocks.append(block)
    return jnp.concatenate(blocks, 0)


def line_scatter(x, axis):
    ways = lax.axis_size(axis)
    here = lax.axis_index(axis)
    size = x.shape[0] // ways
    up = [(i, i + 1) for i in range(ways - 1)]
    down = [(i + 1, i) for i in range(ways - 1)]

    def block(slot):
        return lax.dynamic_slice_in_dim(x, slot * size, size, 0).astype(f32)

    low = None
    high = None
    for k in range(1, ways):
        to_low = block(jnp.maximum(here - (ways - k), 0))
        to_high = block(jnp.minimum(here + (ways - k), ways - 1))
        if low is not None:
            to_low = to_low + low
            to_high = to_high + high
        low = lax.ppermute(to_low.astype(bf16), axis, down).astype(f32)
        high = lax.ppermute(to_high.astype(bf16), axis, up).astype(f32)
    return block(here) + low + high


def shifted(x, axis, by):
    ways = lax.axis_size(axis)
    return lax.ppermute(x, axis, [(i, (i + by) % ways) for i in range(ways)])


def ordered(parts, axis):
    ways = len(parts)
    here = lax.axis_index(axis)
    blocks = []
    for slot in range(ways):
        block = parts[0]
        for at in range(ways):
            if at != slot:
                block = jnp.where(here == at, parts[(at - slot) % ways], block)
        blocks.append(block)
    return blocks


def swap_parts(block_to, axis):
    ways = lax.axis_size(axis)
    here = lax.axis_index(axis)
    parts = [block_to(here)]
    for s in range(1, ways):
        parts.append(shifted(block_to((here + s) % ways), axis, s))
    return parts


def swap_blocks(block_to, axis):
    return ordered(swap_parts(block_to, axis), axis)


class OutWeights:

    def __init__(self, mixer_out):
        rows = mixer_out.T
        self.ways = lax.axis_size("dp")
        self.rows = jnp.concatenate(swap_blocks(lambda i: rows, "tensor"), 1)

    def start(self, started):
        if self.ways == 8:
            rows = after(self.rows, started)
            self.parts = {m: exchange(rows, "dp", m) for m in (2, 4, 6)}

    def finish(self, done):
        if self.ways != 8:
            return lax.all_gather(self.rows, "dp", axis=0, tiled=True)
        here = lax.axis_index("dp")
        parts = dict(zip((2, 4, 6), after([self.parts[m] for m in (2, 4, 6)], done)))
        parts[0] = self.rows
        size = self.rows.shape[0]
        out = jnp.zeros((self.ways * size, self.rows.shape[1]), bf16)
        for m in (0, 2, 4, 6):
            parts[m + 1] = exchange(parts[m], "dp", 1)
        for m, part in parts.items():
            out = lax.dynamic_update_slice_in_dim(out, part, (here ^ m) * size, 0)
        return out

    def start_sum(self, left, right):
        size = left.shape[1] // self.ways
        if self.ways != 8:
            grad = product(left, right, TN).astype(bf16)
            self.kept = lax.psum_scatter(grad, "dp", scatter_dimension=0, tiled=True)
            return self.kept
        core = lax.axis_index("dp") % 2
        blocks = [left[:, i * size : (i + 1) * size] for i in range(self.ways)]
        even = jnp.concatenate(blocks[::2], 1)
        odd = jnp.concatenate(blocks[1::2], 1)
        away = jnp.where(core == 0, odd, even)
        stay = jnp.where(core == 0, even, odd)
        came = exchange(product(away, right, TN).astype(bf16), "dp", 1)
        total = (product(stay, right, TN) + came.astype(f32)).astype(bf16)
        place = lax.axis_index("dp") // 2
        block = lambda i: lax.dynamic_slice_in_dim(total, i * size, size, 0)
        self.kept = block(place)
        self.parts = [exchange(block(place ^ (m // 2)), "dp", m) for m in (2, 4, 6)]
        return self.kept

    def finish_sum(self, width, done):
        total = self.kept
        if self.ways == 8:
            total = total.astype(f32)
            for part in after(self.parts, done):
                total = total + part.astype(f32)
            total = total.astype(bf16)
        blocks = swap_blocks(
            lambda i: lax.dynamic_slice_in_dim(total, i * width, width, 1), "tensor"
        )
        return sum(block.astype(f32) for block in blocks)


class LineFfn:

    def __init__(self, ffn_in, ffn_out, started):
        self.own = jnp.stack([ffn_in[0].T, ffn_in[1].T, ffn_out])
        self.ways = lax.axis_size("dp")

    def middle(self, done):
        return self.own

    def finish(self, done):
        weights = lax.all_gather(self.own, "dp", axis=2, tiled=True)
        return weights[None]

    def gather(self, x, done):
        return line_gather(x, "tensor")

    def scatter(self, x, work):
        grads = work(x)
        return line_scatter(x, "tensor"), grads

    def sum_planes(self, grads):
        return lax.psum_scatter(grads[0], "dp", scatter_dimension=2, tiled=True)

    def sums_middle(self, grads):
        return grads

    def send_sums(self, grads):
        return grads

    def own_grads(self, grads, came):
        return came.astype(f32)


TO_A = [(1, 0), (0, 2), (2, 3), (3, 1)]
TO_B = [(2, 1), (1, 2)]
BACK_A = [(0, 1), (2, 0), (3, 2), (1, 3)]
BACK_B = [(2, 1), (1, 2)]


class PairFfn:

    def __init__(self, ffn_in, ffn_out, started):
        self.core = lax.axis_index("dp") % 2
        self.here = lax.axis_index("tensor")
        ways = lax.axis_size("dp")
        self.groups = [list(range(0, ways, 2)), list(range(1, ways, 2))]
        self.own = after(jnp.stack([ffn_in[0].T, ffn_in[1].T, ffn_out]), started)
        self.a = lax.ppermute(self.own, "tensor", TO_A)
        self.b = lax.ppermute(self.own, "tensor", TO_B)

    def middle(self, done):
        here = self.here
        own, a, b = after((self.own, self.a, self.b), done)
        first = jnp.where(here == 0, own, jnp.where(here == 1, b, a))
        second = jnp.where(here == 3, own, jnp.where(here == 2, b, a))
        mine = jnp.where(self.core == 0, first, second)
        got = exchange(jnp.where(self.core == 0, second, first), "dp", 1)
        low = jnp.where(self.core == 0, mine, got)
        high = jnp.where(self.core == 0, got, mine)
        self.both = jnp.concatenate([low, high], 2)
        return self.both

    def finish(self, done):
        return lax.all_gather(
            self.both, "dp", axis=0, tiled=False, axis_index_groups=self.groups
        )

    def gather(self, x, done):
        far = exchange(x, "tensor", 1)
        if done is not None:
            far = after(far, done)
        return jnp.concatenate([x, exchange(x, "dp", 1), far, exchange(far, "dp", 1)], 0)

    def scatter(self, x, work):
        size = x.shape[0] // 4
        parts = [x[i * size : (i + 1) * size] for i in range(4)]
        far = (parts[2].astype(f32) + exchange(parts[3], "dp", 1).astype(f32)).astype(bf16)
        near = exchange(parts[1], "dp", 1)
        done = work(far)
        far = exchange(far, "tensor", 1)
        if done is not None:
            far = after(far, done)
        return parts[0].astype(f32) + near.astype(f32) + far.astype(f32), done

    def sum_planes(self, grads):
        return lax.psum_scatter(
            grads, "dp", scatter_dimension=0, tiled=False, axis_index_groups=self.groups
        )

    def sums_middle(self, grads):
        half = grads.shape[2] // 2
        low = grads[:, :, :half]
        high = grads[:, :, half:]
        core = self.core
        mine = jnp.where(core == 0, low, high)
        got = exchange(jnp.where(core == 0, high, low), "dp", 1)
        return jnp.where(core == 0, mine, got), jnp.where(core == 0, got, mine)

    def send_sums(self, sums):
        first, second = sums
        here = self.here
        a = lax.ppermute(jnp.where(here < 2, second, first), "tensor", BACK_A)
        b = lax.ppermute(jnp.where(here == 2, second, first), "tensor", BACK_B)
        return a, b

    def own_grads(self, sums, came):
        first, second = sums
        a, b = came
        here = self.here
        other = jnp.where(here == 0, first, jnp.where(here == 3, second, b))
        return a.astype(f32) + other.astype(f32)


CONV_AT = 64


def columns_of(value, dim, rows):
    ways = lax.axis_size("dp")
    shape = value.shape
    value = value.reshape(shape[:dim] + (ways, shape[dim] // ways) + shape[dim + 1 :])
    value = jnp.moveaxis(value, dim, 0).reshape(ways, -1)
    return column_blocks(value, rows)


def column_blocks(value, rows):
    ways, size = value.shape
    lanes = -(-size // rows)
    value = jnp.pad(value, ((0, 0), (0, lanes * rows - size)))
    return value.reshape(ways, lanes, rows).swapaxes(1, 2).reshape(ways * rows, lanes)


def from_columns(columns, shape, dim, rows):
    ways = columns.shape[0] // rows
    size = 1
    for extent in shape:
        size *= extent
    value = columns.reshape(ways, rows, -1).swapaxes(1, 2).reshape(ways, -1)[:, :size]
    value = jnp.moveaxis(value.reshape((ways,) + shape), 0, dim)
    return value.reshape(shape[:dim] + (ways * shape[dim],) + shape[dim + 1 :])


def lanes_of(small, conv, onorm):
    rows, width = small.shape
    used = BETA_AT + width
    rest = LANES - CONV_AT - conv.shape[1] - onorm.shape[1]
    zeros = lambda lanes: jnp.zeros((rows, lanes), small.dtype)
    return jnp.concatenate(
        [zeros(BETA_AT), small, zeros(CONV_AT - used), conv, onorm, zeros(rest)], 1
    )


def fetch_mixer(mixer_in, mixer_small, conv_weight, out_norm):
    rows, width = mixer_in.shape
    small = jnp.moveaxis(mixer_small, 0, 1).reshape(rows, -1)
    conv = column_blocks(conv_weight.reshape(1, -1), rows)
    onorm = column_blocks(out_norm.reshape(1, -1), rows)
    extended = jnp.concatenate([mixer_in, lanes_of(small, conv, onorm)], 1)
    w_in = lax.all_gather(extended, "dp", axis=0, tiled=True)
    at = width + CONV_AT
    w_conv = from_columns(w_in[:, at : at + conv.shape[1]], conv_weight.shape, 2, rows)
    at += conv.shape[1]
    w_onorm = from_columns(w_in[:, at : at + onorm.shape[1]], out_norm.shape, 1, rows)
    return w_in, w_conv, w_onorm


class MixerSums:

    def __init__(self, grad_in, grad_conv, grad_onorm, heads):
        self.heads = heads
        self.ways = lax.axis_size("dp")
        self.rows = grad_in.shape[0] // self.ways
        width = heads * MIX
        conv = columns_of(grad_conv, 2, self.rows)
        onorm = columns_of(grad_onorm, 1, self.rows)
        self.lanes = (conv.shape[1], onorm.shape[1])
        zeros = jnp.zeros((grad_in.shape[0], 2 * heads), f32)
        both = jnp.concatenate(
            [grad_in[:, :width], grad_in[:, width:] + lanes_of(zeros, conv, onorm)], 1
        )
        self.sent = both.astype(bf16)

    def outputs(self):
        heads = self.heads
        rows = self.rows
        width = heads * MIX
        summed = lax.psum_scatter(self.sent, "dp", scatter_dimension=0, tiled=True).astype(f32)
        small = summed[:, width + BETA_AT : width + BETA_AT + 2 * heads]
        at = width + CONV_AT
        shape = (TAPS, heads, CONV // self.ways)
        conv = from_columns(summed[:, at : at + self.lanes[0]], shape, 2, rows)
        at += self.lanes[0]
        shape = (heads, DV // self.ways)
        onorm = from_columns(summed[:, at : at + self.lanes[1]], shape, 1, rows)
        return (
            summed[:, :width], jnp.moveaxis(small.reshape(rows, 2, heads), 1, 0), conv, onorm,
        )


def shards(
    tokens, cotangent, segments, norm_gains, mixer_in, mixer_small, conv_weight, head_params,
    out_norm, mixer_out, ffn_in, ffn_out,
):
    heads = mixer_in.shape[1] // MIX
    all_heads = head_params.shape[1]
    ways = lax.axis_size("dp")
    teams = lax.axis_size("tensor")
    head_start = lax.axis_index("tensor") * heads
    head_local = lax.dynamic_slice_in_dim(head_params, head_start, heads, 1)
    gains = norm_gains.astype(f32)
    own = tokens.shape[0]
    inputs = tokens.astype(f32)
    factor_one = norm_factor(inputs)
    scaled_one = inputs * factor_one
    normed_one = (scaled_one * gains[0]).astype(bf16)
    out_weights = OutWeights(mixer_out)
    w_in, w_conv, w_onorm = fetch_mixer(mixer_in, mixer_small, conv_weight, out_norm)
    conv_rows = w_conv.astype(f32).reshape(TAPS, heads * CONV)
    onorm_row = w_onorm.astype(f32).reshape(1, heads * DV)
    head_rows = head_lanes(head_local)
    places = token_places(segments)
    rows_one = line_gather(normed_one, "tensor")
    rows_one, out_weights.rows = lax.optimization_barrier((rows_one, out_weights.rows))
    out_weights.start(rows_one)
    kind = PairFfn if teams == 4 and ways % 2 == 0 else LineFfn
    ffn = kind(ffn_in, ffn_out, rows_one)
    proj = product(rows_one, w_in, NN)
    constants = (conv_rows, head_rows, onorm_row)
    carry = forward_start(heads)
    mixed = jnp.zeros((proj.shape[0], heads * DV), bf16)
    kept = []
    for part in range(PARTS):
        mixed, keep, carry = mixer_forward(part, mixed, places, proj, *constants, carry, heads)
        kept.append(keep)
        if part == 0:
            carry = after(carry, ffn.middle(carry[0]))
    w_ffn = ffn.finish(mixed)
    came = swap_parts(lambda i: lax.dynamic_slice_in_dim(mixed, i * own, own, 0), "tensor")
    out_t = out_weights.finish(came[1])
    grad_rows = ffn.gather(after(cotangent, rows_one), came[1])
    mixed = jnp.concatenate(ordered(came, "tensor"), 1)
    middle = inputs + product(mixed, out_t, NT)
    factor_two = norm_factor(middle)
    scaled_two = middle * factor_two
    normed_two = (scaled_two * gains[1]).astype(bf16)
    rows_two = ffn.gather(normed_two, None)
    grad_gate, grad_up, hidden, back, forth = ffn_both(rows_two, grad_rows, w_ffn)
    grad_normed_two, ffn_grads = ffn.scatter(
        back,
        lambda sent: ffn_weight_grads(
            after(rows_two, sent), grad_rows, grad_gate, grad_up, hidden, w_ffn.shape[0]
        ),
    )
    ffn_grads = ffn.sum_planes(ffn_grads)
    grad_middle_norm, grad_gain_two = norm_backward(
        grad_normed_two, scaled_two, factor_two, gains[1]
    )
    grad_middle = cotangent.astype(f32) + grad_middle_norm
    branch_grad = grad_middle.astype(bf16)
    grad_mixed = product(branch_grad, out_t, NN).astype(bf16)
    width = heads * DV
    out_grad = out_weights.start_sum(after(branch_grad, grad_mixed), mixed)
    grad_mixed = jnp.concatenate(
        swap_blocks(
            lambda i: lax.dynamic_slice_in_dim(grad_mixed, i * width, width, 1), "tensor"
        ),
        0,
    )
    grad_mixed = after(grad_mixed, out_grad)
    result, _ = ffn.scatter(after(forth, grad_mixed), lambda sent: None)
    result = middle + result
    carry = backward_start(heads)
    grad_proj = jnp.zeros(proj.shape, bf16)
    for part in reversed(range(PARTS)):
        grad_proj, carry = mixer_backward(
            part, grad_proj, places, proj, *constants, kept[part], grad_mixed, carry, heads
        )
        if part == PARTS - 1:
            ffn_sums = ffn.sums_middle(after(ffn_grads, carry))
            carry = after(carry, ffn_sums)
            came = ffn.send_sums(ffn_sums)
    grad_proj, came, result = lax.optimization_barrier((grad_proj, came, result))
    grad_conv, grad_head, grad_onorm = carry[2:]
    summed = MixerSums(
        product(rows_one, grad_proj, TN),
        grad_conv.reshape(TAPS, heads, CONV),
        grad_onorm.reshape(heads, DV),
        heads,
    )
    sent = product(after(grad_proj, summed.sent), w_in, NT).astype(bf16)
    grad_normed_one = line_scatter(sent, "tensor")
    grad_gain_one = jnp.sum(sent.astype(f32) * rows_one.astype(f32), 0) / gains[0]
    out_in, out_small, out_conv, out_onorm = summed.outputs()
    ffn_grads = ffn.own_grads(ffn_sums, came)
    out_out = out_weights.finish_sum(width, sent)
    head_full = lax.dynamic_update_slice_in_dim(
        jnp.zeros((2, all_heads), f32),
        grad_head[:2, BETA_AT + heads : BETA_AT + 2 * heads],
        head_start,
        1,
    )
    totals = sum_everywhere(
        jnp.concatenate([grad_gain_one, grad_gain_two, head_full.reshape(-1)]), ("dp", "tensor")
    )
    d = gains.shape[1]
    grad_scaled = grad_normed_one * gains[0]
    grad_tokens = grad_middle + factor_one * (
        grad_scaled - scaled_one * jnp.mean(grad_scaled * scaled_one, -1, keepdims=True)
    )
    return (
        result.astype(bf16),
        grad_tokens,
        totals[: 2 * d].reshape(2, d),
        out_in,
        out_small,
        out_conv,
        totals[2 * d :].reshape(2, all_heads),
        out_onorm,
        out_out.T,
        ffn_grads[:2].swapaxes(1, 2),
        ffn_grads[2],
    )


def solution(mesh):
    in_specs = (
        P(("dp", "tensor"), None),
        P(("dp", "tensor"), None),
        P("dp", None),
        P(),
        P("dp", "tensor"),
        P(None, "dp", "tensor"),
        P(None, "tensor", "dp"),
        P(),
        P("tensor", "dp"),
        P("tensor", "dp"),
        P(None, "dp", "tensor"),
        P("tensor", "dp"),
    )
    out_specs = (
        P(("dp", "tensor"), None),
        P(("dp", "tensor"), None),
        P(),
        P("dp", "tensor"),
        P(None, "dp", "tensor"),
        P(None, "tensor", "dp"),
        P(),
        P("tensor", "dp"),
        P("tensor", "dp"),
        P(None, "dp", "tensor"),
        P("tensor", "dp"),
    )
    return jax.shard_map(shards, mesh=mesh, in_specs=in_specs, out_specs=out_specs, check_vma=False)
```

```python
import functools
import jax
import jax.numpy as jnp
from jax import lax
from jax.experimental import pallas as pl
from jax.experimental.pallas import tpu as pltpu
from jax.sharding import PartitionSpec as P

DK = 128
DV = 256
MIX = 2 * DK + 2 * DV
CONV = 2 * DK + DV
CHUNK = 128
LANES = 128
TAPS = 4
BASE = 16
PER = 2
BACK = 2
PARTS = 2
BETA_AT = 8

NN = ((1,), (0,))
NT = ((1,), (1,))
TN = ((0,), (0,))

f32 = jnp.float32
bf16 = jnp.bfloat16


def dot(a, b, dims, passes):
    if passes == 6:
        return lax.dot_general(
            a, b, (dims, ((), ())), precision=lax.Precision.HIGHEST, preferred_element_type=f32
        )
    a_hi = a.astype(bf16)
    b_hi = b.astype(bf16)
    out = lax.dot_general(a_hi, b_hi, (dims, ((), ())), preferred_element_type=f32)
    if passes == 3:
        a_lo = (a - a_hi.astype(f32)).astype(bf16)
        b_lo = (b - b_hi.astype(f32)).astype(bf16)
        out = out + lax.dot_general(a_hi, b_lo, (dims, ((), ())), preferred_element_type=f32)
        out = out + lax.dot_general(a_lo, b_hi, (dims, ((), ())), preferred_element_type=f32)
    return out


def exact_left(mask, b):
    hi = b.astype(bf16)
    rest = b - hi.astype(f32)
    mid = rest.astype(bf16)
    low = (rest - mid.astype(f32)).astype(bf16)
    out = lax.dot_general(mask, hi, (NN, ((), ())), preferred_element_type=f32)
    out = out + lax.dot_general(mask, mid, (NN, ((), ())), preferred_element_type=f32)
    return out + lax.dot_general(mask, low, (NN, ((), ())), preferred_element_type=f32)


def sigmoid(x):
    return 1.0 / (1.0 + jnp.exp(-x))


def log1p(y):
    return jnp.where(y < 1e-4, y - 0.5 * y * y, jnp.log(1.0 + y))


def softplus(x):
    return jnp.maximum(x, 0.0) + log1p(jnp.exp(-jnp.abs(x)))


def iotas():
    shape = (CHUNK, CHUNK)
    return lax.broadcasted_iota(jnp.int32, shape, 0), lax.broadcasted_iota(jnp.int32, shape, 1)


def token_scalars(info, head_rows, heads):
    row, col = iotas()
    beta = sigmoid(info)
    rate = -jnp.exp(head_rows[0:1])
    pre = info + head_rows[1:2]
    g = rate * softplus(pre)
    total = exact_left((row >= col).astype(bf16), g)
    lane = lax.broadcasted_iota(jnp.int32, (CHUNK, LANES), 1)
    across = jnp.where(lane < BETA_AT, info, total).T
    return beta, g, pre, total, across


def head_scalars(h, heads, info, beta, total, across):
    row, col = iotas()
    at = BETA_AT + heads + h
    seg_col = info[:, 0:1]
    seg_row = across[0:1, :]
    tot_col = total[:, at : at + 1]
    tot_row = across[at : at + 1, :]
    keep = (seg_col == seg_row) & (row >= col)
    decay = jnp.exp(jnp.where(keep, tot_col - tot_row, -1e30))
    strict = jnp.where(row > col, decay, 0.0)
    beta_col = beta[:, BETA_AT + h : BETA_AT + h + 1]
    carried = jnp.exp(tot_col) * info[:, 7:8]
    last = CHUNK - 1
    end = jnp.where(
        seg_col == seg_col[last : last + 1], jnp.exp(tot_col[last : last + 1] - tot_col), 0.0
    )
    carried_last = carried[last : last + 1]
    return decay, strict, beta_col, carried, end, carried_last


def invert(lowers, passes):
    row, col = iotas()
    shape = (BASE, CHUNK)
    lane = lax.broadcasted_iota(jnp.int32, shape, 1)
    own = lax.broadcasted_iota(jnp.int32, shape, 0)
    start = lane // BASE * BASE
    blocks = CHUNK // BASE
    inside = [lane // BASE == b for b in range(blocks)]
    packs = []
    for lower in lowers:
        packed = jnp.zeros(shape, f32)
        for b in range(blocks):
            packed = jnp.where(inside[b], lower[b * BASE : (b + 1) * BASE], packed)
        packs.append(packed)
    invs = [jnp.where(own == lane % BASE, 1.0, 0.0)] * len(lowers)
    for j in range(BASE - 1):
        at = start + j
        invs = [
            inv - jnp.take_along_axis(packed, at, axis=1) * inv[j : j + 1]
            for inv, packed in zip(invs, packs)
        ]
    invs = [
        jnp.concatenate([jnp.where(inside[b], inv, 0.0) for b in range(blocks)], 0) for inv in invs
    ]
    size = BASE
    while size < CHUNK:
        part = ((row // (2 * size)) == (col // (2 * size))) & ((row // size) != (col // size))
        steps = [
            dot(jnp.where(part, lower, 0.0), inv, NN, passes) for lower, inv in zip(lowers, invs)
        ]
        invs = [inv - dot(inv, step, NN, passes) for inv, step in zip(invs, steps)]
        size *= 2
    return invs


def normalised(act):
    factor = lax.rsqrt(jnp.sum(act * act, -1, keepdims=True) + 1e-06)
    return act * factor, factor


def with_scalars(places, extra, heads):
    lane = lax.broadcasted_iota(jnp.int32, places.shape, 1)
    return jnp.where((lane >= BETA_AT) & (lane < BETA_AT + 2 * heads), extra, places)


def forward_body(
    heads, prec, places_ref, extra_ref, proj_ref, conv_ref, head_ref, onorm_ref, state_in_ref,
    tail_in_ref,
    *refs,
):
    (
        z_ref, mixed_ref, out_ref, delta_ref, across_ref, state_out_ref, solve_ref, kk_ref, qk_ref,
        state_ref, tail_ref,
    ) = refs[-11:]

    @pl.when(pl.program_id(0) == 0)
    def _():
        state_ref[...] = state_in_ref[...]
        tail_ref[...] = tail_in_ref[...]

    rows = PER * CHUNK
    ready = {}
    first = {}
    infos = [
        with_scalars(
            places_ref[u * CHUNK : (u + 1) * CHUNK],
            extra_ref[u * CHUNK : (u + 1) * CHUNK],
            heads,
        )
        for u in range(PER)
    ]
    scalars = [token_scalars(info, head_ref[...], heads) for info in infos]
    for h in range(heads):
        at = h * MIX
        cat = h * CONV
        part = proj_ref[:, at : at + CONV]
        ext = jnp.concatenate([tail_ref[:, cat : cat + CONV], part], 0)
        tail_ref[:, cat : cat + CONV] = part[rows - 8 :]
        mixed = conv_ref[TAPS - 1 : TAPS, cat : cat + CONV] * part
        for s in range(1, TAPS):
            shifted = ext[8 - s : 8 - s + rows]
            mixed = mixed + conv_ref[TAPS - 1 - s : TAPS - s, cat : cat + CONV] * jnp.where(
                places_ref[:, s : s + 1] > 0.5, shifted, 0.0
            )
        mixed_ref[:, cat : cat + CONV] = mixed
        act = mixed * sigmoid(mixed)
        queries, _ = normalised(act[:, :DK])
        queries = queries * DK ** (-0.5)
        keys, _ = normalised(act[:, DK : 2 * DK])
        for u in range(PER):
            own = slice(u * CHUNK, (u + 1) * CHUNK)
            query = queries[own]
            key = keys[own]
            value = act[own, 2 * DK :]
            beta, g, pre, total, across = scalars[u]
            decay, strict, beta_col, carried, end, carried_last = head_scalars(
                h, heads, infos[u], beta, total, across
            )
            inner = dot(jnp.concatenate([key, query], 0), key, NT, prec["kk"])
            kk = inner[:CHUNK]
            qk = inner[CHUNK:]
            kk_ref[u, h] = kk
            qk_ref[u, h] = qk
            first[u, h] = (
                beta_col * strict * kk,
                jnp.concatenate([beta_col * value, (beta_col * carried) * key], 1),
                carried * query, decay * qk, end * key, carried_last,
            )
    order = list(first)
    for at, inv in zip(order, invert([first[at][0] for at in order], prec["inv"])):
        u, h = at
        own = slice(u * CHUNK, (u + 1) * CHUNK)
        lower, sides, reads_q, attend, ends, carried_last = first[at]
        solve_ref[u, h] = inv
        solved = dot(inv, sides, NN, prec["solve"])
        across_ref[own, h * DK : (h + 1) * DK] = solved[:, DV:]
        ready[at] = (
            jnp.concatenate([reads_q, solved[:, DV:]], 0), solved[:, :DV], attend, ends,
            carried_last,
        )
    for u in range(PER):
        own = slice(u * CHUNK, (u + 1) * CHUNK)
        for h in range(heads):
            readers, fixed, attend, ends, carried_last = ready[u, h]
            state = state_ref[h]
            state_out_ref[u, h] = state
            reads = dot(readers, state, NN, prec["state"])
            delta = fixed - reads[CHUNK:]
            state_ref[h] = carried_last * state + dot(ends, delta, TN, prec["state"])
            result = reads[:CHUNK] + dot(attend, delta, NN, prec["attend"])
            delta_ref[own, h * DV : (h + 1) * DV] = delta
            out_ref[own, h * DV : (h + 1) * DV] = result
            gate = proj_ref[own, h * MIX + CONV : (h + 1) * MIX]
            factor = lax.rsqrt(jnp.mean(result * result, -1, keepdims=True) + 1e-05)
            z = result * factor * onorm_ref[:, h * DV : (h + 1) * DV] * (gate * sigmoid(gate))
            z_ref[own, h * DV : (h + 1) * DV] = z.astype(bf16)


def backward_body(
    heads, prec, places_ref, extra_ref, proj_ref, conv_ref, head_ref, onorm_ref,
    mixed_ref, out_ref, delta_ref, across_ref, state_in_ref, solve_ref, kk_ref, qk_ref, dz_ref,
    dstate_in_ref, lead_in_ref, dconv_in_ref, dhead_in_ref, donorm_in_ref,
    *refs,
):
    dproj_ref, dstate_ref, lead_ref, dconv_ref, dhead_ref, donorm_ref = refs[-6:]

    @pl.when(pl.program_id(0) == 0)
    def _():
        dstate_ref[...] = dstate_in_ref[...]
        lead_ref[...] = lead_in_ref[...]
        dconv_ref[...] = dconv_in_ref[...]
        dhead_ref[...] = dhead_in_ref[...]
        donorm_ref[...] = donorm_in_ref[...]

    row, col = iotas()
    lane = lax.broadcasted_iota(jnp.int32, (CHUNK, LANES), 1)
    from_here = (row <= col).astype(bf16)
    items = [(u, h) for u in reversed(range(BACK)) for h in range(heads)]
    rows_of = {u: slice(u * CHUNK, (u + 1) * CHUNK) for u in range(BACK)}
    infos = {
        u: with_scalars(places_ref[rows_of[u]], extra_ref[rows_of[u]], heads)
        for u in range(BACK)
    }
    scalars = {u: token_scalars(infos[u], head_ref[...], heads) for u in range(BACK)}
    made = {}
    for u, h in items:
        own = rows_of[u]
        cat = h * CONV
        at = h * MIX
        mixed = mixed_ref[own, cat : cat + CONV]
        msig = sigmoid(mixed)
        act = mixed * msig
        q_unit, q_factor = normalised(act[:, :DK])
        key, k_factor = normalised(act[:, DK : 2 * DK])
        value = act[:, 2 * DK :]
        beta, g, pre, total, across = scalars[u]
        decay, strict, beta_col, carried, end, carried_last = head_scalars(
            h, heads, infos[u], beta, total, across
        )
        result = out_ref[own, h * DV : (h + 1) * DV]
        gate = proj_ref[own, at + CONV : at + MIX]
        gsig = sigmoid(gate)
        silu = gate * gsig
        onorm = onorm_ref[:, h * DV : (h + 1) * DV]
        factor = lax.rsqrt(jnp.mean(result * result, -1, keepdims=True) + 1e-05)
        normed = result * factor
        dz = dz_ref[own, h * DV : (h + 1) * DV].astype(f32)
        dzn = dz * normed
        donorm_ref[:, h * DV : (h + 1) * DV] += jnp.sum(dzn * silu, 0, keepdims=True)
        dgate = dzn * onorm * (gsig * (1.0 + gate * (1.0 - gsig)))
        dproj_ref[own, at + CONV : at + MIX] = dgate.astype(bf16)
        dnormed = dz * onorm * silu
        dout = factor * (dnormed - normed * jnp.mean(dnormed * normed, -1, keepdims=True))
        through = dot(decay * qk_ref[u, h], dout, TN, prec["attend"])
        made[u, h] = (
            mixed, msig, q_unit, q_factor, key, k_factor, value, decay, strict, beta_col, carried,
            end, carried_last, dout, through,
        )
    chain = {}
    for u, h in items:
        own = rows_of[u]
        q_unit, key, carried, end, carried_last, dout, through = (
            made[u, h][i] for i in (2, 4, 10, 11, 12, 13, 14)
        )
        dnext = dstate_ref[h]
        ddelta = through + dot(end * key, dnext, NN, prec["state"])
        dstate_ref[h] = carried_last * dnext + dot(
            jnp.concatenate(
                [carried * (q_unit * DK ** (-0.5)), -across_ref[own, h * DK : (h + 1) * DK]], 0
            ),
            jnp.concatenate([dout, ddelta], 0),
            TN,
            prec["state"],
        )
        chain[u, h] = (dnext, ddelta)
    solved = {}
    for u, h in items:
        own = rows_of[u]
        dnext, ddelta = chain[u, h]
        delta = delta_ref[own, h * DV : (h + 1) * DV]
        state = state_in_ref[u, h]
        x = dot(solve_ref[u, h], ddelta, TN, prec["solve"])
        dend = dot(delta, dnext, NT, prec["big"])
        dcl = jnp.sum(jnp.sum(state * dnext, 0, keepdims=True), 1, keepdims=True)
        big = dot(
            jnp.concatenate([made[u, h][13], x], 0),
            jnp.concatenate([state, delta], 0),
            NT,
            prec["big"],
        )
        solved[u, h] = (x, dend, dcl, big)
    inner = {}
    for u, h in items:
        q_unit, key, decay, strict, beta_col = (made[u, h][i] for i in (2, 4, 7, 8, 9))
        x, dend, dcl, big = solved[u, h]
        query = q_unit * DK ** (-0.5)
        dqk = decay * big[:CHUNK, DK:]
        das = -strict * big[CHUNK:, DK:]
        bdas = beta_col * das
        rows = dot(jnp.concatenate([dqk, das], 0), key, NN, prec["kk"])
        cols = dot(
            jnp.concatenate([dqk, bdas], 0),
            jnp.concatenate([query, key], 0),
            TN,
            prec["kk"],
        )
        pairs = jnp.where(row > col, dqk * qk_ref[u, h] + bdas * kk_ref[u, h], 0.0)
        inner[u, h] = (rows, cols, exact_left(from_here, pairs))
    sums = {
        u: [jnp.zeros((CHUNK, LANES), f32) for _ in range(4)] for u in range(BACK)
    }
    dacts = {}
    for u, h in items:
        (
            mixed, msig, q_unit, q_factor, key, k_factor, value, decay, strict, beta_col, carried,
            end, carried_last, dout, through,
        ) = made[u, h]
        x, dend, dcl, big = solved[u, h]
        rows, cols, pairs = inner[u, h]
        query = q_unit * DK ** (-0.5)
        dqc = carried * big[:CHUNK, :DK]
        dq = rows[:CHUNK] + dqc
        dk_end = end * dend
        dkb_c = -carried * big[CHUNK:, :DK]
        dk_row_b = rows[CHUNK:] + dkb_c
        dk = beta_col * dk_row_b + cols + dk_end
        xv = x * value
        dbeta = jnp.sum(xv[:, :DK] + xv[:, DK:] + key * dk_row_b, -1, keepdims=True)
        reach = jnp.sum(query * dqc + key * (beta_col * dkb_c), -1, keepdims=True)
        leave = jnp.sum(key * dk_end, -1, keepdims=True)
        spans = jnp.sum(jnp.where(row > col, pairs, 0.0), -1, keepdims=True) + carried_last * dcl
        at_h = lane == BETA_AT + heads + h
        sums[u][0] = jnp.where(lane == BETA_AT + h, dbeta, sums[u][0])
        sums[u][1] = jnp.where(at_h, reach, sums[u][1])
        sums[u][2] = jnp.where(at_h, leave, sums[u][2])
        sums[u][3] = jnp.where(at_h, spans, sums[u][3])
        scale_q = DK ** (-0.5) * q_factor
        daq = scale_q * (dq - q_unit * jnp.sum(q_unit * dq, -1, keepdims=True))
        dak = k_factor * (dk - key * jnp.sum(key * dk, -1, keepdims=True))
        dact = jnp.concatenate([daq, dak, beta_col * x], 1)
        dacts[u, h] = dact * (msig * (1.0 + mixed * (1.0 - msig)))
    for h in range(heads):
        at = h * MIX
        cat = h * CONV
        dmixed = jnp.concatenate([dacts[u, h] for u in range(BACK)], 0)
        ext = jnp.concatenate([dmixed, lead_ref[:, cat : cat + CONV]], 0)
        lead_ref[:, cat : cat + CONV] = dmixed[:8]
        part = proj_ref[:, at : at + CONV]
        dpart = conv_ref[TAPS - 1 : TAPS, cat : cat + CONV] * dmixed
        dconv_ref[TAPS - 1 : TAPS, cat : cat + CONV] += jnp.sum(dmixed * part, 0, keepdims=True)
        for s in range(1, TAPS):
            shifted = jnp.where(
                places_ref[:, 3 + s : 4 + s] > 0.5, ext[s : s + BACK * CHUNK], 0.0
            )
            dpart = dpart + conv_ref[TAPS - 1 - s : TAPS - s, cat : cat + CONV] * shifted
            dconv_ref[TAPS - 1 - s : TAPS - s, cat : cat + CONV] += jnp.sum(
                shifted * part, 0, keepdims=True
            )
        dproj_ref[:, at : at + CONV] = dpart.astype(bf16)
    rate = -jnp.exp(head_ref[0:1])
    for u in range(BACK):
        beta, g, pre, total, across = scalars[u]
        dbeta_all, reach_all, leave_all, spans_all = sums[u]
        dg = spans_all + exact_left(from_here, reach_all)
        dg = dg + exact_left((row > col).astype(bf16), leave_all)
        dpre = dg * rate * sigmoid(pre)
        dsmall = dbeta_all * beta * (1.0 - beta) + dpre
        dproj_ref[rows_of[u], heads * MIX :] = dsmall.astype(bf16)
        dhead_ref[0:1] += jnp.sum(dg * g, 0, keepdims=True)
        dhead_ref[1:2] += jnp.sum(dpre, 0, keepdims=True)


PREC = {"kk": 3, "inv": 3, "solve": 3, "state": 3, "attend": 3, "big": 3}
BUDGET = 56 << 20


def whole(shape):
    return pl.BlockSpec(shape, lambda c: (0,) * len(shape))


def forward_start(heads):
    return [jnp.zeros((heads, DK, DV), f32), jnp.zeros((8, heads * CONV), f32)]


def mixer_forward(part, before, places, proj, conv, head_rows, onorm, carry, heads, prec=PREC):
    length = proj.shape[0]
    count = length // CHUNK
    steps = count // PER // PARTS
    first = part * steps
    chunk = lambda width: pl.BlockSpec((PER * CHUNK, width), lambda c: (first + c, 0))
    lanes = pl.BlockSpec((PER * CHUNK, LANES), lambda c: (first + c, heads * MIX // LANES))
    square = lambda rows, width: pl.BlockSpec(
        (PER, heads, rows, width), lambda c: (first + c, 0, 0, 0)
    )
    outs = pl.pallas_call(
        functools.partial(forward_body, heads, prec),
        grid=(steps,),
        in_specs=[chunk(LANES), lanes, chunk(heads * MIX)]
        + [whole(x.shape) for x in (conv, head_rows, onorm, *carry)]
        + [pl.BlockSpec(memory_space=pl.ANY)] * len(before),
        out_specs=[
            chunk(heads * DV), chunk(heads * CONV), chunk(heads * DV), chunk(heads * DV),
            chunk(heads * DK), square(DK, DV), square(CHUNK, CHUNK), square(CHUNK, CHUNK),
            square(CHUNK, CHUNK),
        ]
        + [whole(x.shape) for x in carry],
        out_shape=[
            jax.ShapeDtypeStruct((length, heads * DV), bf16),
            jax.ShapeDtypeStruct((length, heads * CONV), f32),
            jax.ShapeDtypeStruct((length, heads * DV), f32),
            jax.ShapeDtypeStruct((length, heads * DV), f32),
            jax.ShapeDtypeStruct((length, heads * DK), f32),
            jax.ShapeDtypeStruct((count, heads, DK, DV), f32),
            jax.ShapeDtypeStruct((count, heads, CHUNK, CHUNK), f32),
            jax.ShapeDtypeStruct((count, heads, CHUNK, CHUNK), f32),
            jax.ShapeDtypeStruct((count, heads, CHUNK, CHUNK), f32),
        ]
        + [jax.ShapeDtypeStruct(x.shape, f32) for x in carry],
        compiler_params=pltpu.CompilerParams(
            dimension_semantics=("arbitrary",), vmem_limit_bytes=BUDGET
        ),
        cost_estimate=pl.CostEstimate(
            flops=length * heads * 32000000, bytes_accessed=length * heads * 6000, transcendentals=0
        ),
        input_output_aliases={6 + len(carry) + i: i for i in range(len(before))},
        name="mixer_forward",
    )(places, proj, proj, conv, head_rows, onorm, *carry, *before)
    return outs[:-2], outs[-2:]


def backward_start(heads):
    return [
        jnp.zeros((heads, DK, DV), f32), jnp.zeros((8, heads * CONV), f32),
        jnp.zeros((TAPS, heads * CONV), f32), jnp.zeros((8, LANES), f32),
        jnp.zeros((1, heads * DV), f32),
    ]


def mixer_backward(
    part, before, places, proj, conv, head_rows, onorm, kept, dz, carry, heads, prec=PREC
):
    length = proj.shape[0]
    steps = length // (BACK * CHUNK) // PARTS
    last = part * steps + steps - 1
    chunk = lambda width: pl.BlockSpec((BACK * CHUNK, width), lambda c: (last - c, 0))
    lanes = pl.BlockSpec((BACK * CHUNK, LANES), lambda c: (last - c, heads * MIX // LANES))
    square = lambda rows, width: pl.BlockSpec(
        (BACK, heads, rows, width), lambda c: (last - c, 0, 0, 0)
    )
    dproj, *carry = pl.pallas_call(
        functools.partial(backward_body, heads, prec),
        grid=(steps,),
        in_specs=[chunk(LANES), lanes, chunk(heads * MIX)]
        + [whole(x.shape) for x in (conv, head_rows, onorm)]
        + [
            chunk(heads * CONV), chunk(heads * DV), chunk(heads * DV),
            chunk(heads * DK), square(DK, DV), square(CHUNK, CHUNK), square(CHUNK, CHUNK),
            square(CHUNK, CHUNK), chunk(heads * DV),
        ]
        + [whole(x.shape) for x in carry]
        + [pl.BlockSpec(memory_space=pl.ANY)] * len(before),
        out_specs=[chunk(heads * MIX + LANES)] + [whole(x.shape) for x in carry],
        out_shape=[jax.ShapeDtypeStruct((length, heads * MIX + LANES), bf16)]
        + [jax.ShapeDtypeStruct(x.shape, f32) for x in carry],
        compiler_params=pltpu.CompilerParams(
            dimension_semantics=("arbitrary",), vmem_limit_bytes=BUDGET
        ),
        cost_estimate=pl.CostEstimate(
            flops=length * heads * 48000000, bytes_accessed=length * heads * 7000, transcendentals=0
        ),
        input_output_aliases={7 + len(kept) + len(carry): 0} if before else {},
        name="mixer_backward",
    )(places, proj, proj, conv, head_rows, onorm, *kept, dz, *carry, *before)
    return dproj, carry


def token_places(segments):
    length = segments.shape[-1]
    seg = segments.reshape(length)
    columns = [seg.astype(f32)]
    for s in range(1, TAPS):
        before = jnp.concatenate([jnp.full((s,), -1, seg.dtype), seg[:-s]])
        columns.append((before == seg).astype(f32))
    for s in range(1, TAPS):
        beyond = jnp.concatenate([seg[s:], jnp.full((s,), -1, seg.dtype)])
        columns.append((beyond == seg).astype(f32))
    ends = seg.reshape(-1, CHUNK)[:, -1]
    ends = jnp.concatenate([jnp.full((1,), -1, seg.dtype), ends[:-1]])
    columns.append((jnp.repeat(ends, CHUNK) == seg).astype(f32))
    return jnp.pad(jnp.stack(columns, 1), ((0, 0), (0, LANES - len(columns))))


def head_lanes(head):
    heads = head.shape[1]
    return jnp.pad(head, ((0, 6), (BETA_AT + heads, LANES - BETA_AT - 2 * heads)))


def ffn_body(where, place_ref, rows_ref, cot_ref, *refs):
    w_refs = refs[:-5]
    gate_ref, up_ref, hidden_ref, back_ref, out_ref = refs[-5:]
    pieces = len(where[0])
    size = rows_ref.shape[1] // pieces

    def weight(p, which):
        parts = [w_refs[run[p][0]][run[p][1], which] for run in where]
        return parts[0] if len(parts) == 1 else jnp.concatenate(parts, 1)

    def columns(p):
        return pl.ds(pl.multiple_of((p ^ place_ref[0]) * size, size), size)

    def project(left_ref, which):
        total = None
        for p in range(pieces):
            part = lax.dot_general(
                left_ref[:, columns(p)], weight(p, which), (NT, ((), ())),
                preferred_element_type=f32,
            )
            total = part if total is None else total + part
        return total

    gate = project(rows_ref, 0)
    up = project(rows_ref, 1)
    grad_hidden = project(cot_ref, 2)
    sigma = sigmoid(gate)
    activ = gate * sigma
    hidden = (activ * up).astype(bf16)
    grad_gate = (grad_hidden * up * sigma * (1.0 + gate * (1.0 - sigma))).astype(bf16)
    grad_up = (grad_hidden * activ).astype(bf16)
    hidden_ref[...] = hidden
    gate_ref[...] = grad_gate
    up_ref[...] = grad_up
    for p in range(pieces):
        own = columns(p)
        back = lax.dot_general(
            grad_gate, weight(p, 0), (NN, ((), ())), preferred_element_type=f32
        )
        back = back + lax.dot_general(
            grad_up, weight(p, 1), (NN, ((), ())), preferred_element_type=f32
        )
        back_ref[:, own] = back.astype(bf16)
        out_ref[:, own] = lax.dot_general(
            hidden, weight(p, 2), (NN, ((), ())), preferred_element_type=f32
        ).astype(bf16)


FFN_TILE = 256


def ffn_both(place, rows, cot, weights, where):
    count, d = rows.shape
    hidden = weights[0].shape[2]
    tile = lambda width: pl.BlockSpec((FFN_TILE, width), lambda c, place: (c, 0))
    full = pl.BlockSpec(weights[0].shape, lambda c, place: (0, 0, 0, 0))
    return pl.pallas_call(
        functools.partial(ffn_body, where),
        grid_spec=pltpu.PrefetchScalarGridSpec(
            num_scalar_prefetch=1,
            grid=(count // FFN_TILE,),
            in_specs=[tile(d), tile(d)] + [full] * len(weights),
            out_specs=[tile(hidden), tile(hidden), tile(hidden), tile(d), tile(d)],
        ),
        out_shape=[
            jax.ShapeDtypeStruct((count, width), bf16) for width in (hidden, hidden, hidden, d, d)
        ],
        compiler_params=pltpu.CompilerParams(
            dimension_semantics=("arbitrary",), vmem_limit_bytes=BUDGET
        ),
        cost_estimate=pl.CostEstimate(
            flops=24 * count * d * hidden, bytes_accessed=8 * count * d, transcendentals=0
        ),
        name="ffn_both",
    )(place.reshape(1), rows, cot, *weights)


def ffn_grads_body(place_ref, rows_ref, cot_ref, gate_ref, up_ref, hidden_ref, *refs):
    out_refs = refs[:-1]
    flipped_ref = refs[-1]

    @pl.when(pl.program_id(0) == 0)
    def _():
        for i, ref in enumerate((gate_ref, up_ref, hidden_ref)):
            flipped_ref[i] = ref[...].T

    lanes = rows_ref.shape[1] // len(out_refs)
    for i, right in enumerate((rows_ref, rows_ref, cot_ref)):
        grad = lax.dot_general(
            flipped_ref[i], right[...], (NN, ((), ())), preferred_element_type=f32
        ).astype(bf16)
        for j, out_ref in enumerate(out_refs):
            out_ref[0, i] = grad[:, j * lanes : (j + 1) * lanes]


def ffn_weight_grads(place, rows, cot, gate, up, hidden, pieces, split):
    count, d = rows.shape
    width = hidden.shape[1]
    size = d // pieces
    column = pl.BlockSpec((count, size), lambda p, place: (0, p ^ place[0]))
    full = pl.BlockSpec((count, width), lambda p, place: (0, 0))
    return pl.pallas_call(
        ffn_grads_body,
        grid_spec=pltpu.PrefetchScalarGridSpec(
            num_scalar_prefetch=1,
            grid=(pieces,),
            in_specs=[column, column, full, full, full],
            out_specs=[
                pl.BlockSpec((1, 3, width, size // split), lambda p, place: (p, 0, 0, 0))
            ] * split,
            scratch_shapes=[pltpu.VMEM((3, width, count), bf16)],
        ),
        out_shape=[jax.ShapeDtypeStruct((pieces, 3, width, size // split), bf16)] * split,
        compiler_params=pltpu.CompilerParams(
            dimension_semantics=("arbitrary",), vmem_limit_bytes=BUDGET
        ),
        cost_estimate=pl.CostEstimate(
            flops=12 * count * d * width, bytes_accessed=8 * count * d, transcendentals=0
        ),
        name="ffn_weight_grads",
    )(place.reshape(1), rows, cot, gate, up, hidden)


def norm_factor(values):
    return lax.rsqrt(jnp.mean(values * values, -1, keepdims=True) + 1e-06)


def norm_backward(grad_out, scaled, factor, gain):
    grad_scaled = grad_out * gain
    grad_input = factor * (grad_scaled - scaled * jnp.mean(grad_scaled * scaled, -1, keepdims=True))
    return (grad_input, jnp.sum(grad_out * scaled, 0))


def product(left, right, dims):
    return lax.dot_general(left, right, (dims, ((), ())), preferred_element_type=f32)


def after(x, done):
    return lax.optimization_barrier((x, done))[0]


def exchange(x, axis, bit):
    return lax.ppermute(x, axis, [(i, i ^ bit) for i in range(lax.axis_size(axis))])


def sum_over(x, axis):
    ways = lax.axis_size(axis)
    if ways & (ways - 1):
        return lax.psum(x, axis)
    bit = 1
    while bit < ways:
        x = x + exchange(x, axis, bit)
        bit *= 2
    return x


def line_gather(x, axis, more=()):
    ways = lax.axis_size(axis)
    here = lax.axis_index(axis)
    up = [(i, i + 1) for i in range(ways - 1)]
    down = [(i + 1, i) for i in range(ways - 1)]
    below = [x]
    above = [x]
    for _ in range(ways - 1):
        below.append(lax.ppermute(below[-1], axis, up))
        above.append(lax.ppermute(above[-1], axis, down))
    below, above, more = lax.optimization_barrier((below, above, more))
    blocks = []
    for slot in range(ways):
        block = x
        for at in range(ways):
            if at != slot:
                block = jnp.where(here == at, below[at - slot] if at > slot else above[slot - at], block)
        blocks.append(block)
    return jnp.concatenate(blocks, 0), more


def line_scatter(x, axis, beside=None):
    ways = lax.axis_size(axis)
    here = lax.axis_index(axis)
    size = x.shape[0] // ways
    up = [(i, i + 1) for i in range(ways - 1)]
    down = [(i + 1, i) for i in range(ways - 1)]

    def block(slot):
        return lax.dynamic_slice_in_dim(x, slot * size, size, 0).astype(f32)

    low = None
    high = None
    other = None
    for k in range(1, ways):
        to_low = block(jnp.maximum(here - (ways - k), 0))
        to_high = block(jnp.minimum(here + (ways - k), ways - 1))
        if low is not None:
            to_low = to_low + low
            to_high = to_high + high
        low = lax.ppermute(to_low.astype(bf16), axis, down)
        high = lax.ppermute(to_high.astype(bf16), axis, up)
        if beside is not None:
            other = beside(k, other)
        low, high, other = lax.optimization_barrier((low, high, other))
        low = low.astype(f32)
        high = high.astype(f32)
    return block(here) + low + high, other


def shifted(x, axis, by):
    ways = lax.axis_size(axis)
    return lax.ppermute(x, axis, [(i, (i + by) % ways) for i in range(ways)])


def ordered(parts, axis):
    ways = len(parts)
    here = lax.axis_index(axis)
    blocks = []
    for slot in range(ways):
        block = parts[0]
        for at in range(ways):
            if at != slot:
                block = jnp.where(here == at, parts[(at - slot) % ways], block)
        blocks.append(block)
    return blocks


def swap_parts(block_to, axis):
    ways = lax.axis_size(axis)
    here = lax.axis_index(axis)
    parts = [block_to(here)]
    for s in range(1, ways):
        parts.append(shifted(block_to((here + s) % ways), axis, s))
    return parts


def swap_blocks(block_to, axis):
    return ordered(swap_parts(block_to, axis), axis)


class PlaneSum:

    def __init__(self, left, right):
        self.ways = lax.axis_size("dp")
        self.parts = ()
        if self.ways != 8:
            self.came = ()
            grad = product(left, right, TN).astype(bf16)
            self.total = lax.psum_scatter(grad, "dp", scatter_dimension=0, tiled=True).astype(f32)
            return
        core = lax.axis_index("dp") % 2
        self.size = left.shape[1] // self.ways
        blocks = [left[:, i * self.size : (i + 1) * self.size] for i in range(self.ways)]
        even = jnp.concatenate(blocks[::2], 1)
        odd = jnp.concatenate(blocks[1::2], 1)
        self.stay = jnp.where(core == 0, even, odd)
        self.right = right
        self.came = exchange(
            product(jnp.where(core == 0, odd, even), right, TN).astype(bf16), "dp", 1
        )

    def send(self):
        if self.ways == 8:
            total = product(self.stay, self.right, TN) + self.came.astype(f32)
            total = total.astype(bf16)
            place = lax.axis_index("dp") // 2
            block = lambda i: lax.dynamic_slice_in_dim(total, i * self.size, self.size, 0)
            self.total = block(place)
            self.parts = [exchange(block(place ^ (m // 2)), "dp", m) for m in (2, 4, 6)]

    def finish(self):
        total = self.total.astype(f32)
        for part in self.parts:
            total = total + part.astype(f32)
        return total


class OutWeights:

    def __init__(self, mixer_out):
        rows = mixer_out.T
        self.ways = lax.axis_size("dp")
        self.parts = ()
        self.rows = jnp.concatenate(swap_blocks(lambda i: rows, "tensor"), 1)

    def start(self, started):
        if self.ways == 8:
            rows = after(self.rows, started)
            self.parts = {m: exchange(rows, "dp", m) for m in (2, 4, 6)}

    def finish(self, done):
        if self.ways != 8:
            return lax.all_gather(self.rows, "dp", axis=0, tiled=True)
        here = lax.axis_index("dp")
        parts = dict(zip((2, 4, 6), after([self.parts[m] for m in (2, 4, 6)], done)))
        parts[0] = self.rows
        size = self.rows.shape[0]
        out = jnp.zeros((self.ways * size, self.rows.shape[1]), bf16)
        for m in (0, 2, 4, 6):
            parts[m + 1] = exchange(parts[m], "dp", 1)
        for m, part in parts.items():
            out = lax.dynamic_update_slice_in_dim(out, part, (here ^ m) * size, 0)
        return out

    def send_sum(self, total, width):
        return swap_parts(
            lambda i: lax.dynamic_slice_in_dim(total, i * width, width, 1), "tensor"
        )


class LineFfn:

    def __init__(self, ffn_in, ffn_out, started):
        self.own = jnp.stack([ffn_in[0].T, ffn_in[1].T, ffn_out])
        self.place = jnp.zeros((), jnp.int32)
        self.near = self.far = ()

    def middle(self, done, more):
        return done, more

    def plane_step(self):
        pass

    def finish(self, done):
        weights = lax.all_gather(self.own, "dp", axis=2, tiled=True)
        return (weights[None],)

    pieces = 1
    where = (((0, 0),),)

    def reach(self, x):
        return line_gather(x, "tensor")[0]

    def gather(self, x, far):
        return far

    def halves(self, x):
        return line_scatter(x, "tensor")[0], jnp.zeros((), bf16)

    def cross(self, far):
        return far

    def sum_start(self, grads):
        self.grads = grads

    def sum_step(self, done):
        return ()

    def sum_far(self, sent):
        pass

    def sum_finish(self):
        return lax.psum_scatter(self.grads[0][0], "dp", scatter_dimension=2, tiled=True)

    def send_sums(self, grads):
        return grads

    def own_grads(self, grads, came):
        return came.astype(f32)


TO_A = [(1, 0), (0, 2), (2, 3), (3, 1)]
TO_B = [(2, 1), (1, 2)]
BACK_A = [(0, 1), (2, 0), (3, 2), (1, 3)]
BACK_B = [(2, 1), (1, 2)]


class PairFfn:

    def __init__(self, ffn_in, ffn_out, started):
        self.core = lax.axis_index("dp") % 2
        self.here = lax.axis_index("tensor")
        self.place = lax.axis_index("dp") // 2
        self.own = after(jnp.stack([ffn_in[0].T, ffn_in[1].T, ffn_out]), started)
        self.a = lax.ppermute(self.own, "tensor", TO_A)
        self.b = lax.ppermute(self.own, "tensor", TO_B)

    def middle(self, done, more):
        here = self.here
        self.own, self.a, self.b, done, more = lax.optimization_barrier(
            (self.own, self.a, self.b, done, more)
        )
        own, a, b = self.own, self.a, self.b
        first = jnp.where(here == 0, own, jnp.where(here == 1, b, a))
        second = jnp.where(here == 3, own, jnp.where(here == 2, b, a))
        mine = jnp.where(self.core == 0, first, second)
        got = exchange(jnp.where(self.core == 0, second, first), "dp", 1)
        self.low = jnp.where(self.core == 0, mine, got)
        self.high = jnp.where(self.core == 0, got, mine)
        done = after(done, (self.low, self.high))
        self.near = exchange(self.low, "dp", 2), exchange(self.high, "dp", 4)
        return done, more

    def plane_step(self):
        self.low = jnp.stack([self.low, self.near[0]])
        self.high = jnp.stack([self.high, self.near[1]])
        self.far = exchange(self.low, "dp", 4), exchange(self.high, "dp", 2)

    def finish(self, done):
        far = after(self.far, done)
        return (self.low, far[0], self.high, far[1])

    pieces = 4
    where = (((0, 0), (0, 1), (1, 0), (1, 1)), ((2, 0), (3, 0), (2, 1), (3, 1)))

    def reach(self, x):
        return exchange(x, "tensor", 1)

    def gather(self, x, far):
        return jnp.concatenate([x, exchange(x, "dp", 1), far, exchange(far, "dp", 1)], 0)

    def halves(self, x):
        size = x.shape[0] // 4
        parts = [x[i * size : (i + 1) * size] for i in range(4)]
        far = (parts[2].astype(f32) + exchange(parts[3], "dp", 1).astype(f32)).astype(bf16)
        return parts[0].astype(f32) + exchange(parts[1], "dp", 1).astype(f32), far

    def cross(self, far):
        return exchange(far, "tensor", 1)

    def sum_start(self, grads):
        self.grads = grads
        low, high = grads
        across_x = jnp.stack([low[1], low[3]])
        self.near = exchange(across_x, "dp", 2), exchange(high[2:], "dp", 4)

    def sum_step(self, done):
        low, high = self.grads
        came = after(self.near, done)
        add = lambda x, y: (x.astype(f32) + y.astype(f32)).astype(bf16)
        self.kept = add(low[0], came[0][0]), add(high[0], came[1][0])
        return add(low[2], came[0][1]), add(high[1], came[1][1])

    def sum_far(self, sent):
        self.far = exchange(sent[0], "dp", 4), exchange(sent[1], "dp", 2)

    def sum_finish(self):
        came = self.far
        add = lambda x, y: (x.astype(f32) + y.astype(f32)).astype(bf16)
        low = add(self.kept[0], came[0])
        high = add(self.kept[1], came[1])
        core = self.core
        mine = jnp.where(core == 0, low, high)
        got = exchange(jnp.where(core == 0, high, low), "dp", 1)
        return jnp.where(core == 0, mine, got), jnp.where(core == 0, got, mine)

    def send_sums(self, sums):
        first, second = sums
        here = self.here
        a = lax.ppermute(jnp.where(here < 2, second, first), "tensor", BACK_A)
        b = lax.ppermute(jnp.where(here == 2, second, first), "tensor", BACK_B)
        return a, b

    def own_grads(self, sums, came):
        first, second = sums
        a, b = came
        here = self.here
        other = jnp.where(here == 0, first, jnp.where(here == 3, second, b))
        return a.astype(f32) + other.astype(f32)


CONV_AT = 64


def column_blocks(value, rows):
    ways, size = value.shape
    lanes = -(-size // rows)
    value = jnp.pad(value, ((0, 0), (0, lanes * rows - size)))
    return value.reshape(ways, lanes, rows).swapaxes(1, 2).reshape(ways * rows, lanes)


def from_columns(columns, shape, dim, rows):
    ways = columns.shape[0] // rows
    size = 1
    for extent in shape:
        size *= extent
    value = columns.reshape(ways, rows, -1).swapaxes(1, 2).reshape(ways, -1)[:, :size]
    value = jnp.moveaxis(value.reshape((ways,) + shape), 0, dim)
    return value.reshape(shape[:dim] + (ways * shape[dim],) + shape[dim + 1 :])


def lanes_of(small, conv, onorm):
    rows, width = small.shape
    used = BETA_AT + width
    rest = LANES - CONV_AT - conv.shape[1] - onorm.shape[1]
    zeros = lambda lanes: jnp.zeros((rows, lanes), small.dtype)
    return jnp.concatenate(
        [zeros(BETA_AT), small, zeros(CONV_AT - used), conv, onorm, zeros(rest)], 1
    )


def fetch_mixer(mixer_in, mixer_small, conv_weight, out_norm):
    rows, width = mixer_in.shape
    small = jnp.moveaxis(mixer_small, 0, 1).reshape(rows, -1)
    conv = column_blocks(conv_weight.reshape(1, -1), rows)
    onorm = column_blocks(out_norm.reshape(1, -1), rows)
    extended = jnp.concatenate([mixer_in, lanes_of(small, conv, onorm)], 1)
    w_in = lax.all_gather(extended, "dp", axis=0, tiled=True)
    at = width + CONV_AT
    w_conv = from_columns(w_in[:, at : at + conv.shape[1]], conv_weight.shape, 2, rows)
    at += conv.shape[1]
    w_onorm = from_columns(w_in[:, at : at + onorm.shape[1]], out_norm.shape, 1, rows)
    return w_in, w_conv, w_onorm


def shards(
    tokens, cotangent, segments, norm_gains, mixer_in, mixer_small, conv_weight, head_params,
    out_norm, mixer_out, ffn_in, ffn_out,
):
    heads = mixer_in.shape[1] // MIX
    all_heads = head_params.shape[1]
    ways = lax.axis_size("dp")
    teams = lax.axis_size("tensor")
    head_start = lax.axis_index("tensor") * heads
    head_local = lax.dynamic_slice_in_dim(head_params, head_start, heads, 1)
    gains = norm_gains.astype(f32)
    own = tokens.shape[0]
    inputs = tokens.astype(f32)
    factor_one = norm_factor(inputs)
    scaled_one = inputs * factor_one
    normed_one = (scaled_one * gains[0]).astype(bf16)
    out_weights = OutWeights(mixer_out)
    w_in, w_conv, w_onorm = fetch_mixer(mixer_in, mixer_small, conv_weight, out_norm)
    conv_rows = w_conv.astype(f32).reshape(TAPS, heads * CONV)
    onorm_row = w_onorm.astype(f32).reshape(1, heads * DV)
    head_rows = head_lanes(head_local)
    places = token_places(segments)
    rows_one, (out_weights.rows, constants, places) = line_gather(
        normed_one, "tensor", (out_weights.rows, (conv_rows, head_rows, onorm_row), places)
    )
    out_weights.start(rows_one)
    kind = PairFfn if teams == 4 and ways == 8 else LineFfn
    ffn = kind(ffn_in, ffn_out, rows_one)
    wide = heads * MIX
    proj = product(rows_one, w_in, NN)
    carry = forward_start(heads)
    made = []
    for part in range(PARTS):
        made, carry = mixer_forward(part, made, places, proj, *constants, carry, heads)
        if part == 0:
            carry, (cotangent, out_weights.parts) = ffn.middle(
                carry, (cotangent, out_weights.parts)
            )
            cot_far = ffn.reach(cotangent)
    mixed, *kept = made
    mixed, cot_far, ffn.near = lax.optimization_barrier((mixed, cot_far, ffn.near))
    ffn.plane_step()
    came = swap_parts(lambda i: lax.dynamic_slice_in_dim(mixed, i * own, own, 0), "tensor")
    out_t = out_weights.finish(came[-1])
    grad_rows = ffn.gather(cotangent, after(cot_far, came[-1]))
    mixed = jnp.concatenate(ordered(came, "tensor"), 1)
    middle = inputs + product(mixed, out_t, NT)
    factor_two = norm_factor(middle)
    scaled_two = middle * factor_two
    normed_two = (scaled_two * gains[1]).astype(bf16)
    rows_two = ffn.gather(normed_two, ffn.reach(normed_two))
    w_ffn = ffn.finish(normed_two)
    grad_gate, grad_up, hidden, back, forth = ffn_both(
        ffn.place, rows_two, grad_rows, w_ffn, ffn.where
    )
    grad_normed_two, far = ffn.halves(back)
    ffn_grads = ffn_weight_grads(
        ffn.place, after(rows_two, far), grad_rows, grad_gate, grad_up, hidden,
        ffn.pieces, len(ffn.where),
    )
    far, ffn_grads = lax.optimization_barrier((ffn.cross(far), ffn_grads))
    grad_normed_two = grad_normed_two + far.astype(f32)
    ffn.sum_start(ffn_grads)
    grad_middle_norm, grad_gain_two = norm_backward(
        grad_normed_two, scaled_two, factor_two, gains[1]
    )
    grad_middle = cotangent.astype(f32) + grad_middle_norm
    branch_grad = grad_middle.astype(bf16)
    grad_mixed = product(branch_grad, out_t, NN).astype(bf16)
    width = heads * DV
    came = swap_parts(
        lambda i: lax.dynamic_slice_in_dim(grad_mixed, i * width, width, 1), "tensor"
    )
    branch_grad, forth, near = after((branch_grad, forth, ffn.near), grad_mixed)
    ffn.near = near
    out_sum = PlaneSum(branch_grad, mixed)
    result, far = ffn.halves(forth)
    came, far, sums = lax.optimization_barrier((came, far, ffn.sum_step(grad_mixed)))
    ffn.sum_far(sums)
    result = result, ffn.cross(far)
    grad_mixed = jnp.concatenate(ordered(came, "tensor"), 0)
    carry = backward_start(heads)
    grad_proj = []
    for part in reversed(range(PARTS)):
        dproj, carry = mixer_backward(
            part, grad_proj, places, proj, *constants, kept, grad_mixed, carry, heads
        )
        grad_proj = [dproj]
        if part == PARTS - 1:
            carry, result, ffn.far, out_sum.came = lax.optimization_barrier(
                (carry, result, ffn.far, out_sum.came)
            )
            out_sum.send()
            ffn_sums = ffn.sum_finish()
            carry = after(carry, ffn_sums)
            ffn_came = ffn.send_sums(ffn_sums)
    grad_proj, ffn_came, out_sum.parts = lax.optimization_barrier(
        (dproj, ffn_came, out_sum.parts)
    )
    grad_conv, grad_head, grad_onorm = carry[2:]
    result = middle + result[0] + result[1].astype(f32)
    sent = product(grad_proj, w_in, NT).astype(bf16)
    grad_normed_one = lax.psum_scatter(
        sent, "tensor", scatter_dimension=0, tiled=True
    ).astype(f32)
    grad_proj = after(grad_proj, sent)
    grad_in = PlaneSum(rows_one, grad_proj[:, :wide])
    grad_in.send()
    head_full = lax.dynamic_update_slice_in_dim(
        jnp.zeros((2, all_heads), f32),
        grad_head[:2, BETA_AT + heads : BETA_AT + 2 * heads],
        head_start,
        1,
    )
    d = gains.shape[1]
    sizes = [2 * d + 2 * all_heads, grad_conv.size, grad_onorm.size, 2 * heads * d]
    ends = [sum(sizes[:i]) for i in range(5)]
    at = BETA_AT + 2 * heads
    grad_small = product(rows_one, grad_proj[:, wide:], TN)[:, BETA_AT:at]
    again = after(sent, grad_in.total)
    gain_one = jnp.sum(again.astype(f32) * rows_one.astype(f32), 0) / gains[0]
    parts = [
        gain_one, grad_gain_two, head_full.reshape(-1), grad_conv.reshape(-1),
        grad_onorm.reshape(-1), grad_small.T.reshape(-1),
    ]
    totals = sum_over(jnp.concatenate(parts), "dp")
    shared = totals[: sizes[0]]
    shared = sum(ordered(swap_parts(lambda i: shared, "tensor"), "tensor"))
    grad_in.parts, out_parts = lax.optimization_barrier(
        (grad_in.parts, out_sum.finish().astype(bf16))
    )
    out_out = sum(block.astype(f32) for block in out_weights.send_sum(out_parts, width))
    conv_total, onorm_total, small_total = (totals[ends[i] : ends[i + 1]] for i in (1, 2, 3))
    place = lax.axis_index("dp")

    def own_part(total, shape):
        size = shape[-1] // ways
        return lax.dynamic_slice_in_dim(total.reshape(shape), place * size, size, len(shape) - 1)

    out_conv = own_part(conv_total, (TAPS, heads, CONV))
    out_onorm = own_part(onorm_total, (heads, DV))
    out_small = own_part(small_total, (2, heads, d)).swapaxes(1, 2)
    totals = shared
    out_in = grad_in.finish()
    ffn_grads = ffn.own_grads(ffn_sums, ffn_came)
    grad_scaled = grad_normed_one * gains[0]
    grad_tokens = grad_middle + factor_one * (
        grad_scaled - scaled_one * jnp.mean(grad_scaled * scaled_one, -1, keepdims=True)
    )
    return (
        result.astype(bf16),
        grad_tokens,
        totals[: 2 * d].reshape(2, d),
        out_in,
        out_small,
        out_conv,
        totals[2 * d :].reshape(2, all_heads),
        out_onorm,
        out_out.T,
        ffn_grads[:2].swapaxes(1, 2),
        ffn_grads[2],
    )


def solution(mesh):
    in_specs = (
        P(("dp", "tensor"), None),
        P(("dp", "tensor"), None),
        P("dp", None),
        P(),
        P("dp", "tensor"),
        P(None, "dp", "tensor"),
        P(None, "tensor", "dp"),
        P(),
        P("tensor", "dp"),
        P("tensor", "dp"),
        P(None, "dp", "tensor"),
        P("tensor", "dp"),
    )
    out_specs = (
        P(("dp", "tensor"), None),
        P(("dp", "tensor"), None),
        P(),
        P("dp", "tensor"),
        P(None, "dp", "tensor"),
        P(None, "tensor", "dp"),
        P(),
        P("tensor", "dp"),
        P("tensor", "dp"),
        P(None, "dp", "tensor"),
        P("tensor", "dp"),
    )
    return jax.shard_map(shards, mesh=mesh, in_specs=in_specs, out_specs=out_specs, check_vma=False)
```

```python
import functools
import jax
import jax.numpy as jnp
from jax import lax
from jax.experimental import pallas as pl
from jax.experimental.pallas import tpu as pltpu
from jax.sharding import PartitionSpec as P

DK = 128
DV = 256
MIX = 2 * DK + 2 * DV
CONV = 2 * DK + DV
CHUNK = 128
LANES = 128
TAPS = 4
BASE = 16
PER = 2
BACK = 2
PARTS = 2
BETA_AT = 8

NN = ((1,), (0,))
NT = ((1,), (1,))
TN = ((0,), (0,))

f32 = jnp.float32
bf16 = jnp.bfloat16


def dot(a, b, dims, passes):
    if passes == 6:
        return lax.dot_general(
            a, b, (dims, ((), ())), precision=lax.Precision.HIGHEST, preferred_element_type=f32
        )
    a_hi = a.astype(bf16)
    b_hi = b.astype(bf16)
    out = lax.dot_general(a_hi, b_hi, (dims, ((), ())), preferred_element_type=f32)
    if passes == 3:
        a_lo = (a - a_hi.astype(f32)).astype(bf16)
        b_lo = (b - b_hi.astype(f32)).astype(bf16)
        out = out + lax.dot_general(a_hi, b_lo, (dims, ((), ())), preferred_element_type=f32)
        out = out + lax.dot_general(a_lo, b_hi, (dims, ((), ())), preferred_element_type=f32)
    return out


def exact_left(mask, b):
    hi = b.astype(bf16)
    rest = b - hi.astype(f32)
    mid = rest.astype(bf16)
    low = (rest - mid.astype(f32)).astype(bf16)
    out = lax.dot_general(mask, hi, (NN, ((), ())), preferred_element_type=f32)
    out = out + lax.dot_general(mask, mid, (NN, ((), ())), preferred_element_type=f32)
    return out + lax.dot_general(mask, low, (NN, ((), ())), preferred_element_type=f32)


def sigmoid(x):
    return 1.0 / (1.0 + jnp.exp(-x))


def log1p(y):
    return jnp.where(y < 1e-4, y - 0.5 * y * y, jnp.log(1.0 + y))


def softplus(x):
    return jnp.maximum(x, 0.0) + log1p(jnp.exp(-jnp.abs(x)))


def iotas():
    shape = (CHUNK, CHUNK)
    return lax.broadcasted_iota(jnp.int32, shape, 0), lax.broadcasted_iota(jnp.int32, shape, 1)


def token_scalars(info, head_rows, heads):
    row, col = iotas()
    beta = sigmoid(info)
    rate = -jnp.exp(head_rows[0:1])
    pre = info + head_rows[1:2]
    g = rate * softplus(pre)
    total = exact_left((row >= col).astype(bf16), g)
    lane = lax.broadcasted_iota(jnp.int32, (CHUNK, LANES), 1)
    across = jnp.where(lane < BETA_AT, info, total).T
    return beta, g, pre, total, across


def head_scalars(h, heads, info, beta, total, across):
    row, col = iotas()
    at = BETA_AT + heads + h
    seg_col = info[:, 0:1]
    seg_row = across[0:1, :]
    tot_col = total[:, at : at + 1]
    tot_row = across[at : at + 1, :]
    keep = (seg_col == seg_row) & (row >= col)
    decay = jnp.exp(jnp.where(keep, tot_col - tot_row, -1e30))
    strict = jnp.where(row > col, decay, 0.0)
    beta_col = beta[:, BETA_AT + h : BETA_AT + h + 1]
    carried = jnp.exp(tot_col) * info[:, 7:8]
    last = CHUNK - 1
    end = jnp.where(
        seg_col == seg_col[last : last + 1], jnp.exp(tot_col[last : last + 1] - tot_col), 0.0
    )
    carried_last = carried[last : last + 1]
    return decay, strict, beta_col, carried, end, carried_last


def invert(lowers, passes):
    row, col = iotas()
    shape = (BASE, CHUNK)
    lane = lax.broadcasted_iota(jnp.int32, shape, 1)
    own = lax.broadcasted_iota(jnp.int32, shape, 0)
    start = lane // BASE * BASE
    blocks = CHUNK // BASE
    inside = [lane // BASE == b for b in range(blocks)]
    packs = []
    for lower in lowers:
        packed = jnp.zeros(shape, f32)
        for b in range(blocks):
            packed = jnp.where(inside[b], lower[b * BASE : (b + 1) * BASE], packed)
        packs.append(packed)
    invs = [jnp.where(own == lane % BASE, 1.0, 0.0)] * len(lowers)
    for j in range(BASE - 1):
        at = start + j
        invs = [
            inv - jnp.take_along_axis(packed, at, axis=1) * inv[j : j + 1]
            for inv, packed in zip(invs, packs)
        ]
    invs = [
        jnp.concatenate([jnp.where(inside[b], inv, 0.0) for b in range(blocks)], 0) for inv in invs
    ]
    size = BASE
    while size < CHUNK:
        part = ((row // (2 * size)) == (col // (2 * size))) & ((row // size) != (col // size))
        steps = [
            dot(jnp.where(part, lower, 0.0), inv, NN, passes) for lower, inv in zip(lowers, invs)
        ]
        invs = [inv - dot(inv, step, NN, passes) for inv, step in zip(invs, steps)]
        size *= 2
    return invs


def normalised(act):
    factor = lax.rsqrt(jnp.sum(act * act, -1, keepdims=True) + 1e-06)
    return act * factor, factor


def with_scalars(places, extra, heads):
    lane = lax.broadcasted_iota(jnp.int32, places.shape, 1)
    return jnp.where((lane >= BETA_AT) & (lane < BETA_AT + 2 * heads), extra, places)


def forward_body(
    heads, prec, places_ref, extra_ref, proj_ref, conv_ref, head_ref, onorm_ref, state_in_ref,
    tail_in_ref,
    *refs,
):
    (
        z_ref, mixed_ref, out_ref, delta_ref, across_ref, state_out_ref, solve_ref, kk_ref, qk_ref,
        state_ref, tail_ref,
    ) = refs[-11:]

    @pl.when(pl.program_id(0) == 0)
    def _():
        state_ref[...] = state_in_ref[...]
        tail_ref[...] = tail_in_ref[...]

    rows = PER * CHUNK
    ready = {}
    first = {}
    infos = [
        with_scalars(
            places_ref[u * CHUNK : (u + 1) * CHUNK],
            extra_ref[u * CHUNK : (u + 1) * CHUNK],
            heads,
        )
        for u in range(PER)
    ]
    scalars = [token_scalars(info, head_ref[...], heads) for info in infos]
    for h in range(heads):
        at = h * MIX
        cat = h * CONV
        part = proj_ref[:, at : at + CONV]
        ext = jnp.concatenate([tail_ref[:, cat : cat + CONV], part], 0)
        tail_ref[:, cat : cat + CONV] = part[rows - 8 :]
        mixed = conv_ref[TAPS - 1 : TAPS, cat : cat + CONV] * part
        for s in range(1, TAPS):
            shifted = ext[8 - s : 8 - s + rows]
            mixed = mixed + conv_ref[TAPS - 1 - s : TAPS - s, cat : cat + CONV] * jnp.where(
                places_ref[:, s : s + 1] > 0.5, shifted, 0.0
            )
        mixed_ref[:, cat : cat + CONV] = mixed
        act = mixed * sigmoid(mixed)
        queries, _ = normalised(act[:, :DK])
        queries = queries * DK ** (-0.5)
        keys, _ = normalised(act[:, DK : 2 * DK])
        for u in range(PER):
            own = slice(u * CHUNK, (u + 1) * CHUNK)
            query = queries[own]
            key = keys[own]
            value = act[own, 2 * DK :]
            beta, g, pre, total, across = scalars[u]
            decay, strict, beta_col, carried, end, carried_last = head_scalars(
                h, heads, infos[u], beta, total, across
            )
            inner = dot(jnp.concatenate([key, query], 0), key, NT, prec["kk"])
            kk = inner[:CHUNK]
            qk = inner[CHUNK:]
            kk_ref[u, h] = kk
            qk_ref[u, h] = qk
            first[u, h] = (
                beta_col * strict * kk,
                jnp.concatenate([beta_col * value, (beta_col * carried) * key], 1),
                carried * query, decay * qk, end * key, carried_last,
            )
    order = list(first)
    for at, inv in zip(order, invert([first[at][0] for at in order], prec["inv"])):
        u, h = at
        own = slice(u * CHUNK, (u + 1) * CHUNK)
        lower, sides, reads_q, attend, ends, carried_last = first[at]
        solve_ref[u, h] = inv
        solved = dot(inv, sides, NN, prec["solve"])
        across_ref[own, h * DK : (h + 1) * DK] = solved[:, DV:]
        ready[at] = (
            jnp.concatenate([reads_q, solved[:, DV:]], 0), solved[:, :DV], attend, ends,
            carried_last,
        )
    for u in range(PER):
        own = slice(u * CHUNK, (u + 1) * CHUNK)
        for h in range(heads):
            readers, fixed, attend, ends, carried_last = ready[u, h]
            state = state_ref[h]
            state_out_ref[u, h] = state
            reads = dot(readers, state, NN, prec["state"])
            delta = fixed - reads[CHUNK:]
            state_ref[h] = carried_last * state + dot(ends, delta, TN, prec["state"])
            result = reads[:CHUNK] + dot(attend, delta, NN, prec["attend"])
            delta_ref[own, h * DV : (h + 1) * DV] = delta
            out_ref[own, h * DV : (h + 1) * DV] = result
            gate = proj_ref[own, h * MIX + CONV : (h + 1) * MIX]
            factor = lax.rsqrt(jnp.mean(result * result, -1, keepdims=True) + 1e-05)
            z = result * factor * onorm_ref[:, h * DV : (h + 1) * DV] * (gate * sigmoid(gate))
            z_ref[own, h * DV : (h + 1) * DV] = z.astype(bf16)


def backward_body(
    heads, prec, places_ref, extra_ref, proj_ref, conv_ref, head_ref, onorm_ref,
    mixed_ref, out_ref, delta_ref, across_ref, state_in_ref, solve_ref, kk_ref, qk_ref, dz_ref,
    dstate_in_ref, lead_in_ref, dconv_in_ref, dhead_in_ref, donorm_in_ref,
    *refs,
):
    dproj_ref, dstate_ref, lead_ref, dconv_ref, dhead_ref, donorm_ref = refs[-6:]

    @pl.when(pl.program_id(0) == 0)
    def _():
        dstate_ref[...] = dstate_in_ref[...]
        lead_ref[...] = lead_in_ref[...]
        dconv_ref[...] = dconv_in_ref[...]
        dhead_ref[...] = dhead_in_ref[...]
        donorm_ref[...] = donorm_in_ref[...]

    row, col = iotas()
    lane = lax.broadcasted_iota(jnp.int32, (CHUNK, LANES), 1)
    from_here = (row <= col).astype(bf16)
    items = [(u, h) for u in reversed(range(BACK)) for h in range(heads)]
    rows_of = {u: slice(u * CHUNK, (u + 1) * CHUNK) for u in range(BACK)}
    infos = {
        u: with_scalars(places_ref[rows_of[u]], extra_ref[rows_of[u]], heads)
        for u in range(BACK)
    }
    scalars = {u: token_scalars(infos[u], head_ref[...], heads) for u in range(BACK)}
    made = {}
    for u, h in items:
        own = rows_of[u]
        cat = h * CONV
        at = h * MIX
        mixed = mixed_ref[own, cat : cat + CONV]
        msig = sigmoid(mixed)
        act = mixed * msig
        q_unit, q_factor = normalised(act[:, :DK])
        key, k_factor = normalised(act[:, DK : 2 * DK])
        value = act[:, 2 * DK :]
        beta, g, pre, total, across = scalars[u]
        decay, strict, beta_col, carried, end, carried_last = head_scalars(
            h, heads, infos[u], beta, total, across
        )
        result = out_ref[own, h * DV : (h + 1) * DV]
        gate = proj_ref[own, at + CONV : at + MIX]
        gsig = sigmoid(gate)
        silu = gate * gsig
        onorm = onorm_ref[:, h * DV : (h + 1) * DV]
        factor = lax.rsqrt(jnp.mean(result * result, -1, keepdims=True) + 1e-05)
        normed = result * factor
        dz = dz_ref[own, h * DV : (h + 1) * DV].astype(f32)
        dzn = dz * normed
        donorm_ref[:, h * DV : (h + 1) * DV] += jnp.sum(dzn * silu, 0, keepdims=True)
        dgate = dzn * onorm * (gsig * (1.0 + gate * (1.0 - gsig)))
        dproj_ref[own, at + CONV : at + MIX] = dgate.astype(bf16)
        dnormed = dz * onorm * silu
        dout = factor * (dnormed - normed * jnp.mean(dnormed * normed, -1, keepdims=True))
        through = dot(decay * qk_ref[u, h], dout, TN, prec["attend"])
        made[u, h] = (
            mixed, msig, q_unit, q_factor, key, k_factor, value, decay, strict, beta_col, carried,
            end, carried_last, dout, through,
        )
    chain = {}
    for u, h in items:
        own = rows_of[u]
        q_unit, key, carried, end, carried_last, dout, through = (
            made[u, h][i] for i in (2, 4, 10, 11, 12, 13, 14)
        )
        dnext = dstate_ref[h]
        ddelta = through + dot(end * key, dnext, NN, prec["state"])
        dstate_ref[h] = carried_last * dnext + dot(
            jnp.concatenate(
                [carried * (q_unit * DK ** (-0.5)), -across_ref[own, h * DK : (h + 1) * DK]], 0
            ),
            jnp.concatenate([dout, ddelta], 0),
            TN,
            prec["state"],
        )
        chain[u, h] = (dnext, ddelta)
    solved = {}
    for u, h in items:
        own = rows_of[u]
        dnext, ddelta = chain[u, h]
        delta = delta_ref[own, h * DV : (h + 1) * DV]
        state = state_in_ref[u, h]
        x = dot(solve_ref[u, h], ddelta, TN, prec["solve"])
        dend = dot(delta, dnext, NT, prec["big"])
        dcl = jnp.sum(jnp.sum(state * dnext, 0, keepdims=True), 1, keepdims=True)
        big = dot(
            jnp.concatenate([made[u, h][13], x], 0),
            jnp.concatenate([state, delta], 0),
            NT,
            prec["big"],
        )
        solved[u, h] = (x, dend, dcl, big)
    inner = {}
    for u, h in items:
        q_unit, key, decay, strict, beta_col = (made[u, h][i] for i in (2, 4, 7, 8, 9))
        x, dend, dcl, big = solved[u, h]
        query = q_unit * DK ** (-0.5)
        dqk = decay * big[:CHUNK, DK:]
        das = -strict * big[CHUNK:, DK:]
        bdas = beta_col * das
        rows = dot(jnp.concatenate([dqk, das], 0), key, NN, prec["kk"])
        cols = dot(
            jnp.concatenate([dqk, bdas], 0),
            jnp.concatenate([query, key], 0),
            TN,
            prec["kk"],
        )
        pairs = jnp.where(row > col, dqk * qk_ref[u, h] + bdas * kk_ref[u, h], 0.0)
        inner[u, h] = (rows, cols, exact_left(from_here, pairs))
    sums = {
        u: [jnp.zeros((CHUNK, LANES), f32) for _ in range(4)] for u in range(BACK)
    }
    dacts = {}
    for u, h in items:
        (
            mixed, msig, q_unit, q_factor, key, k_factor, value, decay, strict, beta_col, carried,
            end, carried_last, dout, through,
        ) = made[u, h]
        x, dend, dcl, big = solved[u, h]
        rows, cols, pairs = inner[u, h]
        query = q_unit * DK ** (-0.5)
        dqc = carried * big[:CHUNK, :DK]
        dq = rows[:CHUNK] + dqc
        dk_end = end * dend
        dkb_c = -carried * big[CHUNK:, :DK]
        dk_row_b = rows[CHUNK:] + dkb_c
        dk = beta_col * dk_row_b + cols + dk_end
        xv = x * value
        dbeta = jnp.sum(xv[:, :DK] + xv[:, DK:] + key * dk_row_b, -1, keepdims=True)
        reach = jnp.sum(query * dqc + key * (beta_col * dkb_c), -1, keepdims=True)
        leave = jnp.sum(key * dk_end, -1, keepdims=True)
        spans = jnp.sum(jnp.where(row > col, pairs, 0.0), -1, keepdims=True) + carried_last * dcl
        at_h = lane == BETA_AT + heads + h
        sums[u][0] = jnp.where(lane == BETA_AT + h, dbeta, sums[u][0])
        sums[u][1] = jnp.where(at_h, reach, sums[u][1])
        sums[u][2] = jnp.where(at_h, leave, sums[u][2])
        sums[u][3] = jnp.where(at_h, spans, sums[u][3])
        scale_q = DK ** (-0.5) * q_factor
        daq = scale_q * (dq - q_unit * jnp.sum(q_unit * dq, -1, keepdims=True))
        dak = k_factor * (dk - key * jnp.sum(key * dk, -1, keepdims=True))
        dact = jnp.concatenate([daq, dak, beta_col * x], 1)
        dacts[u, h] = dact * (msig * (1.0 + mixed * (1.0 - msig)))
    for h in range(heads):
        at = h * MIX
        cat = h * CONV
        dmixed = jnp.concatenate([dacts[u, h] for u in range(BACK)], 0)
        ext = jnp.concatenate([dmixed, lead_ref[:, cat : cat + CONV]], 0)
        lead_ref[:, cat : cat + CONV] = dmixed[:8]
        part = proj_ref[:, at : at + CONV]
        dpart = conv_ref[TAPS - 1 : TAPS, cat : cat + CONV] * dmixed
        dconv_ref[TAPS - 1 : TAPS, cat : cat + CONV] += jnp.sum(dmixed * part, 0, keepdims=True)
        for s in range(1, TAPS):
            shifted = jnp.where(
                places_ref[:, 3 + s : 4 + s] > 0.5, ext[s : s + BACK * CHUNK], 0.0
            )
            dpart = dpart + conv_ref[TAPS - 1 - s : TAPS - s, cat : cat + CONV] * shifted
            dconv_ref[TAPS - 1 - s : TAPS - s, cat : cat + CONV] += jnp.sum(
                shifted * part, 0, keepdims=True
            )
        dproj_ref[:, at : at + CONV] = dpart.astype(bf16)
    rate = -jnp.exp(head_ref[0:1])
    for u in range(BACK):
        beta, g, pre, total, across = scalars[u]
        dbeta_all, reach_all, leave_all, spans_all = sums[u]
        dg = spans_all + exact_left(from_here, reach_all)
        dg = dg + exact_left((row > col).astype(bf16), leave_all)
        dpre = dg * rate * sigmoid(pre)
        dsmall = dbeta_all * beta * (1.0 - beta) + dpre
        dproj_ref[rows_of[u], heads * MIX :] = dsmall.astype(bf16)
        dhead_ref[0:1] += jnp.sum(dg * g, 0, keepdims=True)
        dhead_ref[1:2] += jnp.sum(dpre, 0, keepdims=True)


PREC = {"kk": 3, "inv": 3, "solve": 3, "state": 3, "attend": 3, "big": 3}
BUDGET = 56 << 20


def whole(shape):
    return pl.BlockSpec(shape, lambda c: (0,) * len(shape))


def forward_start(heads):
    return [jnp.zeros((heads, DK, DV), f32), jnp.zeros((8, heads * CONV), f32)]


def mixer_forward(part, before, places, proj, conv, head_rows, onorm, carry, heads, prec=PREC):
    length = proj.shape[0]
    count = length // CHUNK
    steps = count // PER // PARTS
    first = part * steps
    chunk = lambda width: pl.BlockSpec((PER * CHUNK, width), lambda c: (first + c, 0))
    lanes = pl.BlockSpec((PER * CHUNK, LANES), lambda c: (first + c, heads * MIX // LANES))
    square = lambda rows, width: pl.BlockSpec(
        (PER, heads, rows, width), lambda c: (first + c, 0, 0, 0)
    )
    outs = pl.pallas_call(
        functools.partial(forward_body, heads, prec),
        grid=(steps,),
        in_specs=[chunk(LANES), lanes, chunk(heads * MIX)]
        + [whole(x.shape) for x in (conv, head_rows, onorm, *carry)]
        + [pl.BlockSpec(memory_space=pl.ANY)] * len(before),
        out_specs=[
            chunk(heads * DV), chunk(heads * CONV), chunk(heads * DV), chunk(heads * DV),
            chunk(heads * DK), square(DK, DV), square(CHUNK, CHUNK), square(CHUNK, CHUNK),
            square(CHUNK, CHUNK),
        ]
        + [whole(x.shape) for x in carry],
        out_shape=[
            jax.ShapeDtypeStruct((length, heads * DV), bf16),
            jax.ShapeDtypeStruct((length, heads * CONV), f32),
            jax.ShapeDtypeStruct((length, heads * DV), f32),
            jax.ShapeDtypeStruct((length, heads * DV), f32),
            jax.ShapeDtypeStruct((length, heads * DK), f32),
            jax.ShapeDtypeStruct((count, heads, DK, DV), f32),
            jax.ShapeDtypeStruct((count, heads, CHUNK, CHUNK), f32),
            jax.ShapeDtypeStruct((count, heads, CHUNK, CHUNK), f32),
            jax.ShapeDtypeStruct((count, heads, CHUNK, CHUNK), f32),
        ]
        + [jax.ShapeDtypeStruct(x.shape, f32) for x in carry],
        compiler_params=pltpu.CompilerParams(
            dimension_semantics=("arbitrary",), vmem_limit_bytes=BUDGET
        ),
        cost_estimate=pl.CostEstimate(
            flops=length * heads * 32000000, bytes_accessed=length * heads * 6000, transcendentals=0
        ),
        input_output_aliases={6 + len(carry) + i: i for i in range(len(before))},
        name="mixer_forward",
    )(places, proj, proj, conv, head_rows, onorm, *carry, *before)
    return outs[:-2], outs[-2:]


def backward_start(heads):
    return [
        jnp.zeros((heads, DK, DV), f32), jnp.zeros((8, heads * CONV), f32),
        jnp.zeros((TAPS, heads * CONV), f32), jnp.zeros((8, LANES), f32),
        jnp.zeros((1, heads * DV), f32),
    ]


def mixer_backward(
    part, before, places, proj, conv, head_rows, onorm, kept, dz, carry, heads, prec=PREC
):
    length = proj.shape[0]
    steps = length // (BACK * CHUNK) // PARTS
    last = part * steps + steps - 1
    chunk = lambda width: pl.BlockSpec((BACK * CHUNK, width), lambda c: (last - c, 0))
    lanes = pl.BlockSpec((BACK * CHUNK, LANES), lambda c: (last - c, heads * MIX // LANES))
    square = lambda rows, width: pl.BlockSpec(
        (BACK, heads, rows, width), lambda c: (last - c, 0, 0, 0)
    )
    dproj, *carry = pl.pallas_call(
        functools.partial(backward_body, heads, prec),
        grid=(steps,),
        in_specs=[chunk(LANES), lanes, chunk(heads * MIX)]
        + [whole(x.shape) for x in (conv, head_rows, onorm)]
        + [
            chunk(heads * CONV), chunk(heads * DV), chunk(heads * DV),
            chunk(heads * DK), square(DK, DV), square(CHUNK, CHUNK), square(CHUNK, CHUNK),
            square(CHUNK, CHUNK), chunk(heads * DV),
        ]
        + [whole(x.shape) for x in carry]
        + [pl.BlockSpec(memory_space=pl.ANY)] * len(before),
        out_specs=[chunk(heads * MIX + LANES)] + [whole(x.shape) for x in carry],
        out_shape=[jax.ShapeDtypeStruct((length, heads * MIX + LANES), bf16)]
        + [jax.ShapeDtypeStruct(x.shape, f32) for x in carry],
        compiler_params=pltpu.CompilerParams(
            dimension_semantics=("arbitrary",), vmem_limit_bytes=BUDGET
        ),
        cost_estimate=pl.CostEstimate(
            flops=length * heads * 48000000, bytes_accessed=length * heads * 7000, transcendentals=0
        ),
        input_output_aliases={7 + len(kept) + len(carry): 0} if before else {},
        name="mixer_backward",
    )(places, proj, proj, conv, head_rows, onorm, *kept, dz, *carry, *before)
    return dproj, carry


def token_places(segments):
    length = segments.shape[-1]
    seg = segments.reshape(length)
    columns = [seg.astype(f32)]
    for s in range(1, TAPS):
        before = jnp.concatenate([jnp.full((s,), -1, seg.dtype), seg[:-s]])
        columns.append((before == seg).astype(f32))
    for s in range(1, TAPS):
        beyond = jnp.concatenate([seg[s:], jnp.full((s,), -1, seg.dtype)])
        columns.append((beyond == seg).astype(f32))
    ends = seg.reshape(-1, CHUNK)[:, -1]
    ends = jnp.concatenate([jnp.full((1,), -1, seg.dtype), ends[:-1]])
    columns.append((jnp.repeat(ends, CHUNK) == seg).astype(f32))
    return jnp.pad(jnp.stack(columns, 1), ((0, 0), (0, LANES - len(columns))))


def head_lanes(head):
    heads = head.shape[1]
    return jnp.pad(head, ((0, 6), (BETA_AT + heads, LANES - BETA_AT - 2 * heads)))


def ffn_body(where, runs, place_ref, *refs):
    step = pl.program_id(0)
    each = pl.num_programs(0) // runs
    rows_refs = refs[:runs]
    cot_refs = refs[runs : 2 * runs]
    outs = refs[len(refs) - 2 * runs - 5 :]
    w_refs = refs[2 * runs : len(refs) - 2 * runs - 5]
    gate_ref, up_ref, hidden_ref = outs[:3]
    back_refs = outs[3 : 3 + runs]
    out_refs = outs[3 + runs : 3 + 2 * runs]
    rows_ref, cot_ref = outs[3 + 2 * runs :]
    for i in range(runs):

        @pl.when(step // each == i)
        def _():
            rows_ref[...] = rows_refs[i][...]
            cot_ref[...] = cot_refs[i][...]

    pieces = len(where[0])
    size = rows_ref.shape[1] // pieces

    def weight(p, which):
        parts = [w_refs[run[p][0]][run[p][1], which] for run in where]
        return parts[0] if len(parts) == 1 else jnp.concatenate(parts, 1)

    def columns(p):
        return pl.ds(pl.multiple_of((p ^ place_ref[0]) * size, size), size)

    def project(left_ref, which):
        total = None
        for p in range(pieces):
            part = lax.dot_general(
                left_ref[:, columns(p)], weight(p, which), (NT, ((), ())),
                preferred_element_type=f32,
            )
            total = part if total is None else total + part
        return total

    gate = project(rows_ref, 0)
    up = project(rows_ref, 1)
    grad_hidden = project(cot_ref, 2)
    sigma = sigmoid(gate)
    activ = gate * sigma
    hidden = (activ * up).astype(bf16)
    grad_gate = (grad_hidden * up * sigma * (1.0 + gate * (1.0 - sigma))).astype(bf16)
    grad_up = (grad_hidden * activ).astype(bf16)
    hidden_ref[...] = hidden
    gate_ref[...] = grad_gate
    up_ref[...] = grad_up
    for p in range(pieces):
        own = columns(p)
        back = lax.dot_general(
            grad_gate, weight(p, 0), (NN, ((), ())), preferred_element_type=f32
        )
        back = back + lax.dot_general(
            grad_up, weight(p, 1), (NN, ((), ())), preferred_element_type=f32
        )
        rows_ref[:, own] = back.astype(bf16)
        cot_ref[:, own] = lax.dot_general(
            hidden, weight(p, 2), (NN, ((), ())), preferred_element_type=f32
        ).astype(bf16)
    for i in range(runs):

        @pl.when(step // each == i)
        def _():
            back_refs[i][...] = rows_ref[...]
            out_refs[i][...] = cot_ref[...]


FFN_TILE = 256


def ffn_both(place, rows, cot, weights, where):
    runs = len(rows)
    count, d = rows[0].shape
    each = count // FFN_TILE
    total = runs * count
    hidden = weights[0].shape[2]

    def run_tile(i):
        return pl.BlockSpec(
            (FFN_TILE, d), lambda c, place: (jnp.clip(c - i * each, 0, each - 1), 0)
        )

    tiles = [run_tile(i) for i in range(runs)]
    wide = pl.BlockSpec((FFN_TILE, hidden), lambda c, place: (c, 0))
    full = pl.BlockSpec(weights[0].shape, lambda c, place: (0, 0, 0, 0))
    gate, up, hidden_out, *out = pl.pallas_call(
        functools.partial(ffn_body, where, runs),
        grid_spec=pltpu.PrefetchScalarGridSpec(
            num_scalar_prefetch=1,
            grid=(runs * each,),
            in_specs=tiles + tiles + [full] * len(weights),
            out_specs=[wide] * 3 + tiles + tiles,
            scratch_shapes=[pltpu.VMEM((FFN_TILE, d), bf16)] * 2,
        ),
        out_shape=[jax.ShapeDtypeStruct((total, hidden), bf16)] * 3
        + [jax.ShapeDtypeStruct((count, d), bf16)] * (2 * runs),
        compiler_params=pltpu.CompilerParams(
            dimension_semantics=("arbitrary",), vmem_limit_bytes=BUDGET
        ),
        cost_estimate=pl.CostEstimate(
            flops=24 * total * d * hidden, bytes_accessed=8 * total * d, transcendentals=0
        ),
        name="ffn_both",
    )(place.reshape(1), *rows, *cot, *weights)
    return gate, up, hidden_out, out[:runs], out[runs:]


def ffn_grads_body(runs, place_ref, *refs):
    rows_refs = refs[:runs]
    cot_refs = refs[runs : 2 * runs]
    gate_ref, up_ref, hidden_ref = refs[2 * runs : 2 * runs + 3]
    out_refs = refs[2 * runs + 3 : -1]
    flipped_ref = refs[-1]

    @pl.when(pl.program_id(0) == 0)
    def _():
        for i, ref in enumerate((gate_ref, up_ref, hidden_ref)):
            flipped_ref[i] = ref[...].T

    rows = jnp.concatenate([ref[...] for ref in rows_refs], 0)
    cot = jnp.concatenate([ref[...] for ref in cot_refs], 0)
    lanes = rows.shape[1] // len(out_refs)
    for i, right in enumerate((rows, rows, cot)):
        grad = lax.dot_general(
            flipped_ref[i], right, (NN, ((), ())), preferred_element_type=f32
        ).astype(bf16)
        for j, out_ref in enumerate(out_refs):
            out_ref[0, i] = grad[:, j * lanes : (j + 1) * lanes]


def ffn_weight_grads(place, rows, cot, gate, up, hidden, pieces, split):
    runs = len(rows)
    count, d = rows[0].shape
    total = runs * count
    width = hidden.shape[1]
    size = d // pieces
    column = pl.BlockSpec((count, size), lambda p, place: (0, p ^ place[0]))
    full = pl.BlockSpec((total, width), lambda p, place: (0, 0))
    return pl.pallas_call(
        functools.partial(ffn_grads_body, runs),
        grid_spec=pltpu.PrefetchScalarGridSpec(
            num_scalar_prefetch=1,
            grid=(pieces,),
            in_specs=[column] * (2 * runs) + [full] * 3,
            out_specs=[
                pl.BlockSpec((1, 3, width, size // split), lambda p, place: (p, 0, 0, 0))
            ] * split,
            scratch_shapes=[pltpu.VMEM((3, width, total), bf16)],
        ),
        out_shape=[jax.ShapeDtypeStruct((pieces, 3, width, size // split), bf16)] * split,
        compiler_params=pltpu.CompilerParams(
            dimension_semantics=("arbitrary",), vmem_limit_bytes=BUDGET
        ),
        cost_estimate=pl.CostEstimate(
            flops=12 * total * d * width, bytes_accessed=8 * total * d, transcendentals=0
        ),
        name="ffn_weight_grads",
    )(place.reshape(1), *rows, *cot, gate, up, hidden)


def norm_factor(values):
    return lax.rsqrt(jnp.mean(values * values, -1, keepdims=True) + 1e-06)


def norm_backward(grad_out, scaled, factor, gain):
    grad_scaled = grad_out * gain
    grad_input = factor * (grad_scaled - scaled * jnp.mean(grad_scaled * scaled, -1, keepdims=True))
    return (grad_input, jnp.sum(grad_out * scaled, 0))


def product(left, right, dims):
    return lax.dot_general(left, right, (dims, ((), ())), preferred_element_type=f32)


def after(x, done):
    return lax.optimization_barrier((x, done))[0]


def exchange(x, axis, bit):
    return lax.ppermute(x, axis, [(i, i ^ bit) for i in range(lax.axis_size(axis))])


def sum_over(x, axis):
    ways = lax.axis_size(axis)
    if ways & (ways - 1):
        return lax.psum(x, axis)
    bit = 1
    while bit < ways:
        x = x + exchange(x, axis, bit)
        bit *= 2
    return x


def line_gather(x, axis, more=()):
    ways = lax.axis_size(axis)
    here = lax.axis_index(axis)
    up = [(i, i + 1) for i in range(ways - 1)]
    down = [(i + 1, i) for i in range(ways - 1)]
    below = [x]
    above = [x]
    for _ in range(ways - 1):
        below.append(lax.ppermute(below[-1], axis, up))
        above.append(lax.ppermute(above[-1], axis, down))
    below, above, more = lax.optimization_barrier((below, above, more))
    blocks = []
    for slot in range(ways):
        block = x
        for at in range(ways):
            if at != slot:
                block = jnp.where(here == at, below[at - slot] if at > slot else above[slot - at], block)
        blocks.append(block)
    return jnp.concatenate(blocks, 0), more


def line_scatter(x, axis, beside=None):
    ways = lax.axis_size(axis)
    here = lax.axis_index(axis)
    size = x.shape[0] // ways
    up = [(i, i + 1) for i in range(ways - 1)]
    down = [(i + 1, i) for i in range(ways - 1)]

    def block(slot):
        return lax.dynamic_slice_in_dim(x, slot * size, size, 0).astype(f32)

    low = None
    high = None
    other = None
    for k in range(1, ways):
        to_low = block(jnp.maximum(here - (ways - k), 0))
        to_high = block(jnp.minimum(here + (ways - k), ways - 1))
        if low is not None:
            to_low = to_low + low
            to_high = to_high + high
        low = lax.ppermute(to_low.astype(bf16), axis, down)
        high = lax.ppermute(to_high.astype(bf16), axis, up)
        if beside is not None:
            other = beside(k, other)
        low, high, other = lax.optimization_barrier((low, high, other))
        low = low.astype(f32)
        high = high.astype(f32)
    return block(here) + low + high, other


def shifted(x, axis, by):
    ways = lax.axis_size(axis)
    return lax.ppermute(x, axis, [(i, (i + by) % ways) for i in range(ways)])


def ordered(parts, axis):
    ways = len(parts)
    here = lax.axis_index(axis)
    blocks = []
    for slot in range(ways):
        block = parts[0]
        for at in range(ways):
            if at != slot:
                block = jnp.where(here == at, parts[(at - slot) % ways], block)
        blocks.append(block)
    return blocks


def swap_parts(block_to, axis):
    ways = lax.axis_size(axis)
    here = lax.axis_index(axis)
    parts = [block_to(here)]
    for s in range(1, ways):
        parts.append(shifted(block_to((here + s) % ways), axis, s))
    return parts


def swap_blocks(block_to, axis):
    return ordered(swap_parts(block_to, axis), axis)


class PlaneSum:

    def __init__(self, left, right):
        self.ways = lax.axis_size("dp")
        self.parts = ()
        if self.ways != 8:
            self.came = ()
            grad = product(left, right, TN).astype(bf16)
            self.total = lax.psum_scatter(grad, "dp", scatter_dimension=0, tiled=True).astype(f32)
            return
        core = lax.axis_index("dp") % 2
        self.size = left.shape[1] // self.ways
        blocks = [left[:, i * self.size : (i + 1) * self.size] for i in range(self.ways)]
        even = jnp.concatenate(blocks[::2], 1)
        odd = jnp.concatenate(blocks[1::2], 1)
        self.stay = jnp.where(core == 0, even, odd)
        self.right = right
        self.came = exchange(
            product(jnp.where(core == 0, odd, even), right, TN).astype(bf16), "dp", 1
        )

    def send(self):
        if self.ways == 8:
            total = product(self.stay, self.right, TN) + self.came.astype(f32)
            total = total.astype(bf16)
            place = lax.axis_index("dp") // 2
            block = lambda i: lax.dynamic_slice_in_dim(total, i * self.size, self.size, 0)
            self.total = block(place)
            self.parts = [exchange(block(place ^ (m // 2)), "dp", m) for m in (2, 4, 6)]

    def finish(self):
        total = self.total.astype(f32)
        for part in self.parts:
            total = total + part.astype(f32)
        return total


class OutWeights:

    def __init__(self, mixer_out):
        rows = mixer_out.T
        self.ways = lax.axis_size("dp")
        self.parts = ()
        self.rows = jnp.concatenate(swap_blocks(lambda i: rows, "tensor"), 1)

    def start(self, started):
        if self.ways == 8:
            rows = after(self.rows, started)
            self.parts = {m: exchange(rows, "dp", m) for m in (2, 4, 6)}

    def finish(self, done):
        if self.ways != 8:
            return lax.all_gather(self.rows, "dp", axis=0, tiled=True)
        here = lax.axis_index("dp")
        parts = dict(zip((2, 4, 6), after([self.parts[m] for m in (2, 4, 6)], done)))
        parts[0] = self.rows
        size = self.rows.shape[0]
        out = jnp.zeros((self.ways * size, self.rows.shape[1]), bf16)
        for m in (0, 2, 4, 6):
            parts[m + 1] = exchange(parts[m], "dp", 1)
        for m, part in parts.items():
            out = lax.dynamic_update_slice_in_dim(out, part, (here ^ m) * size, 0)
        return out

    def send_sum(self, total, width):
        return swap_parts(
            lambda i: lax.dynamic_slice_in_dim(total, i * width, width, 1), "tensor"
        )


class LineFfn:

    def __init__(self, ffn_in, ffn_out, started):
        self.own = jnp.stack([ffn_in[0].T, ffn_in[1].T, ffn_out])
        self.place = jnp.zeros((), jnp.int32)
        self.near = self.far = ()

    def middle(self, done, more):
        return done, more

    def plane_step(self):
        pass

    def finish(self, done):
        weights = lax.all_gather(self.own, "dp", axis=2, tiled=True)
        return (weights[None],)

    pieces = 1
    where = (((0, 0),),)

    def reach(self, x):
        return line_gather(x, "tensor")[0]

    def beside(self, x):
        return ()

    def gather(self, x, near, far):
        return [far]

    def halves(self, x):
        return line_scatter(x[0], "tensor")[0], jnp.zeros((), bf16)

    def cross(self, far):
        return far

    def sum_start(self, grads):
        self.grads = grads

    def sum_step(self, done):
        return ()

    def sum_far(self, sent):
        pass

    def sum_finish(self):
        return lax.psum_scatter(self.grads[0][0], "dp", scatter_dimension=2, tiled=True)

    def send_sums(self, grads):
        return grads

    def own_grads(self, grads, came):
        return came.astype(f32)


TO_A = [(1, 0), (0, 2), (2, 3), (3, 1)]
TO_B = [(2, 1), (1, 2)]
BACK_A = [(0, 1), (2, 0), (3, 2), (1, 3)]
BACK_B = [(2, 1), (1, 2)]


class PairFfn:

    def __init__(self, ffn_in, ffn_out, started):
        self.core = lax.axis_index("dp") % 2
        self.here = lax.axis_index("tensor")
        self.place = lax.axis_index("dp") // 2
        self.own = after(jnp.stack([ffn_in[0].T, ffn_in[1].T, ffn_out]), started)
        self.a = lax.ppermute(self.own, "tensor", TO_A)
        self.b = lax.ppermute(self.own, "tensor", TO_B)

    def middle(self, done, more):
        here = self.here
        self.own, self.a, self.b, done, more = lax.optimization_barrier(
            (self.own, self.a, self.b, done, more)
        )
        own, a, b = self.own, self.a, self.b
        first = jnp.where(here == 0, own, jnp.where(here == 1, b, a))
        second = jnp.where(here == 3, own, jnp.where(here == 2, b, a))
        mine = jnp.where(self.core == 0, first, second)
        got = exchange(jnp.where(self.core == 0, second, first), "dp", 1)
        self.low = jnp.where(self.core == 0, mine, got)
        self.high = jnp.where(self.core == 0, got, mine)
        done = after(done, (self.low, self.high))
        self.near = exchange(self.low, "dp", 2), exchange(self.high, "dp", 4)
        return done, more

    def plane_step(self):
        self.low = jnp.stack([self.low, self.near[0]])
        self.high = jnp.stack([self.high, self.near[1]])
        self.far = exchange(self.low, "dp", 4), exchange(self.high, "dp", 2)

    def finish(self, done):
        far = after(self.far, done)
        return (self.low, far[0], self.high, far[1])

    pieces = 4
    where = (((0, 0), (0, 1), (1, 0), (1, 1)), ((2, 0), (3, 0), (2, 1), (3, 1)))

    def reach(self, x):
        return exchange(x, "tensor", 1)

    def beside(self, x):
        return exchange(x, "dp", 1)

    def gather(self, x, near, far):
        return [x, near, far, exchange(far, "dp", 1)]

    def halves(self, x):
        far = (x[2].astype(f32) + exchange(x[3], "dp", 1).astype(f32)).astype(bf16)
        return x[0].astype(f32) + exchange(x[1], "dp", 1).astype(f32), far

    def cross(self, far):
        return exchange(far, "tensor", 1)

    def sum_start(self, grads):
        self.grads = grads
        low, high = grads
        across_x = jnp.stack([low[1], low[3]])
        self.near = exchange(across_x, "dp", 2), exchange(high[2:], "dp", 4)

    def sum_step(self, done):
        low, high = self.grads
        came = after(self.near, done)
        add = lambda x, y: (x.astype(f32) + y.astype(f32)).astype(bf16)
        self.kept = add(low[0], came[0][0]), add(high[0], came[1][0])
        return add(low[2], came[0][1]), add(high[1], came[1][1])

    def sum_far(self, sent):
        self.far = exchange(sent[0], "dp", 4), exchange(sent[1], "dp", 2)

    def sum_finish(self):
        came = self.far
        add = lambda x, y: (x.astype(f32) + y.astype(f32)).astype(bf16)
        low = add(self.kept[0], came[0])
        high = add(self.kept[1], came[1])
        core = self.core
        mine = jnp.where(core == 0, low, high)
        got = exchange(jnp.where(core == 0, high, low), "dp", 1)
        return jnp.where(core == 0, mine, got), jnp.where(core == 0, got, mine)

    def send_sums(self, sums):
        first, second = sums
        here = self.here
        a = lax.ppermute(jnp.where(here < 2, second, first), "tensor", BACK_A)
        b = lax.ppermute(jnp.where(here == 2, second, first), "tensor", BACK_B)
        return a, b

    def own_grads(self, sums, came):
        first, second = sums
        a, b = came
        here = self.here
        other = jnp.where(here == 0, first, jnp.where(here == 3, second, b))
        return a.astype(f32) + other.astype(f32)


CONV_AT = 64


def column_blocks(value, rows):
    ways, size = value.shape
    lanes = -(-size // rows)
    value = jnp.pad(value, ((0, 0), (0, lanes * rows - size)))
    return value.reshape(ways, lanes, rows).swapaxes(1, 2).reshape(ways * rows, lanes)


def from_columns(columns, shape, dim, rows):
    ways = columns.shape[0] // rows
    size = 1
    for extent in shape:
        size *= extent
    value = columns.reshape(ways, rows, -1).swapaxes(1, 2).reshape(ways, -1)[:, :size]
    value = jnp.moveaxis(value.reshape((ways,) + shape), 0, dim)
    return value.reshape(shape[:dim] + (ways * shape[dim],) + shape[dim + 1 :])


def lanes_of(small, conv, onorm):
    rows, width = small.shape
    used = BETA_AT + width
    rest = LANES - CONV_AT - conv.shape[1] - onorm.shape[1]
    zeros = lambda lanes: jnp.zeros((rows, lanes), small.dtype)
    return jnp.concatenate(
        [zeros(BETA_AT), small, zeros(CONV_AT - used), conv, onorm, zeros(rest)], 1
    )


def fetch_mixer(mixer_in, mixer_small, conv_weight, out_norm):
    rows, width = mixer_in.shape
    small = jnp.moveaxis(mixer_small, 0, 1).reshape(rows, -1)
    conv = column_blocks(conv_weight.reshape(1, -1), rows)
    onorm = column_blocks(out_norm.reshape(1, -1), rows)
    extended = jnp.concatenate([mixer_in, lanes_of(small, conv, onorm)], 1)
    w_in = lax.all_gather(extended, "dp", axis=0, tiled=True)
    at = width + CONV_AT
    w_conv = from_columns(w_in[:, at : at + conv.shape[1]], conv_weight.shape, 2, rows)
    at += conv.shape[1]
    w_onorm = from_columns(w_in[:, at : at + onorm.shape[1]], out_norm.shape, 1, rows)
    return w_in, w_conv, w_onorm


def shards(
    tokens, cotangent, segments, norm_gains, mixer_in, mixer_small, conv_weight, head_params,
    out_norm, mixer_out, ffn_in, ffn_out,
):
    heads = mixer_in.shape[1] // MIX
    all_heads = head_params.shape[1]
    ways = lax.axis_size("dp")
    teams = lax.axis_size("tensor")
    head_start = lax.axis_index("tensor") * heads
    head_local = lax.dynamic_slice_in_dim(head_params, head_start, heads, 1)
    gains = norm_gains.astype(f32)
    own = tokens.shape[0]
    inputs = tokens.astype(f32)
    factor_one = norm_factor(inputs)
    scaled_one = inputs * factor_one
    normed_one = (scaled_one * gains[0]).astype(bf16)
    out_weights = OutWeights(mixer_out)
    w_in, w_conv, w_onorm = fetch_mixer(mixer_in, mixer_small, conv_weight, out_norm)
    conv_rows = w_conv.astype(f32).reshape(TAPS, heads * CONV)
    onorm_row = w_onorm.astype(f32).reshape(1, heads * DV)
    head_rows = head_lanes(head_local)
    places = token_places(segments)
    kind = PairFfn if teams == 4 and ways == 8 else LineFfn
    rows_one, (out_weights.rows, constants, places, cot_near) = line_gather(
        normed_one,
        "tensor",
        (
            out_weights.rows, (conv_rows, head_rows, onorm_row), places,
            kind.beside(None, cotangent),
        ),
    )
    out_weights.start(rows_one)
    ffn = kind(ffn_in, ffn_out, rows_one)
    wide = heads * MIX
    proj = product(rows_one, w_in, NN)
    carry = forward_start(heads)
    made = []
    for part in range(PARTS):
        made, carry = mixer_forward(part, made, places, proj, *constants, carry, heads)
        if part == 0:
            carry, (cotangent, out_weights.parts) = ffn.middle(
                carry, (cotangent, out_weights.parts)
            )
            cot_far = ffn.reach(cotangent)
    mixed, *kept = made
    mixed, cot_far, ffn.near = lax.optimization_barrier((mixed, cot_far, ffn.near))
    ffn.plane_step()
    came = swap_parts(lambda i: lax.dynamic_slice_in_dim(mixed, i * own, own, 0), "tensor")
    out_t = out_weights.finish(came[-1])
    grad_rows = ffn.gather(cotangent, cot_near, after(cot_far, came[-1]))
    mixed = jnp.concatenate(ordered(came, "tensor"), 1)
    middle = inputs + product(mixed, out_t, NT)
    factor_two = norm_factor(middle)
    scaled_two = middle * factor_two
    normed_two = (scaled_two * gains[1]).astype(bf16)
    rows_two = ffn.gather(normed_two, ffn.beside(normed_two), ffn.reach(normed_two))
    w_ffn = ffn.finish(normed_two)
    grad_gate, grad_up, hidden, back, forth = ffn_both(
        ffn.place, rows_two, grad_rows, w_ffn, ffn.where
    )
    grad_normed_two, far = ffn.halves(back)
    ffn_grads = ffn_weight_grads(
        ffn.place, after(rows_two, far), grad_rows, grad_gate, grad_up, hidden,
        ffn.pieces, len(ffn.where),
    )
    far, ffn_grads = lax.optimization_barrier((ffn.cross(far), ffn_grads))
    grad_normed_two = grad_normed_two + far.astype(f32)
    ffn.sum_start(ffn_grads)
    grad_middle_norm, grad_gain_two = norm_backward(
        grad_normed_two, scaled_two, factor_two, gains[1]
    )
    grad_middle = cotangent.astype(f32) + grad_middle_norm
    branch_grad = grad_middle.astype(bf16)
    grad_mixed = product(branch_grad, out_t, NN).astype(bf16)
    width = heads * DV
    came = swap_parts(
        lambda i: lax.dynamic_slice_in_dim(grad_mixed, i * width, width, 1), "tensor"
    )
    branch_grad, forth, near = after((branch_grad, forth, ffn.near), grad_mixed)
    ffn.near = near
    out_sum = PlaneSum(branch_grad, mixed)
    result, far = ffn.halves(forth)
    came, far, sums = lax.optimization_barrier((came, far, ffn.sum_step(grad_mixed)))
    ffn.sum_far(sums)
    result = result, ffn.cross(far)
    grad_mixed = jnp.concatenate(ordered(came, "tensor"), 0)
    carry = backward_start(heads)
    grad_proj = []
    for part in reversed(range(PARTS)):
        dproj, carry = mixer_backward(
            part, grad_proj, places, proj, *constants, kept, grad_mixed, carry, heads
        )
        grad_proj = [dproj]
        if part == PARTS - 1:
            carry, result, ffn.far, out_sum.came = lax.optimization_barrier(
                (carry, result, ffn.far, out_sum.came)
            )
            out_sum.send()
            ffn_sums = ffn.sum_finish()
            carry = after(carry, ffn_sums)
            ffn_came = ffn.send_sums(ffn_sums)
    grad_proj, ffn_came, out_sum.parts = lax.optimization_barrier(
        (dproj, ffn_came, out_sum.parts)
    )
    grad_conv, grad_head, grad_onorm = carry[2:]
    result = middle + result[0] + result[1].astype(f32)
    sent = product(grad_proj, w_in, NT).astype(bf16)
    grad_normed_one = lax.psum_scatter(
        sent, "tensor", scatter_dimension=0, tiled=True
    ).astype(f32)
    grad_proj = after(grad_proj, sent)
    grad_in = PlaneSum(rows_one, grad_proj[:, :wide])
    grad_in.send()
    head_full = lax.dynamic_update_slice_in_dim(
        jnp.zeros((2, all_heads), f32),
        grad_head[:2, BETA_AT + heads : BETA_AT + 2 * heads],
        head_start,
        1,
    )
    d = gains.shape[1]
    sizes = [2 * d + 2 * all_heads, grad_conv.size, grad_onorm.size, 2 * heads * d]
    ends = [sum(sizes[:i]) for i in range(5)]
    at = BETA_AT + 2 * heads
    grad_small = product(rows_one, grad_proj[:, wide:], TN)[:, BETA_AT:at]
    again = after(sent, grad_in.total)
    gain_one = jnp.sum(again.astype(f32) * rows_one.astype(f32), 0) / gains[0]
    parts = [
        gain_one, grad_gain_two, head_full.reshape(-1), grad_conv.reshape(-1),
        grad_onorm.reshape(-1), grad_small.T.reshape(-1),
    ]
    totals = sum_over(jnp.concatenate(parts), "dp")
    shared = totals[: sizes[0]]
    shared = sum(ordered(swap_parts(lambda i: shared, "tensor"), "tensor"))
    out_parts = after(out_sum.finish().astype(bf16), grad_in.total)
    out_out = sum(block.astype(f32) for block in out_weights.send_sum(out_parts, width))
    conv_total, onorm_total, small_total = (totals[ends[i] : ends[i + 1]] for i in (1, 2, 3))
    place = lax.axis_index("dp")

    def own_part(total, shape):
        size = shape[-1] // ways
        return lax.dynamic_slice_in_dim(total.reshape(shape), place * size, size, len(shape) - 1)

    out_conv = own_part(conv_total, (TAPS, heads, CONV))
    out_onorm = own_part(onorm_total, (heads, DV))
    out_small = own_part(small_total, (2, heads, d)).swapaxes(1, 2)
    totals = shared
    out_in = grad_in.finish()
    ffn_grads = ffn.own_grads(ffn_sums, ffn_came)
    grad_scaled = grad_normed_one * gains[0]
    grad_tokens = grad_middle + factor_one * (
        grad_scaled - scaled_one * jnp.mean(grad_scaled * scaled_one, -1, keepdims=True)
    )
    return (
        result.astype(bf16),
        grad_tokens,
        totals[: 2 * d].reshape(2, d),
        out_in,
        out_small,
        out_conv,
        totals[2 * d :].reshape(2, all_heads),
        out_onorm,
        out_out.T,
        ffn_grads[:2].swapaxes(1, 2),
        ffn_grads[2],
    )


def solution(mesh):
    in_specs = (
        P(("dp", "tensor"), None),
        P(("dp", "tensor"), None),
        P("dp", None),
        P(),
        P("dp", "tensor"),
        P(None, "dp", "tensor"),
        P(None, "tensor", "dp"),
        P(),
        P("tensor", "dp"),
        P("tensor", "dp"),
        P(None, "dp", "tensor"),
        P("tensor", "dp"),
    )
    out_specs = (
        P(("dp", "tensor"), None),
        P(("dp", "tensor"), None),
        P(),
        P("dp", "tensor"),
        P(None, "dp", "tensor"),
        P(None, "tensor", "dp"),
        P(),
        P("tensor", "dp"),
        P("tensor", "dp"),
        P(None, "dp", "tensor"),
        P("tensor", "dp"),
    )
    return jax.shard_map(shards, mesh=mesh, in_specs=in_specs, out_specs=out_specs, check_vma=False)
```

```python
import functools
import jax
import jax.numpy as jnp
from jax import lax
from jax.experimental import pallas as pl
from jax.experimental.pallas import tpu as pltpu
from jax.sharding import PartitionSpec as P

DK = 128
DV = 256
MIX = 2 * DK + 2 * DV
CONV = 2 * DK + DV
CHUNK = 128
LANES = 128
TAPS = 4
BASE = 16
PER = 2
BACK = 2
PARTS = 2
BETA_AT = 8

NN = ((1,), (0,))
NT = ((1,), (1,))
TN = ((0,), (0,))

f32 = jnp.float32
bf16 = jnp.bfloat16


def dot(a, b, dims, passes, join=False):
    if passes == 6:
        return lax.dot_general(
            a, b, (dims, ((), ())), precision=lax.Precision.HIGHEST, preferred_element_type=f32
        )
    a_hi = a.astype(bf16)
    b_hi = b.astype(bf16)
    product = lambda x, y: lax.dot_general(x, y, (dims, ((), ())), preferred_element_type=f32)
    if passes == 1:
        return product(a_hi, b_hi)
    a_lo = (a - a_hi.astype(f32)).astype(bf16)
    b_lo = (b - b_hi.astype(f32)).astype(bf16)
    (a_dim,), (b_dim,) = dims
    if not join:
        return product(a_hi, b_hi) + product(a_hi, b_lo) + product(a_lo, b_hi)
    both = product(
        jnp.concatenate([a_hi, a_lo], a_dim), jnp.concatenate([b_hi, b_hi], b_dim)
    )
    return both + product(a_hi, b_lo)


def exact_left(mask, b):
    hi = b.astype(bf16)
    rest = b - hi.astype(f32)
    mid = rest.astype(bf16)
    low = (rest - mid.astype(f32)).astype(bf16)
    out = lax.dot_general(mask, hi, (NN, ((), ())), preferred_element_type=f32)
    out = out + lax.dot_general(mask, mid, (NN, ((), ())), preferred_element_type=f32)
    return out + lax.dot_general(mask, low, (NN, ((), ())), preferred_element_type=f32)


def sigmoid(x):
    return 1.0 / (1.0 + jnp.exp(-x))


def log1p(y):
    return jnp.where(y < 1e-4, y - 0.5 * y * y, jnp.log(1.0 + y))


def softplus(x):
    return jnp.maximum(x, 0.0) + log1p(jnp.exp(-jnp.abs(x)))


def iotas():
    shape = (CHUNK, CHUNK)
    return lax.broadcasted_iota(jnp.int32, shape, 0), lax.broadcasted_iota(jnp.int32, shape, 1)


def token_scalars(info, head_rows, heads):
    row, col = iotas()
    beta = sigmoid(info)
    rate = -jnp.exp(head_rows[0:1])
    pre = info + head_rows[1:2]
    g = rate * softplus(pre)
    total = exact_left((row >= col).astype(bf16), g)
    lane = lax.broadcasted_iota(jnp.int32, (CHUNK, LANES), 1)
    across = jnp.where(lane < BETA_AT, info, total).T
    return beta, g, pre, total, across


def head_scalars(h, heads, info, beta, total, across):
    row, col = iotas()
    at = BETA_AT + heads + h
    seg_col = info[:, 0:1]
    seg_row = across[0:1, :]
    tot_col = total[:, at : at + 1]
    tot_row = across[at : at + 1, :]
    keep = (seg_col == seg_row) & (row >= col)
    decay = jnp.exp(jnp.where(keep, tot_col - tot_row, -1e30))
    strict = jnp.where(row > col, decay, 0.0)
    beta_col = beta[:, BETA_AT + h : BETA_AT + h + 1]
    carried = jnp.exp(tot_col) * info[:, 7:8]
    last = CHUNK - 1
    end = jnp.where(
        seg_col == seg_col[last : last + 1], jnp.exp(tot_col[last : last + 1] - tot_col), 0.0
    )
    carried_last = carried[last : last + 1]
    return decay, strict, beta_col, carried, end, carried_last


def invert(lowers, passes):
    row, col = iotas()
    shape = (BASE, CHUNK)
    lane = lax.broadcasted_iota(jnp.int32, shape, 1)
    own = lax.broadcasted_iota(jnp.int32, shape, 0)
    start = lane // BASE * BASE
    blocks = CHUNK // BASE
    inside = [lane // BASE == b for b in range(blocks)]
    packs = []
    for lower in lowers:
        packed = jnp.zeros(shape, f32)
        for b in range(blocks):
            packed = jnp.where(inside[b], lower[b * BASE : (b + 1) * BASE], packed)
        packs.append(packed)
    invs = [jnp.where(own == lane % BASE, 1.0, 0.0)] * len(lowers)
    for j in range(BASE - 1):
        at = start + j
        invs = [
            inv - jnp.take_along_axis(packed, at, axis=1) * inv[j : j + 1]
            for inv, packed in zip(invs, packs)
        ]
    invs = [
        jnp.concatenate([jnp.where(inside[b], inv, 0.0) for b in range(blocks)], 0) for inv in invs
    ]
    size = BASE
    while size < CHUNK:
        part = ((row // (2 * size)) == (col // (2 * size))) & ((row // size) != (col // size))
        steps = [
            dot(jnp.where(part, lower, 0.0), inv, NN, passes, True) for lower, inv in zip(lowers, invs)
        ]
        invs = [inv - dot(inv, step, NN, passes, True) for inv, step in zip(invs, steps)]
        size *= 2
    return invs


def normalised(act):
    factor = lax.rsqrt(jnp.sum(act * act, -1, keepdims=True) + 1e-06)
    return act * factor, factor


def with_scalars(places, extra, heads):
    lane = lax.broadcasted_iota(jnp.int32, places.shape, 1)
    return jnp.where((lane >= BETA_AT) & (lane < BETA_AT + 2 * heads), extra, places)


def forward_body(
    heads, prec, places_ref, extra_ref, proj_ref, conv_ref, head_ref, onorm_ref, state_in_ref,
    tail_in_ref,
    *refs,
):
    (
        z_ref, mixed_ref, out_ref, delta_ref, across_ref, state_out_ref, solve_ref, kk_ref, qk_ref,
        state_ref, tail_ref,
    ) = refs[-11:]

    @pl.when(pl.program_id(0) == 0)
    def _():
        state_ref[...] = state_in_ref[...]
        tail_ref[...] = tail_in_ref[...]

    rows = PER * CHUNK
    ready = {}
    first = {}
    infos = [
        with_scalars(
            places_ref[u * CHUNK : (u + 1) * CHUNK],
            extra_ref[u * CHUNK : (u + 1) * CHUNK],
            heads,
        )
        for u in range(PER)
    ]
    scalars = [token_scalars(info, head_ref[...], heads) for info in infos]
    for h in range(heads):
        at = h * MIX
        cat = h * CONV
        part = proj_ref[:, at : at + CONV]
        ext = jnp.concatenate([tail_ref[:, cat : cat + CONV], part], 0)
        tail_ref[:, cat : cat + CONV] = part[rows - 8 :]
        mixed = conv_ref[TAPS - 1 : TAPS, cat : cat + CONV] * part
        for s in range(1, TAPS):
            shifted = ext[8 - s : 8 - s + rows]
            mixed = mixed + conv_ref[TAPS - 1 - s : TAPS - s, cat : cat + CONV] * jnp.where(
                places_ref[:, s : s + 1] > 0.5, shifted, 0.0
            )
        mixed_ref[:, cat : cat + CONV] = mixed
        act = mixed * sigmoid(mixed)
        queries, _ = normalised(act[:, :DK])
        queries = queries * DK ** (-0.5)
        keys, _ = normalised(act[:, DK : 2 * DK])
        for u in range(PER):
            own = slice(u * CHUNK, (u + 1) * CHUNK)
            query = queries[own]
            key = keys[own]
            value = act[own, 2 * DK :]
            beta, g, pre, total, across = scalars[u]
            decay, strict, beta_col, carried, end, carried_last = head_scalars(
                h, heads, infos[u], beta, total, across
            )
            inner = dot(jnp.concatenate([key, query], 0), key, NT, prec["kk"], True)
            kk = inner[:CHUNK]
            qk = inner[CHUNK:]
            kk_ref[u, h] = kk
            qk_ref[u, h] = qk
            first[u, h] = (
                beta_col * strict * kk,
                jnp.concatenate([beta_col * value, (beta_col * carried) * key], 1),
                carried * query, decay * qk, end * key, carried_last,
            )
    order = list(first)
    for at, inv in zip(order, invert([first[at][0] for at in order], prec["inv"])):
        u, h = at
        own = slice(u * CHUNK, (u + 1) * CHUNK)
        lower, sides, reads_q, attend, ends, carried_last = first[at]
        solve_ref[u, h] = inv
        solved = dot(inv, sides, NN, prec["solve"], True)
        across_ref[own, h * DK : (h + 1) * DK] = solved[:, DV:]
        ready[at] = (
            jnp.concatenate([reads_q, solved[:, DV:]], 0), solved[:, :DV], attend, ends,
            carried_last,
        )
    for u in range(PER):
        own = slice(u * CHUNK, (u + 1) * CHUNK)
        for h in range(heads):
            readers, fixed, attend, ends, carried_last = ready[u, h]
            state = state_ref[h]
            state_out_ref[u, h] = state
            reads = dot(readers, state, NN, prec["state"], True)
            delta = fixed - reads[CHUNK:]
            state_ref[h] = carried_last * state + dot(ends, delta, TN, prec["state"], True)
            result = reads[:CHUNK] + dot(attend, delta, NN, prec["attend"], True)
            delta_ref[own, h * DV : (h + 1) * DV] = delta
            out_ref[own, h * DV : (h + 1) * DV] = result
            gate = proj_ref[own, h * MIX + CONV : (h + 1) * MIX]
            factor = lax.rsqrt(jnp.mean(result * result, -1, keepdims=True) + 1e-05)
            z = result * factor * onorm_ref[:, h * DV : (h + 1) * DV] * (gate * sigmoid(gate))
            z_ref[own, h * DV : (h + 1) * DV] = z.astype(bf16)


def backward_body(
    heads, prec, places_ref, extra_ref, proj_ref, conv_ref, head_ref, onorm_ref,
    mixed_ref, out_ref, delta_ref, across_ref, state_in_ref, solve_ref, kk_ref, qk_ref, dz_ref,
    dstate_in_ref, lead_in_ref, dconv_in_ref, dhead_in_ref, donorm_in_ref,
    *refs,
):
    dproj_ref, dstate_ref, lead_ref, dconv_ref, dhead_ref, donorm_ref = refs[-6:]

    @pl.when(pl.program_id(0) == 0)
    def _():
        dstate_ref[...] = dstate_in_ref[...]
        lead_ref[...] = lead_in_ref[...]
        dconv_ref[...] = dconv_in_ref[...]
        dhead_ref[...] = dhead_in_ref[...]
        donorm_ref[...] = donorm_in_ref[...]

    row, col = iotas()
    lane = lax.broadcasted_iota(jnp.int32, (CHUNK, LANES), 1)
    from_here = (row <= col).astype(bf16)
    items = [(u, h) for u in reversed(range(BACK)) for h in range(heads)]
    rows_of = {u: slice(u * CHUNK, (u + 1) * CHUNK) for u in range(BACK)}
    infos = {
        u: with_scalars(places_ref[rows_of[u]], extra_ref[rows_of[u]], heads)
        for u in range(BACK)
    }
    scalars = {u: token_scalars(infos[u], head_ref[...], heads) for u in range(BACK)}
    made = {}
    for u, h in items:
        own = rows_of[u]
        cat = h * CONV
        at = h * MIX
        mixed = mixed_ref[own, cat : cat + CONV]
        msig = sigmoid(mixed)
        act = mixed * msig
        q_unit, q_factor = normalised(act[:, :DK])
        key, k_factor = normalised(act[:, DK : 2 * DK])
        value = act[:, 2 * DK :]
        beta, g, pre, total, across = scalars[u]
        decay, strict, beta_col, carried, end, carried_last = head_scalars(
            h, heads, infos[u], beta, total, across
        )
        result = out_ref[own, h * DV : (h + 1) * DV]
        gate = proj_ref[own, at + CONV : at + MIX]
        gsig = sigmoid(gate)
        silu = gate * gsig
        onorm = onorm_ref[:, h * DV : (h + 1) * DV]
        factor = lax.rsqrt(jnp.mean(result * result, -1, keepdims=True) + 1e-05)
        normed = result * factor
        dz = dz_ref[own, h * DV : (h + 1) * DV].astype(f32)
        dzn = dz * normed
        donorm_ref[:, h * DV : (h + 1) * DV] += jnp.sum(dzn * silu, 0, keepdims=True)
        dgate = dzn * onorm * (gsig * (1.0 + gate * (1.0 - gsig)))
        dproj_ref[own, at + CONV : at + MIX] = dgate.astype(bf16)
        dnormed = dz * onorm * silu
        dout = factor * (dnormed - normed * jnp.mean(dnormed * normed, -1, keepdims=True))
        through = dot(decay * qk_ref[u, h], dout, TN, prec["attend"])
        made[u, h] = (
            mixed, msig, q_unit, q_factor, key, k_factor, value, decay, strict, beta_col, carried,
            end, carried_last, dout, through,
        )
    chain = {}
    for u, h in items:
        own = rows_of[u]
        q_unit, key, carried, end, carried_last, dout, through = (
            made[u, h][i] for i in (2, 4, 10, 11, 12, 13, 14)
        )
        dnext = dstate_ref[h]
        ddelta = through + dot(end * key, dnext, NN, prec["state"])
        dstate_ref[h] = carried_last * dnext + dot(
            jnp.concatenate(
                [carried * (q_unit * DK ** (-0.5)), -across_ref[own, h * DK : (h + 1) * DK]], 0
            ),
            jnp.concatenate([dout, ddelta], 0),
            TN,
            prec["state"],
        )
        chain[u, h] = (dnext, ddelta)
    solved = {}
    for u, h in items:
        own = rows_of[u]
        dnext, ddelta = chain[u, h]
        delta = delta_ref[own, h * DV : (h + 1) * DV]
        state = state_in_ref[u, h]
        x = dot(solve_ref[u, h], ddelta, TN, prec["solve"])
        dend = dot(delta, dnext, NT, prec["big"])
        dcl = jnp.sum(jnp.sum(state * dnext, 0, keepdims=True), 1, keepdims=True)
        big = dot(
            jnp.concatenate([made[u, h][13], x], 0),
            jnp.concatenate([state, delta], 0),
            NT,
            prec["big"],
        )
        solved[u, h] = (x, dend, dcl, big)
    inner = {}
    for u, h in items:
        q_unit, key, decay, strict, beta_col = (made[u, h][i] for i in (2, 4, 7, 8, 9))
        x, dend, dcl, big = solved[u, h]
        query = q_unit * DK ** (-0.5)
        dqk = decay * big[:CHUNK, DK:]
        das = -strict * big[CHUNK:, DK:]
        bdas = beta_col * das
        rows = dot(jnp.concatenate([dqk, das], 0), key, NN, prec["kk"])
        cols = dot(
            jnp.concatenate([dqk, bdas], 0),
            jnp.concatenate([query, key], 0),
            TN,
            prec["kk"],
        )
        pairs = jnp.where(row > col, dqk * qk_ref[u, h] + bdas * kk_ref[u, h], 0.0)
        inner[u, h] = (rows, cols, exact_left(from_here, pairs))
    sums = {
        u: [jnp.zeros((CHUNK, LANES), f32) for _ in range(4)] for u in range(BACK)
    }
    dacts = {}
    for u, h in items:
        (
            mixed, msig, q_unit, q_factor, key, k_factor, value, decay, strict, beta_col, carried,
            end, carried_last, dout, through,
        ) = made[u, h]
        x, dend, dcl, big = solved[u, h]
        rows, cols, pairs = inner[u, h]
        query = q_unit * DK ** (-0.5)
        dqc = carried * big[:CHUNK, :DK]
        dq = rows[:CHUNK] + dqc
        dk_end = end * dend
        dkb_c = -carried * big[CHUNK:, :DK]
        dk_row_b = rows[CHUNK:] + dkb_c
        dk = beta_col * dk_row_b + cols + dk_end
        xv = x * value
        dbeta = jnp.sum(xv[:, :DK] + xv[:, DK:] + key * dk_row_b, -1, keepdims=True)
        reach = jnp.sum(query * dqc + key * (beta_col * dkb_c), -1, keepdims=True)
        leave = jnp.sum(key * dk_end, -1, keepdims=True)
        spans = jnp.sum(jnp.where(row > col, pairs, 0.0), -1, keepdims=True) + carried_last * dcl
        at_h = lane == BETA_AT + heads + h
        sums[u][0] = jnp.where(lane == BETA_AT + h, dbeta, sums[u][0])
        sums[u][1] = jnp.where(at_h, reach, sums[u][1])
        sums[u][2] = jnp.where(at_h, leave, sums[u][2])
        sums[u][3] = jnp.where(at_h, spans, sums[u][3])
        scale_q = DK ** (-0.5) * q_factor
        daq = scale_q * (dq - q_unit * jnp.sum(q_unit * dq, -1, keepdims=True))
        dak = k_factor * (dk - key * jnp.sum(key * dk, -1, keepdims=True))
        dact = jnp.concatenate([daq, dak, beta_col * x], 1)
        dacts[u, h] = dact * (msig * (1.0 + mixed * (1.0 - msig)))
    for h in range(heads):
        at = h * MIX
        cat = h * CONV
        dmixed = jnp.concatenate([dacts[u, h] for u in range(BACK)], 0)
        ext = jnp.concatenate([dmixed, lead_ref[:, cat : cat + CONV]], 0)
        lead_ref[:, cat : cat + CONV] = dmixed[:8]
        part = proj_ref[:, at : at + CONV]
        dpart = conv_ref[TAPS - 1 : TAPS, cat : cat + CONV] * dmixed
        dconv_ref[TAPS - 1 : TAPS, cat : cat + CONV] += jnp.sum(dmixed * part, 0, keepdims=True)
        for s in range(1, TAPS):
            shifted = jnp.where(
                places_ref[:, 3 + s : 4 + s] > 0.5, ext[s : s + BACK * CHUNK], 0.0
            )
            dpart = dpart + conv_ref[TAPS - 1 - s : TAPS - s, cat : cat + CONV] * shifted
            dconv_ref[TAPS - 1 - s : TAPS - s, cat : cat + CONV] += jnp.sum(
                shifted * part, 0, keepdims=True
            )
        dproj_ref[:, at : at + CONV] = dpart.astype(bf16)
    rate = -jnp.exp(head_ref[0:1])
    for u in range(BACK):
        beta, g, pre, total, across = scalars[u]
        dbeta_all, reach_all, leave_all, spans_all = sums[u]
        dg = spans_all + exact_left(from_here, reach_all)
        dg = dg + exact_left((row > col).astype(bf16), leave_all)
        dpre = dg * rate * sigmoid(pre)
        dsmall = dbeta_all * beta * (1.0 - beta) + dpre
        dproj_ref[rows_of[u], heads * MIX :] = dsmall.astype(bf16)
        dhead_ref[0:1] += jnp.sum(dg * g, 0, keepdims=True)
        dhead_ref[1:2] += jnp.sum(dpre, 0, keepdims=True)


PREC = {"kk": 3, "inv": 3, "solve": 3, "state": 3, "attend": 3, "big": 3}
BUDGET = 56 << 20


def whole(shape):
    return pl.BlockSpec(shape, lambda c: (0,) * len(shape))


def forward_start(heads):
    return [jnp.zeros((heads, DK, DV), f32), jnp.zeros((8, heads * CONV), f32)]


def mixer_forward(part, before, places, proj, conv, head_rows, onorm, carry, heads, prec=PREC):
    length = proj.shape[0]
    count = length // CHUNK
    steps = count // PER // PARTS
    first = part * steps
    chunk = lambda width: pl.BlockSpec((PER * CHUNK, width), lambda c: (first + c, 0))
    lanes = pl.BlockSpec((PER * CHUNK, LANES), lambda c: (first + c, heads * MIX // LANES))
    square = lambda rows, width: pl.BlockSpec(
        (PER, heads, rows, width), lambda c: (first + c, 0, 0, 0)
    )
    outs = pl.pallas_call(
        functools.partial(forward_body, heads, prec),
        grid=(steps,),
        in_specs=[chunk(LANES), lanes, chunk(heads * MIX)]
        + [whole(x.shape) for x in (conv, head_rows, onorm, *carry)]
        + [pl.BlockSpec(memory_space=pl.ANY)] * len(before),
        out_specs=[
            chunk(heads * DV), chunk(heads * CONV), chunk(heads * DV), chunk(heads * DV),
            chunk(heads * DK), square(DK, DV), square(CHUNK, CHUNK), square(CHUNK, CHUNK),
            square(CHUNK, CHUNK),
        ]
        + [whole(x.shape) for x in carry],
        out_shape=[
            jax.ShapeDtypeStruct((length, heads * DV), bf16),
            jax.ShapeDtypeStruct((length, heads * CONV), f32),
            jax.ShapeDtypeStruct((length, heads * DV), f32),
            jax.ShapeDtypeStruct((length, heads * DV), f32),
            jax.ShapeDtypeStruct((length, heads * DK), f32),
            jax.ShapeDtypeStruct((count, heads, DK, DV), f32),
            jax.ShapeDtypeStruct((count, heads, CHUNK, CHUNK), f32),
            jax.ShapeDtypeStruct((count, heads, CHUNK, CHUNK), f32),
            jax.ShapeDtypeStruct((count, heads, CHUNK, CHUNK), f32),
        ]
        + [jax.ShapeDtypeStruct(x.shape, f32) for x in carry],
        compiler_params=pltpu.CompilerParams(
            dimension_semantics=("arbitrary",), vmem_limit_bytes=BUDGET
        ),
        cost_estimate=pl.CostEstimate(
            flops=length * heads * 32000000, bytes_accessed=length * heads * 6000, transcendentals=0
        ),
        input_output_aliases={6 + len(carry) + i: i for i in range(len(before))},
        name="mixer_forward",
    )(places, proj, proj, conv, head_rows, onorm, *carry, *before)
    return outs[:-2], outs[-2:]


def backward_start(heads):
    return [
        jnp.zeros((heads, DK, DV), f32), jnp.zeros((8, heads * CONV), f32),
        jnp.zeros((TAPS, heads * CONV), f32), jnp.zeros((8, LANES), f32),
        jnp.zeros((1, heads * DV), f32),
    ]


def mixer_backward(
    part, before, places, proj, conv, head_rows, onorm, kept, dz, carry, heads, prec=PREC
):
    length = proj.shape[0]
    steps = length // (BACK * CHUNK) // PARTS
    last = part * steps + steps - 1
    chunk = lambda width: pl.BlockSpec((BACK * CHUNK, width), lambda c: (last - c, 0))
    lanes = pl.BlockSpec((BACK * CHUNK, LANES), lambda c: (last - c, heads * MIX // LANES))
    square = lambda rows, width: pl.BlockSpec(
        (BACK, heads, rows, width), lambda c: (last - c, 0, 0, 0)
    )
    dproj, *carry = pl.pallas_call(
        functools.partial(backward_body, heads, prec),
        grid=(steps,),
        in_specs=[chunk(LANES), lanes, chunk(heads * MIX)]
        + [whole(x.shape) for x in (conv, head_rows, onorm)]
        + [
            chunk(heads * CONV), chunk(heads * DV), chunk(heads * DV),
            chunk(heads * DK), square(DK, DV), square(CHUNK, CHUNK), square(CHUNK, CHUNK),
            square(CHUNK, CHUNK), chunk(heads * DV),
        ]
        + [whole(x.shape) for x in carry]
        + [pl.BlockSpec(memory_space=pl.ANY)] * len(before),
        out_specs=[chunk(heads * MIX + LANES)] + [whole(x.shape) for x in carry],
        out_shape=[jax.ShapeDtypeStruct((length, heads * MIX + LANES), bf16)]
        + [jax.ShapeDtypeStruct(x.shape, f32) for x in carry],
        compiler_params=pltpu.CompilerParams(
            dimension_semantics=("arbitrary",), vmem_limit_bytes=BUDGET
        ),
        cost_estimate=pl.CostEstimate(
            flops=length * heads * 48000000, bytes_accessed=length * heads * 7000, transcendentals=0
        ),
        input_output_aliases={7 + len(kept) + len(carry): 0} if before else {},
        name="mixer_backward",
    )(places, proj, proj, conv, head_rows, onorm, *kept, dz, *carry, *before)
    return dproj, carry


def token_places(segments):
    length = segments.shape[-1]
    seg = segments.reshape(length)
    columns = [seg.astype(f32)]
    for s in range(1, TAPS):
        before = jnp.concatenate([jnp.full((s,), -1, seg.dtype), seg[:-s]])
        columns.append((before == seg).astype(f32))
    for s in range(1, TAPS):
        beyond = jnp.concatenate([seg[s:], jnp.full((s,), -1, seg.dtype)])
        columns.append((beyond == seg).astype(f32))
    ends = seg.reshape(-1, CHUNK)[:, -1]
    ends = jnp.concatenate([jnp.full((1,), -1, seg.dtype), ends[:-1]])
    columns.append((jnp.repeat(ends, CHUNK) == seg).astype(f32))
    return jnp.pad(jnp.stack(columns, 1), ((0, 0), (0, LANES - len(columns))))


def head_lanes(head):
    heads = head.shape[1]
    return jnp.pad(head, ((0, 6), (BETA_AT + heads, LANES - BETA_AT - 2 * heads)))


def ffn_body(where, runs, place_ref, *refs):
    step = pl.program_id(0)
    each = pl.num_programs(0) // runs
    rows_refs = refs[:runs]
    cot_refs = refs[runs : 2 * runs]
    outs = refs[len(refs) - 2 * runs - 5 :]
    w_refs = refs[2 * runs : len(refs) - 2 * runs - 5]
    gate_ref, up_ref, hidden_ref = outs[:3]
    back_refs = outs[3 : 3 + runs]
    out_refs = outs[3 + runs : 3 + 2 * runs]
    rows_ref, cot_ref = outs[3 + 2 * runs :]
    for i in range(runs):

        @pl.when(step // each == i)
        def _():
            rows_ref[...] = rows_refs[i][...]
            cot_ref[...] = cot_refs[i][...]

    pieces = len(where[0])
    size = rows_ref.shape[1] // pieces

    def weight(p, which):
        parts = [w_refs[run[p][0]][run[p][1], which] for run in where]
        return parts[0] if len(parts) == 1 else jnp.concatenate(parts, 1)

    def columns(p):
        return pl.ds(pl.multiple_of((p ^ place_ref[0]) * size, size), size)

    def project(left_ref, which):
        total = None
        for p in range(pieces):
            part = lax.dot_general(
                left_ref[:, columns(p)], weight(p, which), (NT, ((), ())),
                preferred_element_type=f32,
            )
            total = part if total is None else total + part
        return total

    gate = project(rows_ref, 0)
    up = project(rows_ref, 1)
    grad_hidden = project(cot_ref, 2)
    sigma = sigmoid(gate)
    activ = gate * sigma
    hidden = (activ * up).astype(bf16)
    grad_gate = (grad_hidden * up * sigma * (1.0 + gate * (1.0 - sigma))).astype(bf16)
    grad_up = (grad_hidden * activ).astype(bf16)
    hidden_ref[...] = hidden
    gate_ref[...] = grad_gate
    up_ref[...] = grad_up
    for p in range(pieces):
        own = columns(p)
        back = lax.dot_general(
            grad_gate, weight(p, 0), (NN, ((), ())), preferred_element_type=f32
        )
        back = back + lax.dot_general(
            grad_up, weight(p, 1), (NN, ((), ())), preferred_element_type=f32
        )
        rows_ref[:, own] = back.astype(bf16)
        cot_ref[:, own] = lax.dot_general(
            hidden, weight(p, 2), (NN, ((), ())), preferred_element_type=f32
        ).astype(bf16)
    for i in range(runs):

        @pl.when(step // each == i)
        def _():
            back_refs[i][...] = rows_ref[...]
            out_refs[i][...] = cot_ref[...]


FFN_TILE = 256


def ffn_both(place, rows, cot, weights, where):
    runs = len(rows)
    count, d = rows[0].shape
    each = count // FFN_TILE
    total = runs * count
    hidden = weights[0].shape[2]

    def run_tile(i):
        return pl.BlockSpec(
            (FFN_TILE, d), lambda c, place: (jnp.clip(c - i * each, 0, each - 1), 0)
        )

    tiles = [run_tile(i) for i in range(runs)]
    wide = pl.BlockSpec((FFN_TILE, hidden), lambda c, place: (c, 0))
    full = pl.BlockSpec(weights[0].shape, lambda c, place: (0, 0, 0, 0))
    gate, up, hidden_out, *out = pl.pallas_call(
        functools.partial(ffn_body, where, runs),
        grid_spec=pltpu.PrefetchScalarGridSpec(
            num_scalar_prefetch=1,
            grid=(runs * each,),
            in_specs=tiles + tiles + [full] * len(weights),
            out_specs=[wide] * 3 + tiles + tiles,
            scratch_shapes=[pltpu.VMEM((FFN_TILE, d), bf16)] * 2,
        ),
        out_shape=[jax.ShapeDtypeStruct((total, hidden), bf16)] * 3
        + [jax.ShapeDtypeStruct((count, d), bf16)] * (2 * runs),
        compiler_params=pltpu.CompilerParams(
            dimension_semantics=("arbitrary",), vmem_limit_bytes=BUDGET
        ),
        cost_estimate=pl.CostEstimate(
            flops=24 * total * d * hidden, bytes_accessed=8 * total * d, transcendentals=0
        ),
        name="ffn_both",
    )(place.reshape(1), *rows, *cot, *weights)
    return gate, up, hidden_out, out[:runs], out[runs:]


def ffn_grads_body(runs, place_ref, *refs):
    rows_refs = refs[:runs]
    cot_refs = refs[runs : 2 * runs]
    gate_ref, up_ref, hidden_ref = refs[2 * runs : 2 * runs + 3]
    out_refs = refs[2 * runs + 3 : -1]
    flipped_ref = refs[-1]

    @pl.when(pl.program_id(0) == 0)
    def _():
        for i, ref in enumerate((gate_ref, up_ref, hidden_ref)):
            flipped_ref[i] = ref[...].T

    rows = jnp.concatenate([ref[...] for ref in rows_refs], 0)
    cot = jnp.concatenate([ref[...] for ref in cot_refs], 0)
    lanes = rows.shape[1] // len(out_refs)
    for i, right in enumerate((rows, rows, cot)):
        grad = lax.dot_general(
            flipped_ref[i], right, (NN, ((), ())), preferred_element_type=f32
        ).astype(bf16)
        for j, out_ref in enumerate(out_refs):
            out_ref[0, i] = grad[:, j * lanes : (j + 1) * lanes]


def ffn_weight_grads(place, rows, cot, gate, up, hidden, pieces, split):
    runs = len(rows)
    count, d = rows[0].shape
    total = runs * count
    width = hidden.shape[1]
    size = d // pieces
    column = pl.BlockSpec((count, size), lambda p, place: (0, p ^ place[0]))
    full = pl.BlockSpec((total, width), lambda p, place: (0, 0))
    return pl.pallas_call(
        functools.partial(ffn_grads_body, runs),
        grid_spec=pltpu.PrefetchScalarGridSpec(
            num_scalar_prefetch=1,
            grid=(pieces,),
            in_specs=[column] * (2 * runs) + [full] * 3,
            out_specs=[
                pl.BlockSpec((1, 3, width, size // split), lambda p, place: (p, 0, 0, 0))
            ] * split,
            scratch_shapes=[pltpu.VMEM((3, width, total), bf16)],
        ),
        out_shape=[jax.ShapeDtypeStruct((pieces, 3, width, size // split), bf16)] * split,
        compiler_params=pltpu.CompilerParams(
            dimension_semantics=("arbitrary",), vmem_limit_bytes=BUDGET
        ),
        cost_estimate=pl.CostEstimate(
            flops=12 * total * d * width, bytes_accessed=8 * total * d, transcendentals=0
        ),
        name="ffn_weight_grads",
    )(place.reshape(1), *rows, *cot, gate, up, hidden)


def norm_factor(values):
    return lax.rsqrt(jnp.mean(values * values, -1, keepdims=True) + 1e-06)


def norm_backward(grad_out, scaled, factor, gain):
    grad_scaled = grad_out * gain
    grad_input = factor * (grad_scaled - scaled * jnp.mean(grad_scaled * scaled, -1, keepdims=True))
    return (grad_input, jnp.sum(grad_out * scaled, 0))


def product(left, right, dims):
    return lax.dot_general(left, right, (dims, ((), ())), preferred_element_type=f32)


def after(x, done):
    return lax.optimization_barrier((x, done))[0]


def exchange(x, axis, bit):
    return lax.ppermute(x, axis, [(i, i ^ bit) for i in range(lax.axis_size(axis))])


def sum_over(x, axis):
    ways = lax.axis_size(axis)
    if ways & (ways - 1):
        return lax.psum(x, axis)
    bit = 1
    while bit < ways:
        x = x + exchange(x, axis, bit)
        bit *= 2
    return x


def line_gather(x, axis, more=()):
    ways = lax.axis_size(axis)
    here = lax.axis_index(axis)
    up = [(i, i + 1) for i in range(ways - 1)]
    down = [(i + 1, i) for i in range(ways - 1)]
    below = [x]
    above = [x]
    for _ in range(ways - 1):
        below.append(lax.ppermute(below[-1], axis, up))
        above.append(lax.ppermute(above[-1], axis, down))
    below, above, more = lax.optimization_barrier((below, above, more))
    blocks = []
    for slot in range(ways):
        block = x
        for at in range(ways):
            if at != slot:
                block = jnp.where(here == at, below[at - slot] if at > slot else above[slot - at], block)
        blocks.append(block)
    return jnp.concatenate(blocks, 0), more


def line_scatter(x, axis, beside=None):
    ways = lax.axis_size(axis)
    here = lax.axis_index(axis)
    size = x.shape[0] // ways
    up = [(i, i + 1) for i in range(ways - 1)]
    down = [(i + 1, i) for i in range(ways - 1)]

    def block(slot):
        return lax.dynamic_slice_in_dim(x, slot * size, size, 0).astype(f32)

    low = None
    high = None
    other = None
    for k in range(1, ways):
        to_low = block(jnp.maximum(here - (ways - k), 0))
        to_high = block(jnp.minimum(here + (ways - k), ways - 1))
        if low is not None:
            to_low = to_low + low
            to_high = to_high + high
        low = lax.ppermute(to_low.astype(bf16), axis, down)
        high = lax.ppermute(to_high.astype(bf16), axis, up)
        if beside is not None:
            other = beside(k, other)
        low, high, other = lax.optimization_barrier((low, high, other))
        low = low.astype(f32)
        high = high.astype(f32)
    return block(here) + low + high, other


def shifted(x, axis, by):
    ways = lax.axis_size(axis)
    return lax.ppermute(x, axis, [(i, (i + by) % ways) for i in range(ways)])


def ordered(parts, axis):
    ways = len(parts)
    here = lax.axis_index(axis)
    blocks = []
    for slot in range(ways):
        block = parts[0]
        for at in range(ways):
            if at != slot:
                block = jnp.where(here == at, parts[(at - slot) % ways], block)
        blocks.append(block)
    return blocks


def swap_parts(block_to, axis):
    ways = lax.axis_size(axis)
    here = lax.axis_index(axis)
    parts = [block_to(here)]
    for s in range(1, ways):
        parts.append(shifted(block_to((here + s) % ways), axis, s))
    return parts


def swap_blocks(block_to, axis):
    return ordered(swap_parts(block_to, axis), axis)


class PlaneSum:

    def __init__(self, left, right):
        self.ways = lax.axis_size("dp")
        self.parts = ()
        if self.ways != 8:
            self.came = ()
            grad = product(left, right, TN).astype(bf16)
            self.total = lax.psum_scatter(grad, "dp", scatter_dimension=0, tiled=True).astype(f32)
            return
        core = lax.axis_index("dp") % 2
        self.size = left.shape[1] // self.ways
        blocks = [left[:, i * self.size : (i + 1) * self.size] for i in range(self.ways)]
        even = jnp.concatenate(blocks[::2], 1)
        odd = jnp.concatenate(blocks[1::2], 1)
        self.stay = jnp.where(core == 0, even, odd)
        self.right = right
        self.came = exchange(
            product(jnp.where(core == 0, odd, even), right, TN).astype(bf16), "dp", 1
        )

    def send(self):
        if self.ways == 8:
            total = product(self.stay, self.right, TN) + self.came.astype(f32)
            total = total.astype(bf16)
            place = lax.axis_index("dp") // 2
            block = lambda i: lax.dynamic_slice_in_dim(total, i * self.size, self.size, 0)
            self.total = block(place)
            self.parts = [exchange(block(place ^ (m // 2)), "dp", m) for m in (2, 4, 6)]

    def finish(self):
        total = self.total.astype(f32)
        for part in self.parts:
            total = total + part.astype(f32)
        return total


class OutWeights:

    def __init__(self, mixer_out):
        rows = mixer_out.T
        self.ways = lax.axis_size("dp")
        self.parts = ()
        self.rows = jnp.concatenate(swap_blocks(lambda i: rows, "tensor"), 1)

    def start(self, started):
        if self.ways == 8:
            rows = after(self.rows, started)
            self.parts = {m: exchange(rows, "dp", m) for m in (2, 4, 6)}

    def finish(self, done):
        if self.ways != 8:
            return lax.all_gather(self.rows, "dp", axis=0, tiled=True)
        here = lax.axis_index("dp")
        parts = dict(zip((2, 4, 6), after([self.parts[m] for m in (2, 4, 6)], done)))
        parts[0] = self.rows
        size = self.rows.shape[0]
        out = jnp.zeros((self.ways * size, self.rows.shape[1]), bf16)
        for m in (0, 2, 4, 6):
            parts[m + 1] = exchange(parts[m], "dp", 1)
        for m, part in parts.items():
            out = lax.dynamic_update_slice_in_dim(out, part, (here ^ m) * size, 0)
        return out

    def send_sum(self, total, width):
        return swap_parts(
            lambda i: lax.dynamic_slice_in_dim(total, i * width, width, 1), "tensor"
        )


class LineFfn:

    def __init__(self, ffn_in, ffn_out, started):
        self.own = jnp.stack([ffn_in[0].T, ffn_in[1].T, ffn_out])
        self.place = jnp.zeros((), jnp.int32)
        self.near = self.far = ()

    def middle(self, done, more):
        return done, more

    def plane_step(self):
        pass

    def finish(self, done):
        weights = lax.all_gather(self.own, "dp", axis=2, tiled=True)
        return (weights[None],)

    pieces = 1
    where = (((0, 0),),)

    def reach(self, x):
        return line_gather(x, "tensor")[0]

    def beside(self, x):
        return ()

    def gather(self, x, near, far):
        return [far]

    def halves(self, x):
        return line_scatter(x[0], "tensor")[0], jnp.zeros((), bf16)

    def cross(self, far):
        return far

    def sum_start(self, grads):
        self.grads = grads

    def sum_step(self, done):
        return ()

    def sum_far(self, sent):
        pass

    def sum_finish(self):
        return lax.psum_scatter(self.grads[0][0], "dp", scatter_dimension=2, tiled=True)

    def send_sums(self, grads):
        return grads

    def own_grads(self, grads, came):
        return came.astype(f32)


TO_A = [(1, 0), (0, 2), (2, 3), (3, 1)]
TO_B = [(2, 1), (1, 2)]
BACK_A = [(0, 1), (2, 0), (3, 2), (1, 3)]
BACK_B = [(2, 1), (1, 2)]


class PairFfn:

    def __init__(self, ffn_in, ffn_out, started):
        self.core = lax.axis_index("dp") % 2
        self.here = lax.axis_index("tensor")
        self.place = lax.axis_index("dp") // 2
        self.own = after(jnp.stack([ffn_in[0].T, ffn_in[1].T, ffn_out]), started)
        self.a = lax.ppermute(self.own, "tensor", TO_A)
        self.b = lax.ppermute(self.own, "tensor", TO_B)

    def middle(self, done, more):
        here = self.here
        self.own, self.a, self.b, done, more = lax.optimization_barrier(
            (self.own, self.a, self.b, done, more)
        )
        own, a, b = self.own, self.a, self.b
        first = jnp.where(here == 0, own, jnp.where(here == 1, b, a))
        second = jnp.where(here == 3, own, jnp.where(here == 2, b, a))
        mine = jnp.where(self.core == 0, first, second)
        got = exchange(jnp.where(self.core == 0, second, first), "dp", 1)
        self.low = jnp.where(self.core == 0, mine, got)
        self.high = jnp.where(self.core == 0, got, mine)
        done = after(done, (self.low, self.high))
        self.near = exchange(self.low, "dp", 2), exchange(self.high, "dp", 4)
        return done, more

    def plane_step(self):
        self.low = jnp.stack([self.low, self.near[0]])
        self.high = jnp.stack([self.high, self.near[1]])
        self.far = exchange(self.low, "dp", 4), exchange(self.high, "dp", 2)

    def finish(self, done):
        far = after(self.far, done)
        return (self.low, far[0], self.high, far[1])

    pieces = 4
    where = (((0, 0), (0, 1), (1, 0), (1, 1)), ((2, 0), (3, 0), (2, 1), (3, 1)))

    def reach(self, x):
        return exchange(x, "tensor", 1)

    def beside(self, x):
        return exchange(x, "dp", 1)

    def gather(self, x, near, far):
        return [x, near, far, exchange(far, "dp", 1)]

    def halves(self, x):
        far = (x[2].astype(f32) + exchange(x[3], "dp", 1).astype(f32)).astype(bf16)
        return x[0].astype(f32) + exchange(x[1], "dp", 1).astype(f32), far

    def cross(self, far):
        return exchange(far, "tensor", 1)

    def sum_start(self, grads):
        self.grads = grads
        low, high = grads
        across_x = jnp.stack([low[1], low[3]])
        self.near = exchange(across_x, "dp", 2), exchange(high[2:], "dp", 4)

    def sum_step(self, done):
        low, high = self.grads
        came = after(self.near, done)
        add = lambda x, y: (x.astype(f32) + y.astype(f32)).astype(bf16)
        self.kept = add(low[0], came[0][0]), add(high[0], came[1][0])
        return add(low[2], came[0][1]), add(high[1], came[1][1])

    def sum_far(self, sent):
        self.far = exchange(sent[0], "dp", 4), exchange(sent[1], "dp", 2)

    def sum_finish(self):
        came = self.far
        add = lambda x, y: (x.astype(f32) + y.astype(f32)).astype(bf16)
        low = add(self.kept[0], came[0])
        high = add(self.kept[1], came[1])
        core = self.core
        mine = jnp.where(core == 0, low, high)
        got = exchange(jnp.where(core == 0, high, low), "dp", 1)
        return jnp.where(core == 0, mine, got), jnp.where(core == 0, got, mine)

    def send_sums(self, sums):
        first, second = sums
        here = self.here
        a = lax.ppermute(jnp.where(here < 2, second, first), "tensor", BACK_A)
        b = lax.ppermute(jnp.where(here == 2, second, first), "tensor", BACK_B)
        return a, b

    def own_grads(self, sums, came):
        first, second = sums
        a, b = came
        here = self.here
        other = jnp.where(here == 0, first, jnp.where(here == 3, second, b))
        return a.astype(f32) + other.astype(f32)


CONV_AT = 64


def column_blocks(value, rows):
    ways, size = value.shape
    lanes = -(-size // rows)
    value = jnp.pad(value, ((0, 0), (0, lanes * rows - size)))
    return value.reshape(ways, lanes, rows).swapaxes(1, 2).reshape(ways * rows, lanes)


def from_columns(columns, shape, dim, rows):
    ways = columns.shape[0] // rows
    size = 1
    for extent in shape:
        size *= extent
    value = columns.reshape(ways, rows, -1).swapaxes(1, 2).reshape(ways, -1)[:, :size]
    value = jnp.moveaxis(value.reshape((ways,) + shape), 0, dim)
    return value.reshape(shape[:dim] + (ways * shape[dim],) + shape[dim + 1 :])


def lanes_of(small, conv, onorm):
    rows, width = small.shape
    used = BETA_AT + width
    rest = LANES - CONV_AT - conv.shape[1] - onorm.shape[1]
    zeros = lambda lanes: jnp.zeros((rows, lanes), small.dtype)
    return jnp.concatenate(
        [zeros(BETA_AT), small, zeros(CONV_AT - used), conv, onorm, zeros(rest)], 1
    )


def fetch_mixer(mixer_in, mixer_small, conv_weight, out_norm):
    rows, width = mixer_in.shape
    small = jnp.moveaxis(mixer_small, 0, 1).reshape(rows, -1)
    conv = column_blocks(conv_weight.reshape(1, -1), rows)
    onorm = column_blocks(out_norm.reshape(1, -1), rows)
    extended = jnp.concatenate([mixer_in, lanes_of(small, conv, onorm)], 1)
    w_in = lax.all_gather(extended, "dp", axis=0, tiled=True)
    at = width + CONV_AT
    w_conv = from_columns(w_in[:, at : at + conv.shape[1]], conv_weight.shape, 2, rows)
    at += conv.shape[1]
    w_onorm = from_columns(w_in[:, at : at + onorm.shape[1]], out_norm.shape, 1, rows)
    return w_in, w_conv, w_onorm


def shards(
    tokens, cotangent, segments, norm_gains, mixer_in, mixer_small, conv_weight, head_params,
    out_norm, mixer_out, ffn_in, ffn_out,
):
    heads = mixer_in.shape[1] // MIX
    all_heads = head_params.shape[1]
    ways = lax.axis_size("dp")
    teams = lax.axis_size("tensor")
    head_start = lax.axis_index("tensor") * heads
    head_local = lax.dynamic_slice_in_dim(head_params, head_start, heads, 1)
    gains = norm_gains.astype(f32)
    own = tokens.shape[0]
    inputs = tokens.astype(f32)
    factor_one = norm_factor(inputs)
    scaled_one = inputs * factor_one
    normed_one = (scaled_one * gains[0]).astype(bf16)
    out_weights = OutWeights(mixer_out)
    w_in, w_conv, w_onorm = fetch_mixer(mixer_in, mixer_small, conv_weight, out_norm)
    conv_rows = w_conv.astype(f32).reshape(TAPS, heads * CONV)
    onorm_row = w_onorm.astype(f32).reshape(1, heads * DV)
    head_rows = head_lanes(head_local)
    places = token_places(segments)
    kind = PairFfn if teams == 4 and ways == 8 else LineFfn
    rows_one, (out_weights.rows, constants, places, cot_near) = line_gather(
        normed_one,
        "tensor",
        (
            out_weights.rows, (conv_rows, head_rows, onorm_row), places,
            kind.beside(None, cotangent),
        ),
    )
    out_weights.start(rows_one)
    ffn = kind(ffn_in, ffn_out, rows_one)
    wide = heads * MIX
    proj = product(rows_one, w_in, NN)
    carry = forward_start(heads)
    made = []
    for part in range(PARTS):
        made, carry = mixer_forward(part, made, places, proj, *constants, carry, heads)
        if part == 0:
            carry, (cotangent, out_weights.parts) = ffn.middle(
                carry, (cotangent, out_weights.parts)
            )
            cot_far = ffn.reach(cotangent)
    mixed, *kept = made
    mixed, cot_far, ffn.near = lax.optimization_barrier((mixed, cot_far, ffn.near))
    ffn.plane_step()
    came = swap_parts(lambda i: lax.dynamic_slice_in_dim(mixed, i * own, own, 0), "tensor")
    out_t = out_weights.finish(came[-1])
    grad_rows = ffn.gather(cotangent, cot_near, after(cot_far, came[-1]))
    mixed = jnp.concatenate(ordered(came, "tensor"), 1)
    middle = inputs + product(mixed, out_t, NT)
    factor_two = norm_factor(middle)
    scaled_two = middle * factor_two
    normed_two = (scaled_two * gains[1]).astype(bf16)
    rows_two = ffn.gather(normed_two, ffn.beside(normed_two), ffn.reach(normed_two))
    w_ffn = ffn.finish(normed_two)
    grad_gate, grad_up, hidden, back, forth = ffn_both(
        ffn.place, rows_two, grad_rows, w_ffn, ffn.where
    )
    grad_normed_two, far = ffn.halves(back)
    ffn_grads = ffn_weight_grads(
        ffn.place, after(rows_two, far), grad_rows, grad_gate, grad_up, hidden,
        ffn.pieces, len(ffn.where),
    )
    far, ffn_grads = lax.optimization_barrier((ffn.cross(far), ffn_grads))
    grad_normed_two = grad_normed_two + far.astype(f32)
    ffn.sum_start(ffn_grads)
    grad_middle_norm, grad_gain_two = norm_backward(
        grad_normed_two, scaled_two, factor_two, gains[1]
    )
    grad_middle = cotangent.astype(f32) + grad_middle_norm
    branch_grad = grad_middle.astype(bf16)
    grad_mixed = product(branch_grad, out_t, NN).astype(bf16)
    width = heads * DV
    came = swap_parts(
        lambda i: lax.dynamic_slice_in_dim(grad_mixed, i * width, width, 1), "tensor"
    )
    branch_grad, forth, near = after((branch_grad, forth, ffn.near), grad_mixed)
    ffn.near = near
    out_sum = PlaneSum(branch_grad, mixed)
    result, far = ffn.halves(forth)
    came, far, sums = lax.optimization_barrier((came, far, ffn.sum_step(grad_mixed)))
    ffn.sum_far(sums)
    result = result, ffn.cross(far)
    grad_mixed = jnp.concatenate(ordered(came, "tensor"), 0)
    carry = backward_start(heads)
    grad_proj = []
    for part in reversed(range(PARTS)):
        dproj, carry = mixer_backward(
            part, grad_proj, places, proj, *constants, kept, grad_mixed, carry, heads
        )
        grad_proj = [dproj]
        if part == PARTS - 1:
            carry, result, ffn.far, out_sum.came = lax.optimization_barrier(
                (carry, result, ffn.far, out_sum.came)
            )
            out_sum.send()
            ffn_sums = ffn.sum_finish()
            carry = after(carry, ffn_sums)
            ffn_came = ffn.send_sums(ffn_sums)
    grad_proj, ffn_came, out_sum.parts = lax.optimization_barrier(
        (dproj, ffn_came, out_sum.parts)
    )
    grad_conv, grad_head, grad_onorm = carry[2:]
    result = middle + result[0] + result[1].astype(f32)
    sent = product(grad_proj, w_in, NT).astype(bf16)
    grad_normed_one = lax.psum_scatter(
        sent, "tensor", scatter_dimension=0, tiled=True
    ).astype(f32)
    grad_proj, again = after((grad_proj, sent), sent)
    grad_in = PlaneSum(rows_one, grad_proj[:, :wide])
    head_full = lax.dynamic_update_slice_in_dim(
        jnp.zeros((2, all_heads), f32),
        grad_head[:2, BETA_AT + heads : BETA_AT + 2 * heads],
        head_start,
        1,
    )
    d = gains.shape[1]
    sizes = [2 * d + 2 * all_heads, grad_conv.size, grad_onorm.size, 2 * heads * d]
    ends = [sum(sizes[:i]) for i in range(5)]
    at = BETA_AT + 2 * heads
    grad_small = product(rows_one, grad_proj[:, wide:], TN)[:, BETA_AT:at]
    gain_one = jnp.sum(again.astype(f32) * rows_one.astype(f32), 0) / gains[0]
    parts = [
        gain_one, grad_gain_two, head_full.reshape(-1), grad_conv.reshape(-1),
        grad_onorm.reshape(-1), grad_small.T.reshape(-1),
    ]
    totals, grad_in.came = lax.optimization_barrier(
        (sum_over(jnp.concatenate(parts), "dp"), grad_in.came)
    )
    grad_in.send()
    shared = after(totals[: sizes[0]], grad_in.parts)
    shared = sum(ordered(swap_parts(lambda i: shared, "tensor"), "tensor"))
    out_parts = after(out_sum.finish().astype(bf16), grad_in.total)
    out_out = sum(block.astype(f32) for block in out_weights.send_sum(out_parts, width))
    conv_total, onorm_total, small_total = (totals[ends[i] : ends[i + 1]] for i in (1, 2, 3))
    place = lax.axis_index("dp")

    def own_part(total, shape):
        size = shape[-1] // ways
        return lax.dynamic_slice_in_dim(total.reshape(shape), place * size, size, len(shape) - 1)

    out_conv = own_part(conv_total, (TAPS, heads, CONV))
    out_onorm = own_part(onorm_total, (heads, DV))
    out_small = own_part(small_total, (2, heads, d)).swapaxes(1, 2)
    totals = shared
    out_in = grad_in.finish()
    ffn_grads = ffn.own_grads(ffn_sums, ffn_came)
    grad_scaled = grad_normed_one * gains[0]
    grad_tokens = grad_middle + factor_one * (
        grad_scaled - scaled_one * jnp.mean(grad_scaled * scaled_one, -1, keepdims=True)
    )
    return (
        result.astype(bf16),
        grad_tokens,
        totals[: 2 * d].reshape(2, d),
        out_in,
        out_small,
        out_conv,
        totals[2 * d :].reshape(2, all_heads),
        out_onorm,
        out_out.T,
        ffn_grads[:2].swapaxes(1, 2),
        ffn_grads[2],
    )


def solution(mesh):
    in_specs = (
        P(("dp", "tensor"), None),
        P(("dp", "tensor"), None),
        P("dp", None),
        P(),
        P("dp", "tensor"),
        P(None, "dp", "tensor"),
        P(None, "tensor", "dp"),
        P(),
        P("tensor", "dp"),
        P("tensor", "dp"),
        P(None, "dp", "tensor"),
        P("tensor", "dp"),
    )
    out_specs = (
        P(("dp", "tensor"), None),
        P(("dp", "tensor"), None),
        P(),
        P("dp", "tensor"),
        P(None, "dp", "tensor"),
        P(None, "tensor", "dp"),
        P(),
        P("tensor", "dp"),
        P("tensor", "dp"),
        P(None, "dp", "tensor"),
        P("tensor", "dp"),
    )
    return jax.shard_map(shards, mesh=mesh, in_specs=in_specs, out_specs=out_specs, check_vma=False)
```

```python
import functools
import jax
import jax.numpy as jnp
from jax import lax
from jax.experimental import pallas as pl
from jax.experimental.pallas import tpu as pltpu
from jax.sharding import PartitionSpec as P

DK = 128
DV = 256
MIX = 2 * DK + 2 * DV
CONV = 2 * DK + DV
CHUNK = 128
LANES = 128
TAPS = 4
BASE = 16
PER = 2
BACK = 2
PARTS = 2
BETA_AT = 8

NN = ((1,), (0,))
NT = ((1,), (1,))
TN = ((0,), (0,))

f32 = jnp.float32
bf16 = jnp.bfloat16


def dot(a, b, dims, passes, join=False):
    if passes == 6:
        return lax.dot_general(
            a, b, (dims, ((), ())), precision=lax.Precision.HIGHEST, preferred_element_type=f32
        )
    a_hi = a.astype(bf16)
    b_hi = b.astype(bf16)
    product = lambda x, y: lax.dot_general(x, y, (dims, ((), ())), preferred_element_type=f32)
    if passes == 1:
        return product(a_hi, b_hi)
    a_lo = (a - a_hi.astype(f32)).astype(bf16)
    b_lo = (b - b_hi.astype(f32)).astype(bf16)
    (a_dim,), (b_dim,) = dims
    if not join:
        return product(a_hi, b_hi) + product(a_hi, b_lo) + product(a_lo, b_hi)
    both = product(
        jnp.concatenate([a_hi, a_lo], a_dim), jnp.concatenate([b_hi, b_hi], b_dim)
    )
    return both + product(a_hi, b_lo)


def exact_left(mask, b):
    hi = b.astype(bf16)
    rest = b - hi.astype(f32)
    mid = rest.astype(bf16)
    low = (rest - mid.astype(f32)).astype(bf16)
    out = lax.dot_general(mask, hi, (NN, ((), ())), preferred_element_type=f32)
    out = out + lax.dot_general(mask, mid, (NN, ((), ())), preferred_element_type=f32)
    return out + lax.dot_general(mask, low, (NN, ((), ())), preferred_element_type=f32)


def sigmoid(x):
    return 1.0 / (1.0 + jnp.exp(-x))


def log1p(y):
    return jnp.where(y < 1e-4, y - 0.5 * y * y, jnp.log(1.0 + y))


def softplus(x):
    return jnp.maximum(x, 0.0) + log1p(jnp.exp(-jnp.abs(x)))


def iotas():
    shape = (CHUNK, CHUNK)
    return lax.broadcasted_iota(jnp.int32, shape, 0), lax.broadcasted_iota(jnp.int32, shape, 1)


def token_scalars(info, head_rows, heads):
    row, col = iotas()
    beta = sigmoid(info)
    rate = -jnp.exp(head_rows[0:1])
    pre = info + head_rows[1:2]
    g = rate * softplus(pre)
    total = exact_left((row >= col).astype(bf16), g)
    lane = lax.broadcasted_iota(jnp.int32, (CHUNK, LANES), 1)
    across = jnp.where(lane < BETA_AT, info, total).T
    return beta, g, pre, total, across


def head_scalars(h, heads, info, beta, total, across):
    row, col = iotas()
    at = BETA_AT + heads + h
    seg_col = info[:, 0:1]
    seg_row = across[0:1, :]
    tot_col = total[:, at : at + 1]
    tot_row = across[at : at + 1, :]
    keep = (seg_col == seg_row) & (row >= col)
    decay = jnp.exp(jnp.where(keep, tot_col - tot_row, -1e30))
    strict = jnp.where(row > col, decay, 0.0)
    beta_col = beta[:, BETA_AT + h : BETA_AT + h + 1]
    carried = jnp.exp(tot_col) * info[:, 7:8]
    last = CHUNK - 1
    end = jnp.where(
        seg_col == seg_col[last : last + 1], jnp.exp(tot_col[last : last + 1] - tot_col), 0.0
    )
    carried_last = carried[last : last + 1]
    return decay, strict, beta_col, carried, end, carried_last


def invert(lowers, passes):
    row, col = iotas()
    shape = (BASE, CHUNK)
    lane = lax.broadcasted_iota(jnp.int32, shape, 1)
    own = lax.broadcasted_iota(jnp.int32, shape, 0)
    start = lane // BASE * BASE
    blocks = CHUNK // BASE
    inside = [lane // BASE == b for b in range(blocks)]
    packs = []
    for lower in lowers:
        packed = jnp.zeros(shape, f32)
        for b in range(blocks):
            packed = jnp.where(inside[b], lower[b * BASE : (b + 1) * BASE], packed)
        packs.append(packed)
    invs = [jnp.where(own == lane % BASE, 1.0, 0.0)] * len(lowers)
    for j in range(BASE - 1):
        at = start + j
        invs = [
            inv - jnp.take_along_axis(packed, at, axis=1) * inv[j : j + 1]
            for inv, packed in zip(invs, packs)
        ]
    invs = [
        jnp.concatenate([jnp.where(inside[b], inv, 0.0) for b in range(blocks)], 0) for inv in invs
    ]
    size = BASE
    while size < CHUNK:
        part = ((row // (2 * size)) == (col // (2 * size))) & ((row // size) != (col // size))
        steps = [
            dot(jnp.where(part, lower, 0.0), inv, NN, passes, True) for lower, inv in zip(lowers, invs)
        ]
        invs = [inv - dot(inv, step, NN, passes, True) for inv, step in zip(invs, steps)]
        size *= 2
    return invs


def normalised(act):
    factor = lax.rsqrt(jnp.sum(act * act, -1, keepdims=True) + 1e-06)
    return act * factor, factor


def with_scalars(places, extra, heads):
    lane = lax.broadcasted_iota(jnp.int32, places.shape, 1)
    return jnp.where((lane >= BETA_AT) & (lane < BETA_AT + 2 * heads), extra, places)


def forward_body(
    heads, prec, places_ref, extra_ref, proj_ref, conv_ref, head_ref, onorm_ref, state_in_ref,
    tail_in_ref,
    *refs,
):
    (
        z_ref, mixed_ref, out_ref, delta_ref, across_ref, state_out_ref, solve_ref, kk_ref, qk_ref,
        state_ref, tail_ref,
    ) = refs[-11:]

    @pl.when(pl.program_id(0) == 0)
    def _():
        state_ref[...] = state_in_ref[...]
        tail_ref[...] = tail_in_ref[...]

    rows = PER * CHUNK
    ready = {}
    first = {}
    infos = [
        with_scalars(
            places_ref[u * CHUNK : (u + 1) * CHUNK],
            extra_ref[u * CHUNK : (u + 1) * CHUNK],
            heads,
        )
        for u in range(PER)
    ]
    scalars = [token_scalars(info, head_ref[...], heads) for info in infos]
    for h in range(heads):
        at = h * MIX
        cat = h * CONV
        part = proj_ref[:, at : at + CONV]
        ext = jnp.concatenate([tail_ref[:, cat : cat + CONV], part], 0)
        tail_ref[:, cat : cat + CONV] = part[rows - 8 :]
        mixed = conv_ref[TAPS - 1 : TAPS, cat : cat + CONV] * part
        for s in range(1, TAPS):
            shifted = ext[8 - s : 8 - s + rows]
            mixed = mixed + conv_ref[TAPS - 1 - s : TAPS - s, cat : cat + CONV] * jnp.where(
                places_ref[:, s : s + 1] > 0.5, shifted, 0.0
            )
        mixed_ref[:, cat : cat + CONV] = mixed
        act = mixed * sigmoid(mixed)
        queries, _ = normalised(act[:, :DK])
        queries = queries * DK ** (-0.5)
        keys, _ = normalised(act[:, DK : 2 * DK])
        for u in range(PER):
            own = slice(u * CHUNK, (u + 1) * CHUNK)
            query = queries[own]
            key = keys[own]
            value = act[own, 2 * DK :]
            beta, g, pre, total, across = scalars[u]
            decay, strict, beta_col, carried, end, carried_last = head_scalars(
                h, heads, infos[u], beta, total, across
            )
            inner = dot(jnp.concatenate([key, query], 0), key, NT, prec["kk"], True)
            kk = inner[:CHUNK]
            qk = inner[CHUNK:]
            kk_ref[u, h] = kk
            qk_ref[u, h] = qk
            first[u, h] = (
                beta_col * strict * kk,
                jnp.concatenate([beta_col * value, (beta_col * carried) * key], 1),
                carried * query, decay * qk, end * key, carried_last,
            )
    order = list(first)
    for at, inv in zip(order, invert([first[at][0] for at in order], prec["inv"])):
        u, h = at
        own = slice(u * CHUNK, (u + 1) * CHUNK)
        lower, sides, reads_q, attend, ends, carried_last = first[at]
        solve_ref[u, h] = inv
        solved = dot(inv, sides, NN, prec["solve"], True)
        across_ref[own, h * DK : (h + 1) * DK] = solved[:, DV:]
        ready[at] = (
            jnp.concatenate([reads_q, solved[:, DV:]], 0), solved[:, :DV], attend, ends,
            carried_last,
        )
    for u in range(PER):
        own = slice(u * CHUNK, (u + 1) * CHUNK)
        for h in range(heads):
            readers, fixed, attend, ends, carried_last = ready[u, h]
            state = state_ref[h]
            state_out_ref[u, h] = state
            reads = dot(readers, state, NN, prec["state"], True)
            delta = fixed - reads[CHUNK:]
            state_ref[h] = carried_last * state + dot(ends, delta, TN, prec["state"], True)
            result = reads[:CHUNK] + dot(attend, delta, NN, prec["attend"], True)
            delta_ref[own, h * DV : (h + 1) * DV] = delta
            out_ref[own, h * DV : (h + 1) * DV] = result
            gate = proj_ref[own, h * MIX + CONV : (h + 1) * MIX]
            factor = lax.rsqrt(jnp.mean(result * result, -1, keepdims=True) + 1e-05)
            z = result * factor * onorm_ref[:, h * DV : (h + 1) * DV] * (gate * sigmoid(gate))
            z_ref[own, h * DV : (h + 1) * DV] = z.astype(bf16)


def backward_body(
    heads, prec, places_ref, extra_ref, proj_ref, conv_ref, head_ref, onorm_ref,
    mixed_ref, out_ref, delta_ref, across_ref, state_in_ref, solve_ref, kk_ref, qk_ref, dz_ref,
    dstate_in_ref, lead_in_ref, dconv_in_ref, dhead_in_ref, donorm_in_ref,
    *refs,
):
    dproj_ref, dstate_ref, lead_ref, dconv_ref, dhead_ref, donorm_ref = refs[-6:]

    @pl.when(pl.program_id(0) == 0)
    def _():
        dstate_ref[...] = dstate_in_ref[...]
        lead_ref[...] = lead_in_ref[...]
        dconv_ref[...] = dconv_in_ref[...]
        dhead_ref[...] = dhead_in_ref[...]
        donorm_ref[...] = donorm_in_ref[...]

    row, col = iotas()
    lane = lax.broadcasted_iota(jnp.int32, (CHUNK, LANES), 1)
    from_here = (row <= col).astype(bf16)
    items = [(u, h) for u in reversed(range(BACK)) for h in range(heads)]
    rows_of = {u: slice(u * CHUNK, (u + 1) * CHUNK) for u in range(BACK)}
    infos = {
        u: with_scalars(places_ref[rows_of[u]], extra_ref[rows_of[u]], heads)
        for u in range(BACK)
    }
    scalars = {u: token_scalars(infos[u], head_ref[...], heads) for u in range(BACK)}
    made = {}
    for u, h in items:
        own = rows_of[u]
        cat = h * CONV
        at = h * MIX
        mixed = mixed_ref[own, cat : cat + CONV]
        msig = sigmoid(mixed)
        act = mixed * msig
        q_unit, q_factor = normalised(act[:, :DK])
        key, k_factor = normalised(act[:, DK : 2 * DK])
        value = act[:, 2 * DK :]
        beta, g, pre, total, across = scalars[u]
        decay, strict, beta_col, carried, end, carried_last = head_scalars(
            h, heads, infos[u], beta, total, across
        )
        result = out_ref[own, h * DV : (h + 1) * DV]
        gate = proj_ref[own, at + CONV : at + MIX]
        gsig = sigmoid(gate)
        silu = gate * gsig
        onorm = onorm_ref[:, h * DV : (h + 1) * DV]
        factor = lax.rsqrt(jnp.mean(result * result, -1, keepdims=True) + 1e-05)
        normed = result * factor
        dz = dz_ref[own, h * DV : (h + 1) * DV].astype(f32)
        dzn = dz * normed
        donorm_ref[:, h * DV : (h + 1) * DV] += jnp.sum(dzn * silu, 0, keepdims=True)
        dgate = dzn * onorm * (gsig * (1.0 + gate * (1.0 - gsig)))
        dproj_ref[own, at + CONV : at + MIX] = dgate.astype(bf16)
        dnormed = dz * onorm * silu
        dout = factor * (dnormed - normed * jnp.mean(dnormed * normed, -1, keepdims=True))
        through = dot(decay * qk_ref[u, h], dout, TN, prec["attend"])
        made[u, h] = (
            mixed, msig, q_unit, q_factor, key, k_factor, value, decay, strict, beta_col, carried,
            end, carried_last, dout, through,
        )
    chain = {}
    for u, h in items:
        own = rows_of[u]
        q_unit, key, carried, end, carried_last, dout, through = (
            made[u, h][i] for i in (2, 4, 10, 11, 12, 13, 14)
        )
        dnext = dstate_ref[h]
        ddelta = through + dot(end * key, dnext, NN, prec["state"])
        dstate_ref[h] = carried_last * dnext + dot(
            jnp.concatenate(
                [carried * (q_unit * DK ** (-0.5)), -across_ref[own, h * DK : (h + 1) * DK]], 0
            ),
            jnp.concatenate([dout, ddelta], 0),
            TN,
            prec["state"],
        )
        chain[u, h] = (dnext, ddelta)
    solved = {}
    for u, h in items:
        own = rows_of[u]
        dnext, ddelta = chain[u, h]
        delta = delta_ref[own, h * DV : (h + 1) * DV]
        state = state_in_ref[u, h]
        x = dot(solve_ref[u, h], ddelta, TN, prec["solve"])
        dend = dot(delta, dnext, NT, prec["big"])
        dcl = jnp.sum(jnp.sum(state * dnext, 0, keepdims=True), 1, keepdims=True)
        big = dot(
            jnp.concatenate([made[u, h][13], x], 0),
            jnp.concatenate([state, delta], 0),
            NT,
            prec["big"],
        )
        solved[u, h] = (x, dend, dcl, big)
    inner = {}
    for u, h in items:
        q_unit, key, decay, strict, beta_col = (made[u, h][i] for i in (2, 4, 7, 8, 9))
        x, dend, dcl, big = solved[u, h]
        query = q_unit * DK ** (-0.5)
        dqk = decay * big[:CHUNK, DK:]
        das = -strict * big[CHUNK:, DK:]
        bdas = beta_col * das
        rows = dot(jnp.concatenate([dqk, das], 0), key, NN, prec["kk"])
        cols = dot(
            jnp.concatenate([dqk, bdas], 0),
            jnp.concatenate([query, key], 0),
            TN,
            prec["kk"],
        )
        pairs = jnp.where(row > col, dqk * qk_ref[u, h] + bdas * kk_ref[u, h], 0.0)
        inner[u, h] = (rows, cols, exact_left(from_here, pairs))
    sums = {
        u: [jnp.zeros((CHUNK, LANES), f32) for _ in range(4)] for u in range(BACK)
    }
    dacts = {}
    for u, h in items:
        (
            mixed, msig, q_unit, q_factor, key, k_factor, value, decay, strict, beta_col, carried,
            end, carried_last, dout, through,
        ) = made[u, h]
        x, dend, dcl, big = solved[u, h]
        rows, cols, pairs = inner[u, h]
        query = q_unit * DK ** (-0.5)
        dqc = carried * big[:CHUNK, :DK]
        dq = rows[:CHUNK] + dqc
        dk_end = end * dend
        dkb_c = -carried * big[CHUNK:, :DK]
        dk_row_b = rows[CHUNK:] + dkb_c
        dk = beta_col * dk_row_b + cols + dk_end
        xv = x * value
        dbeta = jnp.sum(xv[:, :DK] + xv[:, DK:] + key * dk_row_b, -1, keepdims=True)
        reach = jnp.sum(query * dqc + key * (beta_col * dkb_c), -1, keepdims=True)
        leave = jnp.sum(key * dk_end, -1, keepdims=True)
        spans = jnp.sum(jnp.where(row > col, pairs, 0.0), -1, keepdims=True) + carried_last * dcl
        at_h = lane == BETA_AT + heads + h
        sums[u][0] = jnp.where(lane == BETA_AT + h, dbeta, sums[u][0])
        sums[u][1] = jnp.where(at_h, reach, sums[u][1])
        sums[u][2] = jnp.where(at_h, leave, sums[u][2])
        sums[u][3] = jnp.where(at_h, spans, sums[u][3])
        scale_q = DK ** (-0.5) * q_factor
        daq = scale_q * (dq - q_unit * jnp.sum(q_unit * dq, -1, keepdims=True))
        dak = k_factor * (dk - key * jnp.sum(key * dk, -1, keepdims=True))
        dact = jnp.concatenate([daq, dak, beta_col * x], 1)
        dacts[u, h] = dact * (msig * (1.0 + mixed * (1.0 - msig)))
    for h in range(heads):
        at = h * MIX
        cat = h * CONV
        dmixed = jnp.concatenate([dacts[u, h] for u in range(BACK)], 0)
        ext = jnp.concatenate([dmixed, lead_ref[:, cat : cat + CONV]], 0)
        lead_ref[:, cat : cat + CONV] = dmixed[:8]
        part = proj_ref[:, at : at + CONV]
        dpart = conv_ref[TAPS - 1 : TAPS, cat : cat + CONV] * dmixed
        dconv_ref[TAPS - 1 : TAPS, cat : cat + CONV] += jnp.sum(dmixed * part, 0, keepdims=True)
        for s in range(1, TAPS):
            shifted = jnp.where(
                places_ref[:, 3 + s : 4 + s] > 0.5, ext[s : s + BACK * CHUNK], 0.0
            )
            dpart = dpart + conv_ref[TAPS - 1 - s : TAPS - s, cat : cat + CONV] * shifted
            dconv_ref[TAPS - 1 - s : TAPS - s, cat : cat + CONV] += jnp.sum(
                shifted * part, 0, keepdims=True
            )
        dproj_ref[:, at : at + CONV] = dpart.astype(bf16)
    rate = -jnp.exp(head_ref[0:1])
    for u in range(BACK):
        beta, g, pre, total, across = scalars[u]
        dbeta_all, reach_all, leave_all, spans_all = sums[u]
        dg = spans_all + exact_left(from_here, reach_all)
        dg = dg + exact_left((row > col).astype(bf16), leave_all)
        dpre = dg * rate * sigmoid(pre)
        dsmall = dbeta_all * beta * (1.0 - beta) + dpre
        dproj_ref[rows_of[u], heads * MIX :] = dsmall.astype(bf16)
        dhead_ref[0:1] += jnp.sum(dg * g, 0, keepdims=True)
        dhead_ref[1:2] += jnp.sum(dpre, 0, keepdims=True)


PREC = {"kk": 3, "inv": 3, "solve": 3, "state": 3, "attend": 3, "big": 3}
BUDGET = 56 << 20


def whole(shape):
    return pl.BlockSpec(shape, lambda c: (0,) * len(shape))


def forward_start(heads):
    return [jnp.zeros((heads, DK, DV), f32), jnp.zeros((8, heads * CONV), f32)]


def mixer_forward(part, before, places, proj, conv, head_rows, onorm, carry, heads, prec=PREC):
    length = proj.shape[0]
    count = length // CHUNK
    steps = count // PER // PARTS
    first = part * steps
    chunk = lambda width: pl.BlockSpec((PER * CHUNK, width), lambda c: (first + c, 0))
    lanes = pl.BlockSpec((PER * CHUNK, LANES), lambda c: (first + c, heads * MIX // LANES))
    square = lambda rows, width: pl.BlockSpec(
        (PER, heads, rows, width), lambda c: (first + c, 0, 0, 0)
    )
    outs = pl.pallas_call(
        functools.partial(forward_body, heads, prec),
        grid=(steps,),
        in_specs=[chunk(LANES), lanes, chunk(heads * MIX)]
        + [whole(x.shape) for x in (conv, head_rows, onorm, *carry)]
        + [pl.BlockSpec(memory_space=pl.ANY)] * len(before),
        out_specs=[
            chunk(heads * DV), chunk(heads * CONV), chunk(heads * DV), chunk(heads * DV),
            chunk(heads * DK), square(DK, DV), square(CHUNK, CHUNK), square(CHUNK, CHUNK),
            square(CHUNK, CHUNK),
        ]
        + [whole(x.shape) for x in carry],
        out_shape=[
            jax.ShapeDtypeStruct((length, heads * DV), bf16),
            jax.ShapeDtypeStruct((length, heads * CONV), f32),
            jax.ShapeDtypeStruct((length, heads * DV), f32),
            jax.ShapeDtypeStruct((length, heads * DV), f32),
            jax.ShapeDtypeStruct((length, heads * DK), f32),
            jax.ShapeDtypeStruct((count, heads, DK, DV), f32),
            jax.ShapeDtypeStruct((count, heads, CHUNK, CHUNK), f32),
            jax.ShapeDtypeStruct((count, heads, CHUNK, CHUNK), f32),
            jax.ShapeDtypeStruct((count, heads, CHUNK, CHUNK), f32),
        ]
        + [jax.ShapeDtypeStruct(x.shape, f32) for x in carry],
        compiler_params=pltpu.CompilerParams(
            dimension_semantics=("arbitrary",), vmem_limit_bytes=BUDGET
        ),
        cost_estimate=pl.CostEstimate(
            flops=length * heads * 32000000, bytes_accessed=length * heads * 6000, transcendentals=0
        ),
        input_output_aliases={6 + len(carry) + i: i for i in range(len(before))},
        name="mixer_forward",
    )(places, proj, proj, conv, head_rows, onorm, *carry, *before)
    return outs[:-2], outs[-2:]


def backward_start(heads):
    return [
        jnp.zeros((heads, DK, DV), f32), jnp.zeros((8, heads * CONV), f32),
        jnp.zeros((TAPS, heads * CONV), f32), jnp.zeros((8, LANES), f32),
        jnp.zeros((1, heads * DV), f32),
    ]


def mixer_backward(
    part, before, places, proj, conv, head_rows, onorm, kept, dz, carry, heads, prec=PREC
):
    length = proj.shape[0]
    steps = length // (BACK * CHUNK) // PARTS
    last = part * steps + steps - 1
    chunk = lambda width: pl.BlockSpec((BACK * CHUNK, width), lambda c: (last - c, 0))
    lanes = pl.BlockSpec((BACK * CHUNK, LANES), lambda c: (last - c, heads * MIX // LANES))
    square = lambda rows, width: pl.BlockSpec(
        (BACK, heads, rows, width), lambda c: (last - c, 0, 0, 0)
    )
    dproj, *carry = pl.pallas_call(
        functools.partial(backward_body, heads, prec),
        grid=(steps,),
        in_specs=[chunk(LANES), lanes, chunk(heads * MIX)]
        + [whole(x.shape) for x in (conv, head_rows, onorm)]
        + [
            chunk(heads * CONV), chunk(heads * DV), chunk(heads * DV),
            chunk(heads * DK), square(DK, DV), square(CHUNK, CHUNK), square(CHUNK, CHUNK),
            square(CHUNK, CHUNK), chunk(heads * DV),
        ]
        + [whole(x.shape) for x in carry]
        + [pl.BlockSpec(memory_space=pl.ANY)] * len(before),
        out_specs=[chunk(heads * MIX + LANES)] + [whole(x.shape) for x in carry],
        out_shape=[jax.ShapeDtypeStruct((length, heads * MIX + LANES), bf16)]
        + [jax.ShapeDtypeStruct(x.shape, f32) for x in carry],
        compiler_params=pltpu.CompilerParams(
            dimension_semantics=("arbitrary",), vmem_limit_bytes=BUDGET
        ),
        cost_estimate=pl.CostEstimate(
            flops=length * heads * 48000000, bytes_accessed=length * heads * 7000, transcendentals=0
        ),
        input_output_aliases={7 + len(kept) + len(carry): 0} if before else {},
        name="mixer_backward",
    )(places, proj, proj, conv, head_rows, onorm, *kept, dz, *carry, *before)
    return dproj, carry


def token_places(segments):
    length = segments.shape[-1]
    seg = segments.reshape(length)
    columns = [seg.astype(f32)]
    for s in range(1, TAPS):
        before = jnp.concatenate([jnp.full((s,), -1, seg.dtype), seg[:-s]])
        columns.append((before == seg).astype(f32))
    for s in range(1, TAPS):
        beyond = jnp.concatenate([seg[s:], jnp.full((s,), -1, seg.dtype)])
        columns.append((beyond == seg).astype(f32))
    ends = seg.reshape(-1, CHUNK)[:, -1]
    ends = jnp.concatenate([jnp.full((1,), -1, seg.dtype), ends[:-1]])
    columns.append((jnp.repeat(ends, CHUNK) == seg).astype(f32))
    return jnp.pad(jnp.stack(columns, 1), ((0, 0), (0, LANES - len(columns))))


def head_lanes(head):
    heads = head.shape[1]
    return jnp.pad(head, ((0, 6), (BETA_AT + heads, LANES - BETA_AT - 2 * heads)))


def ffn_body(where, runs, place_ref, *refs):
    step = pl.program_id(0)
    each = pl.num_programs(0) // runs
    rows_refs = refs[:runs]
    cot_refs = refs[runs : 2 * runs]
    outs = refs[len(refs) - 2 * runs - 5 :]
    w_refs = refs[2 * runs : len(refs) - 2 * runs - 5]
    gate_ref, up_ref, hidden_ref = outs[:3]
    back_refs = outs[3 : 3 + runs]
    out_refs = outs[3 + runs : 3 + 2 * runs]
    rows_ref, cot_ref = outs[3 + 2 * runs :]
    for i in range(runs):

        @pl.when(step // each == i)
        def _():
            rows_ref[...] = rows_refs[i][...]
            cot_ref[...] = cot_refs[i][...]

    pieces = len(where[0])
    size = rows_ref.shape[1] // pieces

    def weight(p, which):
        parts = [w_refs[run[p][0]][run[p][1], which] for run in where]
        return parts[0] if len(parts) == 1 else jnp.concatenate(parts, 1)

    def columns(p):
        return pl.ds(pl.multiple_of((p ^ place_ref[0]) * size, size), size)

    def project(left_ref, which):
        total = None
        for p in range(pieces):
            part = lax.dot_general(
                left_ref[:, columns(p)], weight(p, which), (NT, ((), ())),
                preferred_element_type=f32,
            )
            total = part if total is None else total + part
        return total

    gate = project(rows_ref, 0)
    up = project(rows_ref, 1)
    grad_hidden = project(cot_ref, 2)
    sigma = sigmoid(gate)
    activ = gate * sigma
    hidden = (activ * up).astype(bf16)
    grad_gate = (grad_hidden * up * sigma * (1.0 + gate * (1.0 - sigma))).astype(bf16)
    grad_up = (grad_hidden * activ).astype(bf16)
    hidden_ref[...] = hidden
    gate_ref[...] = grad_gate
    up_ref[...] = grad_up
    for p in range(pieces):
        own = columns(p)
        back = lax.dot_general(
            grad_gate, weight(p, 0), (NN, ((), ())), preferred_element_type=f32
        )
        back = back + lax.dot_general(
            grad_up, weight(p, 1), (NN, ((), ())), preferred_element_type=f32
        )
        rows_ref[:, own] = back.astype(bf16)
        cot_ref[:, own] = lax.dot_general(
            hidden, weight(p, 2), (NN, ((), ())), preferred_element_type=f32
        ).astype(bf16)
    for i in range(runs):

        @pl.when(step // each == i)
        def _():
            back_refs[i][...] = rows_ref[...]
            out_refs[i][...] = cot_ref[...]


FFN_TILE = 256


def ffn_both(place, rows, cot, weights, where):
    runs = len(rows)
    count, d = rows[0].shape
    each = count // FFN_TILE
    total = runs * count
    hidden = weights[0].shape[2]

    def run_tile(i):
        return pl.BlockSpec(
            (FFN_TILE, d), lambda c, place: (jnp.clip(c - i * each, 0, each - 1), 0)
        )

    tiles = [run_tile(i) for i in range(runs)]
    wide = pl.BlockSpec((FFN_TILE, hidden), lambda c, place: (c, 0))
    full = pl.BlockSpec(weights[0].shape, lambda c, place: (0, 0, 0, 0))
    gate, up, hidden_out, *out = pl.pallas_call(
        functools.partial(ffn_body, where, runs),
        grid_spec=pltpu.PrefetchScalarGridSpec(
            num_scalar_prefetch=1,
            grid=(runs * each,),
            in_specs=tiles + tiles + [full] * len(weights),
            out_specs=[wide] * 3 + tiles + tiles,
            scratch_shapes=[pltpu.VMEM((FFN_TILE, d), bf16)] * 2,
        ),
        out_shape=[jax.ShapeDtypeStruct((total, hidden), bf16)] * 3
        + [jax.ShapeDtypeStruct((count, d), bf16)] * (2 * runs),
        compiler_params=pltpu.CompilerParams(
            dimension_semantics=("arbitrary",), vmem_limit_bytes=BUDGET
        ),
        cost_estimate=pl.CostEstimate(
            flops=24 * total * d * hidden, bytes_accessed=8 * total * d, transcendentals=0
        ),
        name="ffn_both",
    )(place.reshape(1), *rows, *cot, *weights)
    return gate, up, hidden_out, out[:runs], out[runs:]


def ffn_grads_body(runs, place_ref, *refs):
    rows_refs = refs[:runs]
    cot_refs = refs[runs : 2 * runs]
    gate_ref, up_ref, hidden_ref = refs[2 * runs : 2 * runs + 3]
    out_refs = refs[2 * runs + 3 : -1]
    flipped_ref = refs[-1]

    @pl.when(pl.program_id(0) == 0)
    def _():
        for i, ref in enumerate((gate_ref, up_ref, hidden_ref)):
            flipped_ref[i] = ref[...].T

    rows = jnp.concatenate([ref[...] for ref in rows_refs], 0)
    cot = jnp.concatenate([ref[...] for ref in cot_refs], 0)
    piece = pl.program_id(0)
    lanes = rows.shape[1] // 2
    for i, right in enumerate((rows, rows, cot)):
        grad = lax.dot_general(
            flipped_ref[i], right, (NN, ((), ())), preferred_element_type=f32
        ).astype(bf16)
        if len(out_refs) == 1:
            out_refs[0][0, i] = grad
            continue
        for j, kept in enumerate((piece % 2 == 0, piece < 2)):
            some = grad[:, j * lanes : (j + 1) * lanes]
            for ref, here in ((out_refs[2 * j], kept), (out_refs[2 * j + 1], ~kept)):

                @pl.when(here)
                def _():
                    ref[0, i] = some


def ffn_weight_grads(place, rows, cot, gate, up, hidden, pieces, split):
    runs = len(rows)
    count, d = rows[0].shape
    total = runs * count
    width = hidden.shape[1]
    size = d // pieces
    column = pl.BlockSpec((count, size), lambda p, place: (0, p ^ place[0]))
    if split == 1:
        places = [lambda p: p]
        shape = (pieces, 3, width, size)
    else:
        places = [
            lambda p: p // 2, lambda p: p // 2,
            lambda p: jnp.minimum(p, 1), lambda p: jnp.maximum(p - 2, 0),
        ]
        shape = (pieces // 2, 3, width, size // 2)
    out_specs = [
        pl.BlockSpec((1,) + shape[1:], lambda p, place, at=at: (at(p), 0, 0, 0)) for at in places
    ]
    full = pl.BlockSpec((total, width), lambda p, place: (0, 0))
    return pl.pallas_call(
        functools.partial(ffn_grads_body, runs),
        grid_spec=pltpu.PrefetchScalarGridSpec(
            num_scalar_prefetch=1,
            grid=(pieces,),
            in_specs=[column] * (2 * runs) + [full] * 3,
            out_specs=out_specs,
            scratch_shapes=[pltpu.VMEM((3, width, total), bf16)],
        ),
        out_shape=[jax.ShapeDtypeStruct(shape, bf16)] * len(out_specs),
        compiler_params=pltpu.CompilerParams(
            dimension_semantics=("arbitrary",), vmem_limit_bytes=BUDGET
        ),
        cost_estimate=pl.CostEstimate(
            flops=12 * total * d * width, bytes_accessed=8 * total * d, transcendentals=0
        ),
        name="ffn_weight_grads",
    )(place.reshape(1), *rows, *cot, gate, up, hidden)


def norm_factor(values):
    return lax.rsqrt(jnp.mean(values * values, -1, keepdims=True) + 1e-06)


def norm_backward(grad_out, scaled, factor, gain):
    grad_scaled = grad_out * gain
    grad_input = factor * (grad_scaled - scaled * jnp.mean(grad_scaled * scaled, -1, keepdims=True))
    return (grad_input, jnp.sum(grad_out * scaled, 0))


def product(left, right, dims):
    return lax.dot_general(left, right, (dims, ((), ())), preferred_element_type=f32)


def after(x, done):
    return lax.optimization_barrier((x, done))[0]


def exchange(x, axis, bit):
    return lax.ppermute(x, axis, [(i, i ^ bit) for i in range(lax.axis_size(axis))])


def sum_over(x, axis):
    ways = lax.axis_size(axis)
    if ways & (ways - 1):
        return lax.psum(x, axis)
    bit = 1
    while bit < ways:
        x = x + exchange(x, axis, bit)
        bit *= 2
    return x


def line_gather(x, axis, more=()):
    ways = lax.axis_size(axis)
    here = lax.axis_index(axis)
    up = [(i, i + 1) for i in range(ways - 1)]
    down = [(i + 1, i) for i in range(ways - 1)]
    below = [x]
    above = [x]
    for _ in range(ways - 1):
        below.append(lax.ppermute(below[-1], axis, up))
        above.append(lax.ppermute(above[-1], axis, down))
    below, above, more = lax.optimization_barrier((below, above, more))
    blocks = []
    for slot in range(ways):
        block = x
        for at in range(ways):
            if at != slot:
                block = jnp.where(here == at, below[at - slot] if at > slot else above[slot - at], block)
        blocks.append(block)
    return jnp.concatenate(blocks, 0), more


def line_scatter(x, axis, beside=None):
    ways = lax.axis_size(axis)
    here = lax.axis_index(axis)
    size = x.shape[0] // ways
    up = [(i, i + 1) for i in range(ways - 1)]
    down = [(i + 1, i) for i in range(ways - 1)]

    def block(slot):
        return lax.dynamic_slice_in_dim(x, slot * size, size, 0).astype(f32)

    low = None
    high = None
    other = None
    for k in range(1, ways):
        to_low = block(jnp.maximum(here - (ways - k), 0))
        to_high = block(jnp.minimum(here + (ways - k), ways - 1))
        if low is not None:
            to_low = to_low + low
            to_high = to_high + high
        low = lax.ppermute(to_low.astype(bf16), axis, down)
        high = lax.ppermute(to_high.astype(bf16), axis, up)
        if beside is not None:
            other = beside(k, other)
        low, high, other = lax.optimization_barrier((low, high, other))
        low = low.astype(f32)
        high = high.astype(f32)
    return block(here) + low + high, other


def shifted(x, axis, by):
    ways = lax.axis_size(axis)
    return lax.ppermute(x, axis, [(i, (i + by) % ways) for i in range(ways)])


def ordered(parts, axis):
    ways = len(parts)
    here = lax.axis_index(axis)
    blocks = []
    for slot in range(ways):
        block = parts[0]
        for at in range(ways):
            if at != slot:
                block = jnp.where(here == at, parts[(at - slot) % ways], block)
        blocks.append(block)
    return blocks


def swap_parts(block_to, axis):
    ways = lax.axis_size(axis)
    here = lax.axis_index(axis)
    parts = [block_to(here)]
    for s in range(1, ways):
        parts.append(shifted(block_to((here + s) % ways), axis, s))
    return parts


def swap_blocks(block_to, axis):
    return ordered(swap_parts(block_to, axis), axis)


class PlaneSum:

    def __init__(self, left, right):
        self.ways = lax.axis_size("dp")
        self.parts = ()
        if self.ways != 8:
            self.came = ()
            grad = product(left, right, TN).astype(bf16)
            self.total = lax.psum_scatter(grad, "dp", scatter_dimension=0, tiled=True).astype(f32)
            return
        core = lax.axis_index("dp") % 2
        self.size = left.shape[1] // self.ways
        blocks = [left[:, i * self.size : (i + 1) * self.size] for i in range(self.ways)]
        even = jnp.concatenate(blocks[::2], 1)
        odd = jnp.concatenate(blocks[1::2], 1)
        self.stay = jnp.where(core == 0, even, odd)
        self.right = right
        self.came = exchange(
            product(jnp.where(core == 0, odd, even), right, TN).astype(bf16), "dp", 1
        )

    def send(self):
        if self.ways == 8:
            total = product(self.stay, self.right, TN) + self.came.astype(f32)
            total = total.astype(bf16)
            place = lax.axis_index("dp") // 2
            block = lambda i: lax.dynamic_slice_in_dim(total, i * self.size, self.size, 0)
            self.total = block(place)
            self.parts = [exchange(block(place ^ (m // 2)), "dp", m) for m in (2, 4, 6)]

    def finish(self):
        total = self.total.astype(f32)
        for part in self.parts:
            total = total + part.astype(f32)
        return total


class OutWeights:

    def __init__(self, mixer_out):
        rows = mixer_out.T
        self.ways = lax.axis_size("dp")
        self.parts = ()
        self.rows = jnp.concatenate(swap_blocks(lambda i: rows, "tensor"), 1)

    def start(self, started):
        if self.ways == 8:
            rows = after(self.rows, started)
            self.parts = {m: exchange(rows, "dp", m) for m in (2, 4, 6)}

    def finish(self, done):
        if self.ways != 8:
            return lax.all_gather(self.rows, "dp", axis=0, tiled=True)
        here = lax.axis_index("dp")
        parts = dict(zip((2, 4, 6), after([self.parts[m] for m in (2, 4, 6)], done)))
        parts[0] = self.rows
        size = self.rows.shape[0]
        out = jnp.zeros((self.ways * size, self.rows.shape[1]), bf16)
        for m in (0, 2, 4, 6):
            parts[m + 1] = exchange(parts[m], "dp", 1)
        for m, part in parts.items():
            out = lax.dynamic_update_slice_in_dim(out, part, (here ^ m) * size, 0)
        return out

    def send_sum(self, total, width):
        return swap_parts(
            lambda i: lax.dynamic_slice_in_dim(total, i * width, width, 1), "tensor"
        )


class LineFfn:

    def __init__(self, ffn_in, ffn_out, started):
        self.own = jnp.stack([ffn_in[0].T, ffn_in[1].T, ffn_out])
        self.place = jnp.zeros((), jnp.int32)
        self.near = self.far = ()

    def middle(self, done, more):
        return done, more

    def plane_step(self):
        pass

    def finish(self, done):
        weights = lax.all_gather(self.own, "dp", axis=2, tiled=True)
        return (weights[None],)

    pieces = 1
    where = (((0, 0),),)

    def reach(self, x):
        return line_gather(x, "tensor")[0]

    def beside(self, x):
        return ()

    def gather(self, x, near, far):
        return [far]

    def halves(self, x):
        return line_scatter(x[0], "tensor")[0], jnp.zeros((), bf16)

    def cross(self, far):
        return far

    def sum_start(self, grads):
        self.grads = grads

    def sum_step(self, done):
        return ()

    def sum_far(self, sent):
        pass

    def sum_finish(self):
        return lax.psum_scatter(self.grads[0][0], "dp", scatter_dimension=2, tiled=True)

    def send_sums(self, grads):
        return grads

    def own_grads(self, grads, came):
        return came.astype(f32)


TO_A = [(1, 0), (0, 2), (2, 3), (3, 1)]
TO_B = [(2, 1), (1, 2)]
BACK_A = [(0, 1), (2, 0), (3, 2), (1, 3)]
BACK_B = [(2, 1), (1, 2)]


class PairFfn:

    def __init__(self, ffn_in, ffn_out, started):
        self.core = lax.axis_index("dp") % 2
        self.here = lax.axis_index("tensor")
        self.place = lax.axis_index("dp") // 2
        self.own = after(jnp.stack([ffn_in[0].T, ffn_in[1].T, ffn_out]), started)
        self.a = lax.ppermute(self.own, "tensor", TO_A)
        self.b = lax.ppermute(self.own, "tensor", TO_B)

    def middle(self, done, more):
        here = self.here
        self.own, self.a, self.b, done, more = lax.optimization_barrier(
            (self.own, self.a, self.b, done, more)
        )
        own, a, b = self.own, self.a, self.b
        first = jnp.where(here == 0, own, jnp.where(here == 1, b, a))
        second = jnp.where(here == 3, own, jnp.where(here == 2, b, a))
        mine = jnp.where(self.core == 0, first, second)
        got = exchange(jnp.where(self.core == 0, second, first), "dp", 1)
        self.low = jnp.where(self.core == 0, mine, got)
        self.high = jnp.where(self.core == 0, got, mine)
        done = after(done, (self.low, self.high))
        self.near = exchange(self.low, "dp", 2), exchange(self.high, "dp", 4)
        return done, more

    def plane_step(self):
        self.low = jnp.stack([self.low, self.near[0]])
        self.high = jnp.stack([self.high, self.near[1]])
        self.far = exchange(self.low, "dp", 4), exchange(self.high, "dp", 2)

    def finish(self, done):
        far = after(self.far, done)
        return (self.low, far[0], self.high, far[1])

    pieces = 4
    where = (((0, 0), (0, 1), (1, 0), (1, 1)), ((2, 0), (3, 0), (2, 1), (3, 1)))

    def reach(self, x):
        return exchange(x, "tensor", 1)

    def beside(self, x):
        return exchange(x, "dp", 1)

    def gather(self, x, near, far):
        return [x, near, far, exchange(far, "dp", 1)]

    def halves(self, x):
        far = (x[2].astype(f32) + exchange(x[3], "dp", 1).astype(f32)).astype(bf16)
        return x[0].astype(f32) + exchange(x[1], "dp", 1).astype(f32), far

    def cross(self, far):
        return exchange(far, "tensor", 1)

    def sum_start(self, grads):
        self.stay = grads[0], grads[2]
        self.near = exchange(grads[1], "dp", 2), exchange(grads[3], "dp", 4)

    def sum_step(self, done):
        low, high = self.stay
        came = after(self.near, done)
        add = lambda x, y: (x.astype(f32) + y.astype(f32)).astype(bf16)
        self.kept = add(low[0], came[0][0]), add(high[0], came[1][0])
        return add(low[1], came[0][1]), add(high[1], came[1][1])

    def sum_far(self, sent):
        self.far = exchange(sent[0], "dp", 4), exchange(sent[1], "dp", 2)

    def sum_finish(self):
        came = self.far
        add = lambda x, y: (x.astype(f32) + y.astype(f32)).astype(bf16)
        low = add(self.kept[0], came[0])
        high = add(self.kept[1], came[1])
        core = self.core
        mine = jnp.where(core == 0, low, high)
        got = exchange(jnp.where(core == 0, high, low), "dp", 1)
        return jnp.where(core == 0, mine, got), jnp.where(core == 0, got, mine)

    def send_sums(self, sums):
        first, second = sums
        here = self.here
        a = lax.ppermute(jnp.where(here < 2, second, first), "tensor", BACK_A)
        b = lax.ppermute(jnp.where(here == 2, second, first), "tensor", BACK_B)
        return a, b

    def own_grads(self, sums, came):
        first, second = sums
        a, b = came
        here = self.here
        other = jnp.where(here == 0, first, jnp.where(here == 3, second, b))
        return a.astype(f32) + other.astype(f32)


CONV_AT = 64


def column_blocks(value, rows):
    ways, size = value.shape
    lanes = -(-size // rows)
    value = jnp.pad(value, ((0, 0), (0, lanes * rows - size)))
    return value.reshape(ways, lanes, rows).swapaxes(1, 2).reshape(ways * rows, lanes)


def from_columns(columns, shape, dim, rows):
    ways = columns.shape[0] // rows
    size = 1
    for extent in shape:
        size *= extent
    value = columns.reshape(ways, rows, -1).swapaxes(1, 2).reshape(ways, -1)[:, :size]
    value = jnp.moveaxis(value.reshape((ways,) + shape), 0, dim)
    return value.reshape(shape[:dim] + (ways * shape[dim],) + shape[dim + 1 :])


def lanes_of(small, conv, onorm):
    rows, width = small.shape
    used = BETA_AT + width
    rest = LANES - CONV_AT - conv.shape[1] - onorm.shape[1]
    zeros = lambda lanes: jnp.zeros((rows, lanes), small.dtype)
    return jnp.concatenate(
        [zeros(BETA_AT), small, zeros(CONV_AT - used), conv, onorm, zeros(rest)], 1
    )


def fetch_mixer(mixer_in, mixer_small, conv_weight, out_norm):
    rows, width = mixer_in.shape
    small = jnp.moveaxis(mixer_small, 0, 1).reshape(rows, -1)
    conv = column_blocks(conv_weight.reshape(1, -1), rows)
    onorm = column_blocks(out_norm.reshape(1, -1), rows)
    extended = jnp.concatenate([mixer_in, lanes_of(small, conv, onorm)], 1)
    w_in = lax.all_gather(extended, "dp", axis=0, tiled=True)
    at = width + CONV_AT
    w_conv = from_columns(w_in[:, at : at + conv.shape[1]], conv_weight.shape, 2, rows)
    at += conv.shape[1]
    w_onorm = from_columns(w_in[:, at : at + onorm.shape[1]], out_norm.shape, 1, rows)
    return w_in, w_conv, w_onorm


def shards(
    tokens, cotangent, segments, norm_gains, mixer_in, mixer_small, conv_weight, head_params,
    out_norm, mixer_out, ffn_in, ffn_out,
):
    heads = mixer_in.shape[1] // MIX
    all_heads = head_params.shape[1]
    ways = lax.axis_size("dp")
    teams = lax.axis_size("tensor")
    head_start = lax.axis_index("tensor") * heads
    head_local = lax.dynamic_slice_in_dim(head_params, head_start, heads, 1)
    gains = norm_gains.astype(f32)
    own = tokens.shape[0]
    inputs = tokens.astype(f32)
    factor_one = norm_factor(inputs)
    scaled_one = inputs * factor_one
    normed_one = (scaled_one * gains[0]).astype(bf16)
    out_weights = OutWeights(mixer_out)
    w_in, w_conv, w_onorm = fetch_mixer(mixer_in, mixer_small, conv_weight, out_norm)
    conv_rows = w_conv.astype(f32).reshape(TAPS, heads * CONV)
    onorm_row = w_onorm.astype(f32).reshape(1, heads * DV)
    head_rows = head_lanes(head_local)
    places = token_places(segments)
    kind = PairFfn if teams == 4 and ways == 8 else LineFfn
    rows_one, (out_weights.rows, constants, places, cot_near) = line_gather(
        normed_one,
        "tensor",
        (
            out_weights.rows, (conv_rows, head_rows, onorm_row), places,
            kind.beside(None, cotangent),
        ),
    )
    out_weights.start(rows_one)
    ffn = kind(ffn_in, ffn_out, rows_one)
    wide = heads * MIX
    proj = product(rows_one, w_in, NN)
    carry = forward_start(heads)
    made = []
    for part in range(PARTS):
        made, carry = mixer_forward(part, made, places, proj, *constants, carry, heads)
        if part == 0:
            carry, (cotangent, out_weights.parts) = ffn.middle(
                carry, (cotangent, out_weights.parts)
            )
            cot_far = ffn.reach(cotangent)
    mixed, *kept = made
    mixed, cot_far, ffn.near = lax.optimization_barrier((mixed, cot_far, ffn.near))
    ffn.plane_step()
    came = swap_parts(lambda i: lax.dynamic_slice_in_dim(mixed, i * own, own, 0), "tensor")
    out_t = out_weights.finish(came[-1])
    grad_rows = ffn.gather(cotangent, cot_near, after(cot_far, came[-1]))
    mixed = jnp.concatenate(ordered(came, "tensor"), 1)
    middle = inputs + product(mixed, out_t, NT)
    factor_two = norm_factor(middle)
    scaled_two = middle * factor_two
    normed_two = (scaled_two * gains[1]).astype(bf16)
    rows_two = ffn.gather(normed_two, ffn.beside(normed_two), ffn.reach(normed_two))
    w_ffn = ffn.finish(normed_two)
    grad_gate, grad_up, hidden, back, forth = ffn_both(
        ffn.place, rows_two, grad_rows, w_ffn, ffn.where
    )
    grad_normed_two, far = ffn.halves(back)
    ffn_grads = ffn_weight_grads(
        ffn.place, after(rows_two, far), grad_rows, grad_gate, grad_up, hidden,
        ffn.pieces, len(ffn.where),
    )
    far, ffn_grads = lax.optimization_barrier((ffn.cross(far), ffn_grads))
    grad_normed_two = grad_normed_two + far.astype(f32)
    ffn.sum_start(ffn_grads)
    grad_middle_norm, grad_gain_two = norm_backward(
        grad_normed_two, scaled_two, factor_two, gains[1]
    )
    grad_middle = cotangent.astype(f32) + grad_middle_norm
    branch_grad = grad_middle.astype(bf16)
    grad_mixed = product(branch_grad, out_t, NN).astype(bf16)
    width = heads * DV
    came = swap_parts(
        lambda i: lax.dynamic_slice_in_dim(grad_mixed, i * width, width, 1), "tensor"
    )
    branch_grad, forth, near = after((branch_grad, forth, ffn.near), grad_mixed)
    ffn.near = near
    out_sum = PlaneSum(branch_grad, mixed)
    result, far = ffn.halves(forth)
    came, far, sums = lax.optimization_barrier((came, far, ffn.sum_step(grad_mixed)))
    ffn.sum_far(sums)
    result = result, ffn.cross(far)
    grad_mixed = jnp.concatenate(ordered(came, "tensor"), 0)
    carry = backward_start(heads)
    grad_proj = []
    for part in reversed(range(PARTS)):
        dproj, carry = mixer_backward(
            part, grad_proj, places, proj, *constants, kept, grad_mixed, carry, heads
        )
        grad_proj = [dproj]
        if part == PARTS - 1:
            carry, result, ffn.far, out_sum.came = lax.optimization_barrier(
                (carry, result, ffn.far, out_sum.came)
            )
            out_sum.send()
            ffn_sums = ffn.sum_finish()
            carry = after(carry, ffn_sums)
            ffn_came = ffn.send_sums(ffn_sums)
    grad_proj, ffn_came, out_sum.parts = lax.optimization_barrier(
        (dproj, ffn_came, out_sum.parts)
    )
    grad_conv, grad_head, grad_onorm = carry[2:]
    result = middle + result[0] + result[1].astype(f32)
    sent = product(grad_proj, w_in, NT).astype(bf16)
    grad_normed_one = lax.psum_scatter(
        sent, "tensor", scatter_dimension=0, tiled=True
    ).astype(f32)
    grad_proj, again = after((grad_proj, sent), sent)
    grad_in = PlaneSum(rows_one, grad_proj[:, :wide])
    head_full = lax.dynamic_update_slice_in_dim(
        jnp.zeros((2, all_heads), f32),
        grad_head[:2, BETA_AT + heads : BETA_AT + 2 * heads],
        head_start,
        1,
    )
    d = gains.shape[1]
    sizes = [2 * d + 2 * all_heads, grad_conv.size, grad_onorm.size, 2 * heads * d]
    ends = [sum(sizes[:i]) for i in range(5)]
    at = BETA_AT + 2 * heads
    grad_small = product(rows_one, grad_proj[:, wide:], TN)[:, BETA_AT:at]
    gain_one = jnp.sum(again.astype(f32) * rows_one.astype(f32), 0) / gains[0]
    parts = [
        gain_one, grad_gain_two, head_full.reshape(-1), grad_conv.reshape(-1),
        grad_onorm.reshape(-1), grad_small.T.reshape(-1),
    ]
    totals, grad_in.came = lax.optimization_barrier(
        (sum_over(jnp.concatenate(parts), "dp"), grad_in.came)
    )
    grad_in.send()
    shared = after(totals[: sizes[0]], grad_in.parts)
    shared = sum(ordered(swap_parts(lambda i: shared, "tensor"), "tensor"))
    out_parts = after(out_sum.finish().astype(bf16), grad_in.total)
    out_out = sum(block.astype(f32) for block in out_weights.send_sum(out_parts, width))
    conv_total, onorm_total, small_total = (totals[ends[i] : ends[i + 1]] for i in (1, 2, 3))
    place = lax.axis_index("dp")

    def own_part(total, shape):
        size = shape[-1] // ways
        return lax.dynamic_slice_in_dim(total.reshape(shape), place * size, size, len(shape) - 1)

    out_conv = own_part(conv_total, (TAPS, heads, CONV))
    out_onorm = own_part(onorm_total, (heads, DV))
    out_small = own_part(small_total, (2, heads, d)).swapaxes(1, 2)
    totals = shared
    out_in = grad_in.finish()
    ffn_grads = ffn.own_grads(ffn_sums, ffn_came)
    grad_scaled = grad_normed_one * gains[0]
    grad_tokens = grad_middle + factor_one * (
        grad_scaled - scaled_one * jnp.mean(grad_scaled * scaled_one, -1, keepdims=True)
    )
    return (
        result.astype(bf16),
        grad_tokens,
        totals[: 2 * d].reshape(2, d),
        out_in,
        out_small,
        out_conv,
        totals[2 * d :].reshape(2, all_heads),
        out_onorm,
        out_out.T,
        ffn_grads[:2].swapaxes(1, 2),
        ffn_grads[2],
    )


def solution(mesh):
    in_specs = (
        P(("dp", "tensor"), None),
        P(("dp", "tensor"), None),
        P("dp", None),
        P(),
        P("dp", "tensor"),
        P(None, "dp", "tensor"),
        P(None, "tensor", "dp"),
        P(),
        P("tensor", "dp"),
        P("tensor", "dp"),
        P(None, "dp", "tensor"),
        P("tensor", "dp"),
    )
    out_specs = (
        P(("dp", "tensor"), None),
        P(("dp", "tensor"), None),
        P(),
        P("dp", "tensor"),
        P(None, "dp", "tensor"),
        P(None, "tensor", "dp"),
        P(),
        P("tensor", "dp"),
        P("tensor", "dp"),
        P(None, "dp", "tensor"),
        P("tensor", "dp"),
    )
    return jax.shard_map(shards, mesh=mesh, in_specs=in_specs, out_specs=out_specs, check_vma=False)
```
